32 devices in a mesh: member: 4 (over z), tile: 4 (over x, core), batch: 2 (over y).
Axes of the slice: x: 2, y: 2, z: 4, core: 2. Of those that a mesh axis runs over, the one named last changes fastest.
Arguments:
- latent: bfloat16 [4, 2, 4096, 1024], P('member', 'batch', 'tile'), may hold values from -6 to 6
- w_in: bfloat16 [1024, 1024], replicated, may hold values from -0.1875 to 0.1875
- w_out: bfloat16 [1024, 112], replicated, may hold values from -0.1875 to 0.1875
- observed: bfloat16 [2, 512, 1792], P('batch', 'tile'), may hold values from -5 to 5
- patch_index: int32 [2, 256], P('batch', 'tile'), may hold values from 0 to 127
- counts: int32 [2, 256], P('batch', 'tile'), may hold values from 1 to 8
Outputs:
- grad_w1: float32 [1024, 1024], P(('member', 'tile', 'batch'))
- grad_w2: float32 [1024, 112], P(('member', 'tile', 'batch'))
The draws below stay inside these ranges and needn't reach their ends.
Inputs may be any that keep to these rules, and one draw needn't show every extreme that they name: `patch_index`: a candidate of the same tile and lead time.
All inputs are finite; a program needn't handle non-finite values.
Results may differ from the reference program's by a relative error of at most 0.0017.
Values sent between devices are 32-bit elements; how exact they have to be, the bound alone decides.
No kernel may reach another device: no remote copies, remote signals or barrier semaphores. Data moves between devices by JAX's collectives and lax.ppermute only.
A program may use at most 64 MiB of HBM per device.

```python
import jax
import jax.numpy as jnp
from jax import lax

D = 1024
HID = 1024
CH = 112
PATCH = 16
POOL = 128
FEAT = 1792
SAMP = 64
MEMBERS = 4
LEADS = 2
CELLS = 4096
N_TILE = 4


def touch_ends(result, own_key, low, high):
    index_at = [jax.random.randint(jax.random.fold_in(own_key, axis), (), 0, length) for axis, length in enumerate(result.shape)]
    main_axis = result.shape.index(max(result.shape))
    beside = index_at[:main_axis] + [(index_at[main_axis] + 1) % result.shape[main_axis]] + index_at[main_axis + 1:]
    return result.at[tuple(index_at)].set(low).at[tuple(beside)].set(high)


def steps_of(own_key, extent, cuts, least, largest):
    def one(position, parts):
        heights = jax.random.uniform(jax.random.fold_in(jax.random.fold_in(own_key, 6), position), (parts,), jnp.float32, least / len(cuts), largest / len(cuts))
        return jnp.repeat(jnp.exp(heights), extent[position] // parts).reshape((-1,) + (1,) * (len(extent) - position - 1))

    level = one(*cuts[0])
    for cut in cuts[1:]:
        level = level * one(*cut)
    return level


def scatter_about(key, extent, spread, most, shards=(), kind=jnp.bfloat16):
    entries = jax.random.normal(key, extent, jnp.float32) * spread
    if len(shards) > 0:
        entries = steps_of(key, extent, shards, -0.22, 0.18) * entries
    return jnp.clip(entries, min=-most, max=most).astype(kind)


def setup_inputs(seed: int = 0) -> dict:
    splits = jax.random.split(jax.random.key(seed), 7)
    latent = scatter_about(splits[0], (MEMBERS, LEADS, CELLS, D), 1.0, 6.0, ((0, 4), (1, 2), (2, 4)))
    w_in = scatter_about(splits[1], (D, HID), D ** -0.5, 0.1875)
    w_out = scatter_about(splits[2], (HID, CH), HID ** -0.5, 0.1875)
    observed = scatter_about(splits[3], (LEADS, POOL * N_TILE, FEAT), 0.7, 5.0, ((0, 2), (1, 4)))
    patch_index = touch_ends(jax.random.randint(splits[4], (LEADS, SAMP * N_TILE), 0, POOL), jax.random.fold_in(splits[4], 1), 0, POOL - 1).astype(jnp.int32)
    counts = touch_ends(jax.random.randint(splits[5], (LEADS, SAMP * N_TILE), 1, 9), jax.random.fold_in(splits[5], 1), 1, 8).astype(jnp.int32)
    return {"latent": latent, "w_in": w_in, "w_out": w_out, "observed": observed, "patch_index": patch_index, "counts": counts}


def smooth_grad(deltas):
    return deltas / jnp.sqrt(lax.optimization_barrier(jnp.sum(deltas * deltas, axis=-1, keepdims=True)) + 1.0)

def decode(rows_in, w_in, w_out):
    preact = jnp.dot(rows_in, w_in, preferred_element_type=jnp.float32)
    hidden = jax.nn.silu(preact).astype(jnp.bfloat16)
    decoded = jnp.dot(hidden, w_out, preferred_element_type=jnp.float32)
    return (preact, hidden, decoded)

def reference(latent, w_in, w_out, observed, patch_index, counts):
    npatch = CELLS // PATCH
    flat_latent = latent.reshape(MEMBERS, LEADS * CELLS, D)

    def forward(rows_in):
        return decode(rows_in, w_in, w_out)[2]
    decoded = lax.map(forward, flat_latent)
    patches = decoded.reshape(MEMBERS, LEADS, npatch, PATCH * CH)
    tiles = jnp.arange(npatch, dtype=jnp.int32) // SAMP * POOL
    picked = (patch_index + tiles[None, :]).astype(jnp.int32)
    target = jnp.take_along_axis(observed, picked[:, :, None], axis=1).astype(jnp.float32)
    own = smooth_grad(patches - target[None])

    def pair_of(single):
        return lax.optimization_barrier(jnp.sum(smooth_grad(single[None] - patches), axis=0))
    pair = lax.map(pair_of, patches)
    weight = counts.astype(jnp.float32)[None, :, :, None]
    grad_patch = weight * (own / MEMBERS - pair / (MEMBERS * MEMBERS))
    grad_decoded = grad_patch.reshape(MEMBERS, LEADS * CELLS, CH).astype(jnp.bfloat16)

    def accumulate(totals, inputs):
        rows_in, grad_out = inputs
        preact, hidden, decoded_rows = decode(rows_in, w_in, w_out)
        grad_hidden = lax.dot_general(grad_out, w_out, (((1,), (1,)), ((), ())), preferred_element_type=jnp.float32)
        sigma = jax.nn.sigmoid(preact)
        grad_preact = (grad_hidden * sigma * (1.0 + preact * (1.0 - sigma))).astype(jnp.bfloat16)
        first = lax.dot_general(rows_in, grad_preact, (((0,), (0,)), ((), ())), preferred_element_type=jnp.float32)
        second = lax.dot_general(hidden, grad_out, (((0,), (0,)), ((), ())), preferred_element_type=jnp.float32)
        return ((totals[0] + first, totals[1] + second), None)
    start = (jnp.zeros((D, HID), jnp.float32), jnp.zeros((HID, CH), jnp.float32))
    totals, unused = lax.scan(accumulate, start, (flat_latent, grad_decoded))
    return (totals[0], totals[1])
```

```python
import functools

import jax
import jax.numpy as jnp
import numpy as np
from jax import lax
from jax.experimental import pallas as pl
from jax.experimental.pallas import tpu as pltpu
from jax.sharding import PartitionSpec as P

PATCH = 16
CORES = 2
MIB = 1 << 20
NT = (((1,), (1,)), ((), ()))
WHOLE = pl.BlockSpec(memory_space=pltpu.VMEM)


def chunk_of(extent, target):
    return target if extent % target == 0 else extent


def forward_body(latent_ref, w_in_ref, w_out_t_ref, hidden_ref, slope_ref, decoded_ref):
    preact = jnp.dot(latent_ref[...], w_in_ref[...], preferred_element_type=jnp.float32)
    sigma = 1.0 / (1.0 + jnp.exp(-preact))
    hidden = (preact * sigma).astype(jnp.bfloat16)
    hidden_ref[...] = hidden
    slope_ref[...] = sigma * (1.0 + preact * (1.0 - sigma))
    decoded_ref[...] = lax.dot_general(hidden, w_out_t_ref[...], NT, preferred_element_type=jnp.float32)


def forward(rows_in, w_in, w_out_t):
    nrows, depth = rows_in.shape
    width = w_in.shape[1]
    channels = w_out_t.shape[0]
    block = chunk_of(nrows, 256)
    return pl.pallas_call(
        forward_body,
        grid=(nrows // block,),
        in_specs=[
            pl.BlockSpec((block, depth), lambda i: (i, 0)),
            pl.BlockSpec((depth, width), lambda i: (0, 0)),
            pl.BlockSpec((channels, width), lambda i: (0, 0)),
        ],
        out_specs=[
            pl.BlockSpec((block, width), lambda i: (i, 0)),
            pl.BlockSpec((block, width), lambda i: (i, 0)),
            pl.BlockSpec((block, channels), lambda i: (i, 0)),
        ],
        out_shape=[
            jax.ShapeDtypeStruct((nrows, width), jnp.bfloat16),
            jax.ShapeDtypeStruct((nrows, width), jnp.float32),
            jax.ShapeDtypeStruct((nrows, channels), jnp.float32),
        ],
        compiler_params=pltpu.CompilerParams(vmem_limit_bytes=24 * MIB),
        cost_estimate=pl.CostEstimate(
            flops=2 * nrows * width * (depth + channels), bytes_accessed=10 * MIB, transcendentals=nrows * width
        ),
        name="forward",
    )(rows_in, w_in, w_out_t)


def score_body(x_ref, pool_ref, index_ref, count_ref, out_ref):
    members, npatch, _ = x_ref.shape
    npool = pool_ref.shape[0]
    choose = index_ref[...] == lax.broadcasted_iota(jnp.int32, (npatch, npool), 1)
    target = jnp.dot(choose.astype(jnp.bfloat16), pool_ref[...], preferred_element_type=jnp.float32)
    weight = count_ref[...].astype(jnp.float32)

    def direction(delta):
        return delta / jnp.sqrt(jnp.sum(delta * delta, axis=-1, keepdims=True) + 1.0)

    xs = [x_ref[m] for m in range(members)]
    pair = [jnp.zeros_like(xs[0]) for _ in range(members)]
    for m in range(members):
        for k in range(m + 1, members):
            term = direction(xs[m] - xs[k])
            pair[m] = pair[m] + term
            pair[k] = pair[k] - term
    for m in range(members):
        own = direction(xs[m] - target)
        out_ref[m] = weight * (own / members - pair[m] / (members * members))


def score(grouped, pool, index, count):
    return pl.pallas_call(
        score_body,
        in_specs=[WHOLE] * 4,
        out_specs=WHOLE,
        out_shape=jax.ShapeDtypeStruct(grouped.shape, jnp.float32),
        compiler_params=pltpu.CompilerParams(vmem_limit_bytes=24 * MIB),
        cost_estimate=pl.CostEstimate(flops=30 * grouped.size, bytes_accessed=8 * grouped.size, transcendentals=0),
        name="score",
    )(grouped, pool, index, count)


def first_body(step, g_ref, slope_ref, w_out_t_ref, latent_t_ref, hidden_t_ref, out_ref, gp_ref, g16_ref):
    j = pl.program_id(0)
    width = out_ref.shape[1] - g_ref.shape[1]
    g16 = g_ref[...].astype(jnp.bfloat16)
    gh = jnp.dot(g16, w_out_t_ref[...], preferred_element_type=jnp.float32)
    gp = (gh * slope_ref[...]).astype(jnp.bfloat16)
    gp_ref[...] = gp
    columns = pl.ds(pl.multiple_of(j * step, step), step)
    out_ref[:, columns] = jnp.dot(latent_t_ref[...], gp, preferred_element_type=jnp.float32)

    @pl.when(j == 0)
    def _():
        g16_ref[...] = g16
        out_ref[:, width:] = jnp.dot(hidden_t_ref[...], g16, preferred_element_type=jnp.float32)


def first_products(g, slope, w_out_t, latent_t, hidden_t):
    nrows, channels = g.shape
    width = slope.shape[1]
    picked = latent_t.shape[0]
    step = chunk_of(width, 256)
    return pl.pallas_call(
        functools.partial(first_body, step),
        grid=(width // step,),
        in_specs=[
            pl.BlockSpec((nrows, channels), lambda j: (0, 0)),
            pl.BlockSpec((nrows, step), lambda j: (0, j)),
            pl.BlockSpec((channels, step), lambda j: (0, j)),
            pl.BlockSpec((picked, nrows), lambda j: (0, 0)),
            pl.BlockSpec((picked, nrows), lambda j: (0, 0)),
        ],
        out_specs=[
            pl.BlockSpec((picked, width + channels), lambda j: (0, 0)),
            pl.BlockSpec((nrows, step), lambda j: (0, j)),
            pl.BlockSpec((nrows, channels), lambda j: (0, 0)),
        ],
        out_shape=[
            jax.ShapeDtypeStruct((picked, width + channels), jnp.float32),
            jax.ShapeDtypeStruct((nrows, width), jnp.bfloat16),
            jax.ShapeDtypeStruct((nrows, channels), jnp.bfloat16),
        ],
        compiler_params=pltpu.CompilerParams(vmem_limit_bytes=24 * MIB),
        cost_estimate=pl.CostEstimate(
            flops=2 * nrows * (width * (channels + picked)), bytes_accessed=8 * MIB, transcendentals=0
        ),
        name="first_products",
    )(g, slope, w_out_t, latent_t, hidden_t)


def more_body(step, cuts, gp_ref, g16_ref, latent_t_ref, hidden_t_ref, *out_refs):
    j = pl.program_id(0)
    width = out_refs[0].shape[1] - g16_ref.shape[1]
    columns = pl.ds(pl.multiple_of(j * step, step), step)
    product = jnp.dot(latent_t_ref[...], gp_ref[...], preferred_element_type=jnp.float32)
    for out_ref, low, high in zip(out_refs, cuts[:-1], cuts[1:]):
        out_ref[:, columns] = product[low:high]

    @pl.when(j == 0)
    def _():
        second = jnp.dot(hidden_t_ref[...], g16_ref[...], preferred_element_type=jnp.float32)
        for out_ref, low, high in zip(out_refs, cuts[:-1], cuts[1:]):
            out_ref[:, width:] = second[low:high]


def more_products(gp, g16, latent_t, hidden_t, sizes):
    nrows, channels = g16.shape
    width = gp.shape[1]
    picked = latent_t.shape[0]
    step = chunk_of(width, 256)
    cuts = tuple(int(c) for c in np.cumsum([0, *sizes]))
    return pl.pallas_call(
        functools.partial(more_body, step, cuts),
        grid=(width // step,),
        in_specs=[
            pl.BlockSpec((nrows, step), lambda j: (0, j)),
            pl.BlockSpec((nrows, channels), lambda j: (0, 0)),
            pl.BlockSpec((picked, nrows), lambda j: (0, 0)),
            pl.BlockSpec((picked, nrows), lambda j: (0, 0)),
        ],
        out_specs=[pl.BlockSpec((size, width + channels), lambda j: (0, 0)) for size in sizes],
        out_shape=[jax.ShapeDtypeStruct((size, width + channels), jnp.float32) for size in sizes],
        compiler_params=pltpu.CompilerParams(vmem_limit_bytes=24 * MIB),
        cost_estimate=pl.CostEstimate(
            flops=2 * nrows * picked * (width + channels), bytes_accessed=6 * MIB, transcendentals=0
        ),
        name="more_products",
    )(gp, g16, latent_t, hidden_t)


def piece_orders(nz, nx, nc, ny, ra, rb, rc):
    def grid(xs, ys, zs, rows, order):
        cells = {"x": list(xs), "y": list(ys), "z": list(zs), "r": list(rows)}
        mesh = np.meshgrid(*[cells[k] for k in order], indexing="ij")
        by = {k: v.reshape(-1) for k, v in zip(order, mesh)}
        return np.stack([by["z"], by["x"], by["y"], by["r"]], axis=1)

    a_rows, b_rows, c_rows = range(ra), range(ra, ra + rb), range(ra + rb, ra + rb + rc)
    z, x, y = range(nz), range(nx), range(ny)
    a_send = grid(x[1:], y, z, a_rows, "xyzr")
    b_send = grid(x, y[1:], z, b_rows, "yxzr")
    c_all = grid(x, y, z, c_rows, "zxyr")
    a_keep = grid(x[:1], y, z, a_rows, "xyzr")
    b_keep = grid(x, y[:1], z, b_rows, "yxzr")

    def at(core, parts):
        rows = np.concatenate(parts, axis=0)
        return np.concatenate([np.full((len(rows), 1), core), rows], axis=1)

    other = [at(core, [a_send, b_send]) for core in range(1, nc)]
    rest = [at(core, [c_all, a_keep, b_keep]) for core in range(1, nc)]
    return {
        "sizes": (len(a_send), len(b_send), len(c_all), len(a_keep), len(b_keep)),
        "first": np.concatenate(other, axis=0),
        "second": np.concatenate(rest + [at(0, [a_send, b_send])], axis=0),
        "third": at(0, [c_all, a_keep, b_keep]),
    }


def shards(latent, w_in, w_out, observed, patch_index, counts):
    rows_in = latent[0, 0]
    nrows, depth = rows_in.shape
    width, channels = w_out.shape
    nz, nt, ny = (lax.axis_size(name) for name in ("member", "tile", "batch"))
    nc, nx = CORES, nt // CORES
    me_z, me_t, me_y = (lax.axis_index(name) for name in ("member", "tile", "batch"))
    me_x, me_c = me_t // nc, me_t % nc
    w_out_t = w_out.T

    hidden, slope, decoded = forward(rows_in, w_in, w_out_t)
    npatch = nrows // PATCH
    share = npatch // nz
    blocks = decoded.reshape(nz, share, PATCH * channels)
    grouped = lax.all_to_all(blocks, "member", split_axis=0, concat_axis=0, tiled=True)

    height = depth // (nz * nt * ny)
    rc = max(height // 4, 1)
    ra = (height - rc) // 2
    rb = height - rc - ra
    orders = piece_orders(nz, nx, nc, ny, ra, rb, rc)

    def pick(order, matrix):
        core, z, x, y, row = (jnp.asarray(order[:, k], jnp.int32) for k in range(5))
        tile = (x + me_x) % nx * nc + (core + me_c) % nc
        source = ((z * nt + tile) * ny + (y + me_y) % ny) * height + row
        choose = (source[:, None] == jnp.arange(matrix.shape[1], dtype=jnp.int32)[None, :]).astype(jnp.bfloat16)
        return lax.dot_general(choose, matrix, NT, preferred_element_type=jnp.float32).astype(jnp.bfloat16)

    latent_t = {name: pick(orders[name], rows_in) for name in ("first", "second", "third")}
    hidden_t = {name: pick(orders[name], hidden) for name in ("first", "second", "third")}

    index = lax.dynamic_slice_in_dim(patch_index[0], me_z * share, share, 0)[:, None]
    count = lax.dynamic_slice_in_dim(counts[0], me_z * share, share, 0)[:, None]
    scored = score(grouped, observed[0], index, count)
    returned = lax.all_to_all(scored, "member", split_axis=0, concat_axis=0, tiled=True)
    g = returned.reshape(nrows, channels)

    def shift_core(value, j):
        return lax.ppermute(value, "tile", [(t, t // nc * nc + (t % nc + j) % nc) for t in range(nt)])

    def shift_x(value, j):
        return lax.ppermute(value, "tile", [(t, (t // nc + j) % nx * nc + t % nc) for t in range(nt)])

    def shift_y(value, j):
        return lax.ppermute(value, "batch", [(t, (t + j) % ny) for t in range(ny)])

    na_send, nb_send, n_c, na_keep, nb_keep = orders["sizes"]
    n_rest = n_c + na_keep + nb_keep

    first, gp, g16 = first_products(g, slope, w_out_t, latent_t["first"], hidden_t["first"])
    from_core_send = shift_core(first, 1)
    rest, a_send, b_send = more_products(
        gp, g16, latent_t["second"], hidden_t["second"], (n_rest, na_send, nb_send)
    )
    from_core_rest = shift_core(rest, 1)
    a_send = a_send + from_core_send[:na_send]
    b_send = b_send + from_core_send[na_send:]

    def pieces(value, count):
        return value.reshape(count, value.shape[0] // count, value.shape[1])

    def send_all(value, count, shift):
        stacked = pieces(value, count)
        return [shift(stacked[j], j + 1) for j in range(count)]

    a_got = send_all(a_send, nx - 1, shift_x)
    b_got = send_all(b_send, ny - 1, shift_y)
    c_own, a_keep, b_keep = more_products(gp, g16, latent_t["third"], hidden_t["third"], (n_c, na_keep, nb_keep))
    c_own = c_own + from_core_rest[:n_c]
    c_got = lax.all_to_all(pieces(c_own, nz), "member", split_axis=0, concat_axis=0, tiled=True)
    a_keep = sum(a_got, a_keep + from_core_rest[n_c:n_c + na_keep])
    b_keep = sum(b_got, b_keep + from_core_rest[n_c + na_keep:])

    a_keep, b_keep = pieces(a_keep, ny), pieces(b_keep, nx)
    a_got = [shift_y(a_keep[j], j) for j in range(1, ny)]
    b_got = [shift_x(b_keep[j], j) for j in range(1, nx)]
    a_here = pieces(sum(a_got, a_keep[0]), nz)
    b_here = pieces(sum(b_got, b_keep[0]), nz)
    ab_got = lax.all_to_all(
        jnp.concatenate([a_here, b_here], axis=1), "member", split_axis=0, concat_axis=0, tiled=True
    )

    c_here = pieces(jnp.sum(c_got, axis=0), nx)
    c_here = sum([shift_x(c_here[j], j) for j in range(1, nx)], c_here[0])
    c_here = pieces(c_here, ny)
    c_here = sum([shift_y(c_here[j], j) for j in range(1, ny)], c_here[0])
    total = jnp.concatenate([jnp.sum(ab_got, axis=0), c_here], axis=0)
    return (total[:, :width], total[:, width:])


def solution(mesh):
    in_specs = (
        P("member", "batch", "tile", None),
        P(),
        P(),
        P("batch", "tile", None),
        P("batch", "tile"),
        P("batch", "tile"),
    )
    out_specs = (P(("member", "tile", "batch"), None), P(("member", "tile", "batch"), None))
    return jax.shard_map(shards, mesh=mesh, in_specs=in_specs, out_specs=out_specs, check_vma=False)
```

```python
import functools

import jax
import jax.numpy as jnp
import numpy as np
from jax import lax
from jax.experimental import pallas as pl
from jax.experimental.pallas import tpu as pltpu
from jax.sharding import PartitionSpec as P

PATCH = 16
CORES = 2
LANES = 128
MIB = 1 << 20
NT = (((1,), (1,)), ((), ()))
WHOLE = pl.BlockSpec(memory_space=pltpu.VMEM)


def params(mib=24):
    return pltpu.CompilerParams(vmem_limit_bytes=mib * MIB)


def cost(flops, moved):
    return pl.CostEstimate(flops=int(flops), bytes_accessed=int(moved), transcendentals=0)


def packing(channels):
    spare = LANES - channels
    carriers = PATCH * channels // LANES
    per_cell = channels // spare
    assert carriers * LANES == PATCH * channels and per_cell * spare == channels
    return spare, carriers, per_cell


def pack(cell, channels):
    spare, carriers, per_cell = packing(channels)
    extra = [cell(j) for j in range(carriers, PATCH)]
    lane = lax.broadcasted_iota(jnp.int32, extra[0].shape, 1)
    rows = []
    for j in range(carriers):
        piece = extra[j // per_cell]
        moved = pltpu.roll(piece, channels - j % per_cell * spare, 1)
        rows.append(jnp.where(lane < channels, cell(j), moved))
    return rows


def unpack(rows, channels):
    spare, carriers, per_cell = packing(channels)
    lane = lax.broadcasted_iota(jnp.int32, rows[0].shape, 1)
    cells = list(rows)
    for first in range(0, carriers, per_cell):
        value = jnp.zeros_like(rows[0])
        for i in range(per_cell):
            moved = pltpu.roll(rows[first + i], (i * spare - channels) % LANES, 1)
            value = jnp.where((lane >= i * spare) & (lane < (i + 1) * spare), moved, value)
        cells.append(value)
    return cells


def decode_body(latent_ref, w_in_ref, w_out_t_ref, packed_ref, cells):
    channels = w_out_t_ref.shape[0]
    share = packed_ref.shape[2]
    preact = jnp.dot(latent_ref[...], w_in_ref[...], preferred_element_type=jnp.float32)
    hidden = (preact / (1.0 + jnp.exp(-preact))).astype(jnp.bfloat16)
    cells[:, :channels] = lax.dot_general(hidden, w_out_t_ref[...], NT, preferred_element_type=jnp.float32)
    for j, row in enumerate(pack(lambda j: cells[pl.ds(j, share, stride=PATCH), :], channels)):
        packed_ref[0, j] = row


def decode(rows_in, w_in, w_out_t, parts):
    nrows, depth = rows_in.shape
    width = w_in.shape[1]
    channels = w_out_t.shape[0]
    block = nrows // parts
    share = block // PATCH
    carriers = packing(channels)[1]
    return pl.pallas_call(
        decode_body,
        grid=(parts,),
        in_specs=[
            pl.BlockSpec((block, depth), lambda i: (i, 0)),
            pl.BlockSpec((depth, width), lambda i: (0, 0)),
            pl.BlockSpec((channels, width), lambda i: (0, 0)),
        ],
        out_specs=pl.BlockSpec((1, carriers, share, LANES), lambda i: (i, 0, 0, 0)),
        out_shape=jax.ShapeDtypeStruct((parts, carriers, share, LANES), jnp.float32),
        scratch_shapes=[pltpu.VMEM((block, LANES), jnp.float32)],
        compiler_params=params(56),
        cost_estimate=cost(2 * nrows * width * (depth + channels), 5 * MIB),
        name="decode",
    )(rows_in, w_in, w_out_t)


def fill_choice(source_ref, choice):
    picked, extent = choice.shape
    for low in range(0, picked, LANES):
        high = min(low + LANES, picked)
        across = jnp.broadcast_to(source_ref[:, low:high], (LANES, high - low))
        down = jnp.transpose(across)
        for left in range(0, extent, LANES):
            here = lax.broadcasted_iota(jnp.int32, down.shape, 1) + left
            choice[low:high, left:left + LANES] = jnp.where(down == here, 1.0, 0.0).astype(jnp.bfloat16)


def slope_body(source_ref, latent_ref, w_in_ref, slope_ref, hidden_t_ref, choice):
    @pl.when(pl.program_id(0) == 0)
    def _():
        fill_choice(source_ref, choice)

    preact = jnp.dot(latent_ref[...], w_in_ref[...], preferred_element_type=jnp.float32)
    scale = 1.0 + jnp.exp(-preact)
    sigma = 1.0 / scale
    slope_ref[...] = sigma * (1.0 + preact * (1.0 - sigma))
    hidden = (preact / scale).astype(jnp.bfloat16)
    ordered = lax.dot_general(choice[...], hidden, NT, preferred_element_type=jnp.float32)
    hidden_t_ref[...] = ordered.astype(jnp.bfloat16)


def slopes(source, rows_in, w_in):
    nrows, depth = rows_in.shape
    width = w_in.shape[1]
    picked = source.shape[1]
    block = 256 if nrows % 256 == 0 else nrows
    return pl.pallas_call(
        slope_body,
        grid=(nrows // block,),
        in_specs=[
            pl.BlockSpec((1, picked), lambda i: (0, 0)),
            pl.BlockSpec((block, depth), lambda i: (i, 0)),
            pl.BlockSpec((depth, width), lambda i: (0, 0)),
        ],
        out_specs=[
            pl.BlockSpec((block, width), lambda i: (i, 0)),
            pl.BlockSpec((picked, block), lambda i: (0, i)),
        ],
        out_shape=[
            jax.ShapeDtypeStruct((nrows, width), jnp.float32),
            jax.ShapeDtypeStruct((picked, nrows), jnp.bfloat16),
        ],
        scratch_shapes=[pltpu.VMEM((picked, width), jnp.bfloat16)],
        compiler_params=params(),
        cost_estimate=cost(2 * nrows * width * depth, 4 * MIB),
        name="slopes",
    )(source, rows_in, w_in)


def order_body(source_ref, matrix_ref, out_ref, choice):
    @pl.when(pl.program_id(0) == 0)
    def _():
        fill_choice(source_ref, choice)

    ordered = lax.dot_general(choice[...], matrix_ref[...], NT, preferred_element_type=jnp.float32)
    out_ref[...] = ordered.astype(jnp.bfloat16)


def ordered_transpose(source, matrix):
    nrows, extent = matrix.shape
    picked = source.shape[1]
    block = 256 if nrows % 256 == 0 else nrows
    return pl.pallas_call(
        order_body,
        grid=(nrows // block,),
        in_specs=[
            pl.BlockSpec((1, picked), lambda i: (0, 0)),
            pl.BlockSpec((block, extent), lambda i: (i, 0)),
        ],
        out_specs=pl.BlockSpec((picked, block), lambda i: (0, i)),
        out_shape=jax.ShapeDtypeStruct((picked, nrows), jnp.bfloat16),
        scratch_shapes=[pltpu.VMEM((picked, extent), jnp.bfloat16)],
        compiler_params=params(),
        cost_estimate=cost(nrows * extent * picked, 4 * MIB),
        name="ordered_transpose",
    )(source, matrix)


def score_body(channels, x_ref, pool_ref, index_ref, count_ref, out_ref):
    members, carriers, share, _ = x_ref.shape
    npool, total = pool_ref.shape
    choose = index_ref[...] == lax.broadcasted_iota(jnp.int32, (share, npool), 1)
    flat = jnp.dot(
        jnp.where(choose, 1.0, 0.0).astype(jnp.bfloat16), pool_ref[...], preferred_element_type=jnp.float32
    )
    weight = count_ref[...].astype(jnp.float32)

    def cell(j):
        start = j * channels
        low = start // LANES * LANES
        part = flat[:, low:min(low + 2 * LANES, total)]
        return pltpu.roll(part, (low - start) % part.shape[1], 1)[:, :LANES]

    target = pack(cell, channels)

    def inverse_norm(delta):
        squares = sum(d * d for d in delta)
        return 1.0 / jnp.sqrt(jnp.sum(squares, axis=-1, keepdims=True) + 1.0)

    xs = [[x_ref[m, j] for j in range(carriers)] for m in range(members)]
    pair = [[jnp.zeros_like(xs[0][0])] * carriers for _ in range(members)]
    for m in range(members):
        for k in range(m + 1, members):
            delta = [p - q for p, q in zip(xs[m], xs[k])]
            inverse = inverse_norm(delta)
            pair[m] = [p + d * inverse for p, d in zip(pair[m], delta)]
            pair[k] = [p - d * inverse for p, d in zip(pair[k], delta)]
    for m in range(members):
        delta = [p - q for p, q in zip(xs[m], target)]
        inverse = inverse_norm(delta)
        for j in range(carriers):
            out_ref[m, j] = weight * (delta[j] * inverse / members - pair[m][j] / (members * members))


def score(grouped, pool, index, count, channels):
    return pl.pallas_call(
        functools.partial(score_body, channels),
        in_specs=[WHOLE] * 4,
        out_specs=WHOLE,
        out_shape=jax.ShapeDtypeStruct(grouped.shape, jnp.float32),
        compiler_params=params(),
        cost_estimate=cost(30 * grouped.size, 8 * grouped.size),
        name="score",
    )(grouped, pool, index, count)


def column_steps(width):
    step = 256 if width % 256 == 0 else width
    return [slice(low, low + step) for low in range(0, width, step)]


def first_body(low, high, scored_ref, slope_ref, w_out_t_ref, latent_t_ref, hidden_t_ref, out_ref, gp_ref, g16_ref, cells):
    parts, carriers, share, _ = scored_ref.shape
    channels, width = w_out_t_ref.shape
    for q in range(parts):
        rows = [scored_ref[q, j] for j in range(carriers)]
        for j, value in enumerate(unpack(rows, channels)):
            cells[pl.ds(q * share * PATCH + j, share, stride=PATCH), :] = value
    g16 = cells[:, :channels].astype(jnp.bfloat16)
    g16_ref[...] = g16
    for columns in column_steps(width):
        gh = jnp.dot(g16, w_out_t_ref[:, columns], preferred_element_type=jnp.float32)
        gp = (gh * slope_ref[:, columns]).astype(jnp.bfloat16)
        gp_ref[:, columns] = gp
        out_ref[:, columns] = jnp.dot(latent_t_ref[low:high], gp, preferred_element_type=jnp.float32)
    out_ref[:, width:] = jnp.dot(hidden_t_ref[low:high], g16, preferred_element_type=jnp.float32)


def first_products(scored, slope, w_out_t, latent_t, hidden_t, low, high):
    nrows, width = slope.shape
    channels = w_out_t.shape[0]
    return pl.pallas_call(
        functools.partial(first_body, low, high),
        in_specs=[WHOLE] * 5,
        out_specs=[WHOLE] * 3,
        out_shape=[
            jax.ShapeDtypeStruct((high - low, width + channels), jnp.float32),
            jax.ShapeDtypeStruct((nrows, width), jnp.bfloat16),
            jax.ShapeDtypeStruct((nrows, channels), jnp.bfloat16),
        ],
        scratch_shapes=[pltpu.VMEM((nrows, LANES), jnp.float32)],
        compiler_params=params(),
        cost_estimate=cost(2 * nrows * width * (channels + high - low), 8 * MIB),
        name="first_products",
    )(scored, slope, w_out_t, latent_t, hidden_t)


def more_body(cuts, gp_ref, g16_ref, latent_t_ref, hidden_t_ref, *out_refs):
    width = gp_ref.shape[1]
    low, high = cuts[0][0], cuts[-1][1]

    def put(columns, product):
        for out_ref, (start, end) in zip(out_refs, cuts):
            out_ref[:, columns] = product[start - low:end - low]

    for columns in column_steps(width):
        put(columns, jnp.dot(latent_t_ref[low:high], gp_ref[:, columns], preferred_element_type=jnp.float32))
    put(slice(width, None), jnp.dot(hidden_t_ref[low:high], g16_ref[...], preferred_element_type=jnp.float32))


def more_products(gp, g16, latent_t, hidden_t, cuts):
    nrows, channels = g16.shape
    width = gp.shape[1]
    picked = cuts[-1][1] - cuts[0][0]
    return pl.pallas_call(
        functools.partial(more_body, tuple(cuts)),
        in_specs=[WHOLE] * 4,
        out_specs=[WHOLE] * len(cuts),
        out_shape=[jax.ShapeDtypeStruct((end - start, width + channels), jnp.float32) for start, end in cuts],
        compiler_params=params(),
        cost_estimate=cost(2 * nrows * picked * (width + channels), 6 * MIB),
        name="more_products",
    )(gp, g16, latent_t, hidden_t)


def add_body(plans, count, *refs):
    inputs, outputs = refs[:count], refs[count:]
    for out_ref, plan in zip(outputs, plans):
        for at, rows, sources in plan:
            total = None
            for which, low in sources:
                value = inputs[which][low:low + rows]
                total = value if total is None else total + value
            out_ref[at:at + rows] = total


def add_rows(inputs, plans):
    columns = inputs[0].shape[1]
    sizes = [sum(rows for _, rows, _ in plan) for plan in plans]
    return pl.pallas_call(
        functools.partial(add_body, plans, len(inputs)),
        in_specs=[WHOLE] * len(inputs),
        out_specs=[WHOLE] * len(plans),
        out_shape=[jax.ShapeDtypeStruct((size, columns), jnp.float32) for size in sizes],
        compiler_params=params(),
        cost_estimate=cost(3 * sum(sizes) * columns, 12 * sum(sizes) * columns),
        name="add_rows",
    )(*inputs)


def finish_body(across_ref, *refs):
    *rest_refs, first_ref, second_ref = refs
    width = first_ref.shape[1]
    rows = across_ref.shape[1]
    total = across_ref[0]
    for z in range(1, across_ref.shape[0]):
        total = total + across_ref[z]
    last = rest_refs[0][...]
    for ref in rest_refs[1:]:
        last = last + ref[...]
    for low, high, value in ((0, rows, total), (rows, first_ref.shape[0], last)):
        first_ref[low:high] = value[:, :width]
        second_ref[low:high] = value[:, width:]


def finish(across, rest, width):
    height = across.shape[1] + rest[0].shape[0]
    columns = across.shape[2]
    return pl.pallas_call(
        finish_body,
        in_specs=[WHOLE] * (1 + len(rest)),
        out_specs=[WHOLE] * 2,
        out_shape=[
            jax.ShapeDtypeStruct((height, width), jnp.float32),
            jax.ShapeDtypeStruct((height, columns - width), jnp.float32),
        ],
        compiler_params=params(),
        cost_estimate=cost(across.size, 4 * across.size),
        name="finish",
    )(across, *rest)


def row_order(nz, nx, nc, ny, height):
    near = 2 if nz % 2 == 0 else 1
    far = nz // near
    rc = max(height // 4, 1)
    more = -(-(height - rc) * 2 // 3)
    a_rows = [range(0, more if z % 2 == 0 else height - rc - more) for z in range(nz)]
    b_rows = [range(a_rows[z].stop, height - rc) for z in range(nz)]
    c_rows = range(height - rc, height)
    x_last, y_last, far_last = [[*range(1, n), 0] for n in (nx, ny, far)]

    def part_a(xs):
        return [(x, y, 0, z // near, z % near, r) for x in xs for y in y_last for z in range(nz) for r in a_rows[z]]

    def part_b(ys):
        return [(x, y, 0, z // near, z % near, r) for y in ys for x in x_last for z in range(nz) for r in b_rows[z]]

    def part_c(nears):
        return [(x, y, 1, f, n, r) for n in nears for f in far_last for x in x_last for y in y_last for r in c_rows]

    pieces = [
        part_a(range(1, nx)), part_b(range(1, ny)), part_c(range(1, near)),
        part_c([0]), part_a([0]), part_b([0]),
    ]
    sizes = [len(piece) for piece in pieces]
    half = [row for piece in pieces for row in piece]
    table = np.array([(core, *row) for core in [*range(1, nc), 0] for row in half], np.int32).T
    return table, sizes, near, far, a_rows, b_rows, rc


def shards(latent, w_in, w_out, observed, patch_index, counts):
    rows_in = latent[0, 0]
    nrows, depth = rows_in.shape
    width, channels = w_out.shape
    nz, nt, ny = (lax.axis_size(name) for name in ("member", "tile", "batch"))
    nc, nx = CORES, nt // CORES
    me_z, me_t, me_y = (lax.axis_index(name) for name in ("member", "tile", "batch"))
    me_x, me_c = me_t // nc, me_t % nc
    w_out_t = w_out.T
    height = depth // (nz * nt * ny)
    table, sizes, near, far, a_rows, b_rows, rc = row_order(nz, nx, nc, ny, height)

    share = nrows // PATCH // nz
    packed = decode(rows_in, w_in, w_out_t, nz)
    grouped = lax.all_to_all(packed, "member", split_axis=0, concat_axis=0, tiled=True)

    core, x, y, relative, f, n, row = (jnp.asarray(table[k:k + 1]) for k in range(7))
    z = (f + relative * (me_z // near)) % far * near + (n + relative * (me_z % near)) % near
    tile = (x + me_x) % nx * nc + (core + me_c) % nc
    source = ((z * nt + tile) * ny + (y + me_y) % ny) * height + row
    slope, hidden_t = slopes(source, rows_in, w_in)
    index = lax.dynamic_slice_in_dim(patch_index[0], me_z * share, share, 0)[:, None]
    count = lax.dynamic_slice_in_dim(counts[0], me_z * share, share, 0)[:, None]
    grouped, slope, hidden_t, index, count = lax.optimization_barrier((grouped, slope, hidden_t, index, count))

    scored = score(grouped, observed[0], index, count, channels)
    returned = lax.all_to_all(scored, "member", split_axis=0, concat_axis=0, tiled=True)
    latent_t = ordered_transpose(source, rows_in)
    returned, latent_t = lax.optimization_barrier((returned, latent_t))

    def shift_core(value, j):
        return lax.ppermute(value, "tile", [(t, t // nc * nc + (t % nc + j) % nc) for t in range(nt)])

    def shift_x(value, j):
        return lax.ppermute(value, "tile", [(t, (t // nc + j) % nx * nc + t % nc) for t in range(nt)])

    def shift_y(value, j):
        return lax.ppermute(value, "batch", [(t, (t + j) % ny) for t in range(ny)])

    def shift_near(value, j):
        return lax.ppermute(value, "member", [(t, t // near * near + (t % near + j) % near) for t in range(nz)])

    def shift_far(value, j):
        return lax.ppermute(value, "member", [(t, (t // near + j) % far * near + t % near) for t in range(nz)])

    def send_all(value, others, shift):
        if others == 1:
            return [shift(value, 1)]
        return [shift(v, j + 1) for j, v in enumerate(jnp.split(value, others, axis=0))] if others else []

    na, nb, nc_send, nc_keep, na_keep, nb_keep = sizes
    n_send, n_keep = na + nb + nc_send, nc_keep + na_keep + nb_keep
    half = n_send + n_keep

    first, gp, g16 = first_products(returned, slope, w_out_t, latent_t, hidden_t, 0, n_send)
    from_core = shift_core(first, 1)
    (own_send,) = more_products(gp, g16, latent_t, hidden_t, [(half, half + n_send)])
    a_send, b_send, c_send = add_rows(
        [own_send, from_core],
        [
            [(0, na, [(0, 0), (1, 0)])],
            [(0, nb, [(0, na), (1, na)])],
            [(0, nc_send, [(0, na + nb), (1, na + nb)])],
        ],
    )
    a_got = send_all(a_send, nx - 1, shift_x)
    b_got = send_all(b_send, ny - 1, shift_y)
    c_got = send_all(c_send, near - 1, shift_near)
    other_keep, own_keep = more_products(
        gp, g16, latent_t, hidden_t, [(n_send, half)]
    ) + more_products(gp, g16, latent_t, hidden_t, [(half + n_send, 2 * half)])
    core_keep = shift_core(other_keep, 1)

    inputs = [own_keep, core_keep, *a_got, *b_got, *c_got]
    a_in = range(2, 2 + len(a_got))
    b_in = range(a_in.stop, a_in.stop + len(b_got))
    c_in = range(b_in.stop, b_in.stop + len(c_got))

    def summed(base, got, low, rows):
        return [(0, rows, [(0, base + low), (1, base + low), *[(k, low) for k in got]])]

    a_base, b_base = nc_keep, nc_keep + na_keep
    a_cut, b_cut, c_cut = na_keep // ny * (ny - 1), nb_keep // nx * (nx - 1), nc_keep // far * (far - 1)
    c_send, a_send, b_send = add_rows(
        inputs,
        [
            summed(0, c_in, 0, c_cut),
            summed(a_base, a_in, 0, a_cut),
            summed(b_base, b_in, 0, b_cut),
        ],
    )
    c_got = send_all(c_send, far - 1, shift_far)
    a_got = send_all(a_send, ny - 1, shift_y)
    b_got = send_all(b_send, nx - 1, shift_x)
    c_keep, a_keep, b_keep = add_rows(
        inputs,
        [
            summed(0, c_in, c_cut, nc_keep - c_cut),
            summed(a_base, a_in, a_cut, na_keep - a_cut),
            summed(b_base, b_in, b_cut, nb_keep - b_cut),
        ],
    )

    inputs = [a_keep, *a_got, b_keep, *b_got]
    plan, a_low, b_low, at = [], 0, 0, 0
    for k in range(nz):
        plan.append((at, len(a_rows[k]), [(i, a_low) for i in range(1 + len(a_got))]))
        a_low, at = a_low + len(a_rows[k]), at + len(a_rows[k])
        plan.append((at, len(b_rows[k]), [(1 + len(a_got) + i, b_low) for i in range(1 + len(b_got))]))
        b_low, at = b_low + len(b_rows[k]), at + len(b_rows[k])
    (joined,) = add_rows(inputs, [plan])
    across = lax.all_to_all(
        joined.reshape(nz, height - rc, joined.shape[1]), "member", split_axis=0, concat_axis=0, tiled=True
    )
    c_rows = c_keep.shape[0]
    cut = c_rows // nx * (nx - 1)
    (c_send, c_keep) = add_rows(
        [c_keep, *c_got],
        [
            [(0, cut, [(i, 0) for i in range(1 + len(c_got))])],
            [(0, c_rows - cut, [(i, cut) for i in range(1 + len(c_got))])],
        ],
    )
    c_got = send_all(c_send, nx - 1, shift_x)
    c_rows = c_keep.shape[0]
    cut = c_rows // ny * (ny - 1)
    (c_send, c_keep) = add_rows(
        [c_keep, *c_got],
        [
            [(0, cut, [(i, 0) for i in range(1 + len(c_got))])],
            [(0, c_rows - cut, [(i, cut) for i in range(1 + len(c_got))])],
        ],
    )
    c_got = send_all(c_send, ny - 1, shift_y)
    return tuple(finish(across, [c_keep, *c_got], width))


def solution(mesh):
    in_specs = (
        P("member", "batch", "tile", None),
        P(),
        P(),
        P("batch", "tile", None),
        P("batch", "tile"),
        P("batch", "tile"),
    )
    out_specs = (P(("member", "tile", "batch"), None), P(("member", "tile", "batch"), None))
    return jax.shard_map(shards, mesh=mesh, in_specs=in_specs, out_specs=out_specs, check_vma=False)
```

```python
import functools

import jax
import jax.numpy as jnp
import numpy as np
from jax import lax
from jax.experimental import pallas as pl
from jax.experimental.pallas import tpu as pltpu
from jax.sharding import PartitionSpec as P

PATCH = 16
CORES = 2
LANES = 128
MIB = 1 << 20
NT = (((1,), (1,)), ((), ()))
WHOLE = pl.BlockSpec()
ANY = pl.BlockSpec(memory_space=pl.ANY)
MOST = 56


def params(mib=24):
    return pltpu.CompilerParams(vmem_limit_bytes=mib * MIB)


def cost(flops, moved):
    return pl.CostEstimate(flops=int(flops), bytes_accessed=int(moved), transcendentals=0)


def packing(channels):
    spare = LANES - channels
    carriers = PATCH * channels // LANES
    per_cell = channels // spare
    assert carriers * LANES == PATCH * channels and per_cell * spare == channels
    return spare, carriers, per_cell


def pack(cell, channels):
    spare, carriers, per_cell = packing(channels)
    extra = [cell(j) for j in range(carriers, PATCH)]
    lane = lax.broadcasted_iota(jnp.int32, extra[0].shape, 1)
    rows = []
    for j in range(carriers):
        piece = extra[j // per_cell]
        moved = pltpu.roll(piece, channels - j % per_cell * spare, 1)
        rows.append(jnp.where(lane < channels, cell(j), moved))
    return rows


def unpack(rows, channels):
    spare, carriers, per_cell = packing(channels)
    lane = lax.broadcasted_iota(jnp.int32, rows[0].shape, 1)
    cells = list(rows)
    for first in range(0, carriers, per_cell):
        value = jnp.zeros_like(rows[0])
        for i in range(per_cell):
            moved = pltpu.roll(rows[first + i], (i * spare - channels) % LANES, 1)
            value = jnp.where((lane >= i * spare) & (lane < (i + 1) * spare), moved, value)
        cells.append(value)
    return cells


def column_steps(width):
    step = 256 if width % 256 == 0 else width
    return [slice(low, low + step) for low in range(0, width, step)]


def decode_body(latent_ref, w_in_ref, w_out_t_ref, packed_ref, rows, w_in, w_out_t, hidden, cells, packed, row_sems, w_sems, sems):
    parts, block, _ = rows.shape
    channels, width = w_out_t.shape
    share = packed.shape[2]
    column = column_steps(width)
    row_copies = [
        pltpu.make_async_copy(latent_ref.at[pl.ds(q * block, block)], rows.at[q], row_sems.at[q]) for q in range(parts)
    ]
    w_copies = [
        pltpu.make_async_copy(w_in_ref.at[:, pl.ds(c.start, c.stop - c.start)], w_in.at[:, c], w_sems.at[k])
        for k, c in enumerate(column)
    ]
    last_copy = pltpu.make_async_copy(w_out_t_ref, w_out_t, sems.at[parts])
    row_copies[0].start()
    for copy in w_copies:
        copy.start()
    last_copy.start()
    for copy in row_copies[1:]:
        copy.start()

    def silu(preact):
        return (preact / (1.0 + jnp.exp(-preact))).astype(jnp.bfloat16)

    results = []
    for q in range(parts):
        row_copies[q].wait()
        if q == 0:
            for copy, c in zip(w_copies, column):
                copy.wait()
                hidden[:, c] = silu(jnp.dot(rows[q], w_in[:, c], preferred_element_type=jnp.float32))
            last_copy.wait()
            value = hidden[...]
        else:
            value = silu(jnp.dot(rows[q], w_in[...], preferred_element_type=jnp.float32))
        cells[:, :channels] = lax.dot_general(value, w_out_t[...], NT, preferred_element_type=jnp.float32)
        for j, row in enumerate(pack(lambda j: cells[pl.ds(j, share, stride=PATCH), :], channels)):
            packed[q, j] = row
        results.append(pltpu.make_async_copy(packed.at[q], packed_ref.at[q], sems.at[q]))
        results[-1].start()
    for copy in results:
        copy.wait()


def decode(rows_in, w_in, w_out_t, parts):
    nrows, depth = rows_in.shape
    width = w_in.shape[1]
    channels = w_out_t.shape[0]
    block = nrows // parts
    share = block // PATCH
    carriers = packing(channels)[1]
    out = (parts, carriers, share, LANES)
    return pl.pallas_call(
        decode_body,
        in_specs=[ANY] * 3,
        out_specs=ANY,
        out_shape=jax.ShapeDtypeStruct(out, jnp.float32),
        scratch_shapes=[
            pltpu.VMEM((parts, block, depth), jnp.bfloat16),
            pltpu.VMEM((depth, width), jnp.bfloat16),
            pltpu.VMEM((channels, width), jnp.bfloat16),
            pltpu.VMEM((block, width), jnp.bfloat16),
            pltpu.VMEM((block, LANES), jnp.float32),
            pltpu.VMEM(out, jnp.float32),
            pltpu.SemaphoreType.DMA((parts,)),
            pltpu.SemaphoreType.DMA((len(column_steps(width)),)),
            pltpu.SemaphoreType.DMA((parts + 1,)),
        ],
        compiler_params=params(MOST),
        cost_estimate=cost(2 * nrows * width * (depth + channels), 5 * MIB),
        name="decode",
    )(rows_in, w_in, w_out_t)


def fill_choice(source_ref, choice):
    picked, extent = choice.shape
    for low in range(0, picked, LANES):
        high = min(low + LANES, picked)
        across = jnp.broadcast_to(source_ref[:, low:high], (LANES, high - low))
        down = jnp.transpose(across)
        for left in range(0, extent, LANES):
            here = lax.broadcasted_iota(jnp.int32, down.shape, 1) + left
            choice[low:high, left:left + LANES] = jnp.where(down == here, 1.0, 0.0).astype(jnp.bfloat16)


def slope_body(source_ref, latent_ref, w_in_ref, slope_ref, hidden_t_ref, choice):
    @pl.when(pl.program_id(0) == 0)
    def _():
        fill_choice(source_ref, choice)

    preact = jnp.dot(latent_ref[...], w_in_ref[...], preferred_element_type=jnp.float32)
    scale = 1.0 + jnp.exp(-preact)
    sigma = 1.0 / scale
    slope_ref[...] = sigma * (1.0 + preact * (1.0 - sigma))
    hidden = (preact / scale).astype(jnp.bfloat16)
    ordered = lax.dot_general(choice[...], hidden, NT, preferred_element_type=jnp.float32)
    hidden_t_ref[...] = ordered.astype(jnp.bfloat16)


def slopes(source, rows_in, w_in):
    nrows, depth = rows_in.shape
    width = w_in.shape[1]
    picked = source.shape[1]
    block = 256 if nrows % 256 == 0 else nrows
    return pl.pallas_call(
        slope_body,
        grid=(nrows // block,),
        in_specs=[
            pl.BlockSpec((1, picked), lambda i: (0, 0)),
            pl.BlockSpec((block, depth), lambda i: (i, 0)),
            pl.BlockSpec((depth, width), lambda i: (0, 0)),
        ],
        out_specs=[
            pl.BlockSpec((block, width), lambda i: (i, 0)),
            pl.BlockSpec((picked, block), lambda i: (0, i)),
        ],
        out_shape=[
            jax.ShapeDtypeStruct((nrows, width), jnp.float32),
            jax.ShapeDtypeStruct((picked, nrows), jnp.bfloat16),
        ],
        scratch_shapes=[pltpu.VMEM((picked, width), jnp.bfloat16)],
        compiler_params=params(MOST),
        cost_estimate=cost(2 * nrows * width * depth, 4 * MIB),
        name="slopes",
    )(source, rows_in, w_in)


def order_body(source_ref, matrix_ref, out_ref, choice):
    @pl.when(pl.program_id(0) == 0)
    def _():
        fill_choice(source_ref, choice)

    ordered = lax.dot_general(choice[...], matrix_ref[...], NT, preferred_element_type=jnp.float32)
    out_ref[...] = ordered.astype(jnp.bfloat16)


def ordered_transpose(source, matrix):
    nrows, extent = matrix.shape
    picked = source.shape[1]
    block = 256 if nrows % 256 == 0 else nrows
    return pl.pallas_call(
        order_body,
        grid=(nrows // block,),
        in_specs=[
            pl.BlockSpec((1, picked), lambda i: (0, 0)),
            pl.BlockSpec((block, extent), lambda i: (i, 0)),
        ],
        out_specs=pl.BlockSpec((picked, block), lambda i: (0, i)),
        out_shape=jax.ShapeDtypeStruct((picked, nrows), jnp.bfloat16),
        scratch_shapes=[pltpu.VMEM((picked, extent), jnp.bfloat16)],
        compiler_params=params(MOST),
        cost_estimate=cost(nrows * extent * picked, 4 * MIB),
        name="ordered_transpose",
    )(source, matrix)


def score_body(channels, x_ref, pool_ref, index_ref, count_ref, out_ref):
    members, carriers, share, _ = x_ref.shape
    npool, total = pool_ref.shape
    choose = index_ref[...] == lax.broadcasted_iota(jnp.int32, (share, npool), 1)
    flat = jnp.dot(
        jnp.where(choose, 1.0, 0.0).astype(jnp.bfloat16), pool_ref[...], preferred_element_type=jnp.float32
    )
    weight = count_ref[...].astype(jnp.float32)

    def cell(j):
        start = j * channels
        low = start // LANES * LANES
        part = flat[:, low:min(low + 2 * LANES, total)]
        return pltpu.roll(part, (low - start) % part.shape[1], 1)[:, :LANES]

    target = pack(cell, channels)

    def inverse_norm(delta):
        squares = sum(d * d for d in delta)
        return 1.0 / jnp.sqrt(jnp.sum(squares, axis=-1, keepdims=True) + 1.0)

    xs = [[x_ref[m, j] for j in range(carriers)] for m in range(members)]
    pair = [[jnp.zeros_like(xs[0][0])] * carriers for _ in range(members)]
    for m in range(members):
        for k in range(m + 1, members):
            delta = [p - q for p, q in zip(xs[m], xs[k])]
            inverse = inverse_norm(delta)
            pair[m] = [p + d * inverse for p, d in zip(pair[m], delta)]
            pair[k] = [p - d * inverse for p, d in zip(pair[k], delta)]
    for m in range(members):
        delta = [p - q for p, q in zip(xs[m], target)]
        inverse = inverse_norm(delta)
        for j in range(carriers):
            out_ref[m, j] = weight * (delta[j] * inverse / members - pair[m][j] / (members * members))


def score(grouped, pool, index, count, channels):
    return pl.pallas_call(
        functools.partial(score_body, channels),
        in_specs=[WHOLE] * 4,
        out_specs=WHOLE,
        out_shape=jax.ShapeDtypeStruct(grouped.shape, jnp.float32),
        compiler_params=params(),
        cost_estimate=cost(30 * grouped.size, 8 * grouped.size),
        name="score",
    )(grouped, pool, index, count)


def products_body(
    cuts, scored_ref, slope_ref, w_out_t_ref, latent_t_ref, hidden_t_ref, *refs
):
    out_refs, scratch = refs[:len(cuts)], refs[len(cuts):]
    scored, slope, w_out_t, latent_t, hidden_t, cells, result, in_sems, slope_sems, out_sems = scratch
    parts, carriers, share, _ = scored.shape
    channels, width = w_out_t.shape
    column = column_steps(width)
    scored_copy, w_copy, latent_copy, hidden_copy = (
        pltpu.make_async_copy(source, target, in_sems.at[k])
        for k, (source, target) in enumerate(
            [(scored_ref, scored), (w_out_t_ref, w_out_t), (latent_t_ref, latent_t), (hidden_t_ref, hidden_t)]
        )
    )
    slope_copies = [
        pltpu.make_async_copy(slope_ref.at[:, pl.ds(c.start, c.stop - c.start)], slope.at[:, c], slope_sems.at[k])
        for k, c in enumerate(column)
    ]
    scored_copy.start()
    w_copy.start()
    slope_copies[0].start()
    latent_copy.start()
    for copy in slope_copies[1:]:
        copy.start()
    hidden_copy.start()

    scored_copy.wait()
    for q in range(parts):
        rows = [scored[q, j] for j in range(carriers)]
        for j, value in enumerate(unpack(rows, channels)):
            cells[pl.ds(q * share * PATCH + j, share, stride=PATCH), :] = value
    lane = lax.broadcasted_iota(jnp.int32, cells.shape, 1)
    g = jnp.where(lane < channels, cells[...], 0.0).astype(jnp.bfloat16)

    results = []

    def put(k, c, product):
        result[:, c] = product
        for i, (out_ref, (start, end)) in enumerate(zip(out_refs, cuts)):
            copy = pltpu.make_async_copy(
                result.at[pl.ds(start, end - start), c],
                out_ref.at[:, pl.ds(c.start, c.stop - c.start)],
                out_sems.at[k, i],
            )
            copy.start()
            results.append(copy)

    w_copy.wait()
    for k, c in enumerate(column):
        gh = jnp.dot(g[:, :channels], w_out_t[:, c], preferred_element_type=jnp.float32)
        slope_copies[k].wait()
        gp = (gh * slope[:, c]).astype(jnp.bfloat16)
        if k == 0:
            latent_copy.wait()
        put(k, c, jnp.dot(latent_t[...], gp, preferred_element_type=jnp.float32))
    hidden_copy.wait()
    put(len(column), slice(width, width + LANES), jnp.dot(hidden_t[...], g, preferred_element_type=jnp.float32))
    for copy in results:
        copy.wait()


def products(scored, slope, w_out_t, latent_t, hidden_t, cuts):
    nrows, width = slope.shape
    channels = w_out_t.shape[0]
    picked = latent_t.shape[0]
    steps = len(column_steps(width))
    return pl.pallas_call(
        functools.partial(products_body, tuple(cuts)),
        in_specs=[ANY] * 5,
        out_specs=[ANY] * len(cuts),
        out_shape=[jax.ShapeDtypeStruct((end - start, width + LANES), jnp.float32) for start, end in cuts],
        scratch_shapes=[
            pltpu.VMEM(scored.shape, jnp.float32),
            pltpu.VMEM(slope.shape, jnp.float32),
            pltpu.VMEM(w_out_t.shape, jnp.bfloat16),
            pltpu.VMEM(latent_t.shape, jnp.bfloat16),
            pltpu.VMEM(hidden_t.shape, jnp.bfloat16),
            pltpu.VMEM((nrows, LANES), jnp.float32),
            pltpu.VMEM((picked, width + LANES), jnp.float32),
            pltpu.SemaphoreType.DMA((4,)),
            pltpu.SemaphoreType.DMA((steps,)),
            pltpu.SemaphoreType.DMA((steps + 1, len(cuts))),
        ],
        compiler_params=params(MOST),
        cost_estimate=cost(2 * nrows * width * (channels + picked), 12 * MIB),
        name="products",
    )(scored, slope, w_out_t, latent_t, hidden_t)


def add_body(plans, count, *refs):
    inputs, outputs = refs[:count], refs[count:]
    for out_ref, plan in zip(outputs, plans):
        for at, rows, sources in plan:
            total = None
            for which, low in sources:
                value = inputs[which][low:low + rows]
                total = value if total is None else total + value
            out_ref[at:at + rows] = total


def add_rows(inputs, plans):
    columns = inputs[0].shape[1]
    sizes = [sum(rows for _, rows, _ in plan) for plan in plans]
    return pl.pallas_call(
        functools.partial(add_body, plans, len(inputs)),
        in_specs=[WHOLE] * len(inputs),
        out_specs=[WHOLE] * len(plans),
        out_shape=[jax.ShapeDtypeStruct((size, columns), jnp.float32) for size in sizes],
        compiler_params=params(),
        cost_estimate=cost(3 * sum(sizes) * columns, 12 * sum(sizes) * columns),
        name="add_rows",
    )(*inputs)


def finish_body(across_ref, *refs):
    *rest_refs, first_ref, second_ref = refs
    width = first_ref.shape[1]
    rows = across_ref.shape[1]
    total = across_ref[0]
    for z in range(1, across_ref.shape[0]):
        total = total + across_ref[z]
    last = rest_refs[0][...]
    for ref in rest_refs[1:]:
        last = last + ref[...]
    for low, high, value in ((0, rows, total), (rows, first_ref.shape[0], last)):
        first_ref[low:high] = value[:, :width]
        second_ref[low:high] = value[:, width:width + second_ref.shape[1]]


def finish(across, rest, width, channels):
    height = across.shape[1] + rest[0].shape[0]
    return pl.pallas_call(
        finish_body,
        in_specs=[WHOLE] * (1 + len(rest)),
        out_specs=[WHOLE] * 2,
        out_shape=[
            jax.ShapeDtypeStruct((height, width), jnp.float32),
            jax.ShapeDtypeStruct((height, channels), jnp.float32),
        ],
        compiler_params=params(),
        cost_estimate=cost(across.size, 4 * across.size),
        name="finish",
    )(across, *rest)


def row_order(nz, nx, nc, ny, height):
    near = 2 if nz % 2 == 0 else 1
    far = nz // near
    rc = max(height // 4, 1)
    more = -(-(height - rc) * 2 // 3)
    a_rows = [range(0, more if z % 2 == 0 else height - rc - more) for z in range(nz)]
    b_rows = [range(a_rows[z].stop, height - rc) for z in range(nz)]
    c_rows = range(height - rc, height)
    x_last, y_last, far_last = [[*range(1, n), 0] for n in (nx, ny, far)]

    def part_a(xs):
        return [(x, y, 0, z // near, z % near, r) for x in xs for y in y_last for z in range(nz) for r in a_rows[z]]

    def part_b(ys):
        return [(x, y, 0, z // near, z % near, r) for y in ys for x in x_last for z in range(nz) for r in b_rows[z]]

    def part_c(nears):
        return [(x, y, 1, f, n, r) for n in nears for f in far_last for x in x_last for y in y_last for r in c_rows]

    pieces = [
        part_a(range(1, nx)), part_b(range(1, ny)), part_c(range(1, near)),
        part_c([0]), part_a([0]), part_b([0]),
    ]
    sizes = [len(piece) for piece in pieces]
    half = [row for piece in pieces for row in piece]
    table = np.array([(core, *row) for core in [*range(1, nc), 0] for row in half], np.int32).T
    return table, sizes, near, far, a_rows, b_rows, rc


def shards(latent, w_in, w_out, observed, patch_index, counts):
    rows_in = latent[0, 0]
    nrows, depth = rows_in.shape
    width, channels = w_out.shape
    nz, nt, ny = (lax.axis_size(name) for name in ("member", "tile", "batch"))
    nc, nx = CORES, nt // CORES
    me_z, me_t, me_y = (lax.axis_index(name) for name in ("member", "tile", "batch"))
    me_x, me_c = me_t // nc, me_t % nc
    w_out_t = w_out.T
    height = depth // (nz * nt * ny)
    table, sizes, near, far, a_rows, b_rows, rc = row_order(nz, nx, nc, ny, height)

    share = nrows // PATCH // nz
    packed = decode(rows_in, w_in, w_out_t, nz)
    grouped = lax.all_to_all(packed, "member", split_axis=0, concat_axis=0, tiled=True)

    core, x, y, relative, f, n, row = (jnp.asarray(table[k:k + 1]) for k in range(7))
    z = (f + relative * (me_z // near)) % far * near + (n + relative * (me_z % near)) % near
    tile = (x + me_x) % nx * nc + (core + me_c) % nc
    source = ((z * nt + tile) * ny + (y + me_y) % ny) * height + row
    slope, hidden_t = slopes(source, rows_in, w_in)
    index = lax.dynamic_slice_in_dim(patch_index[0], me_z * share, share, 0)[:, None]
    count = lax.dynamic_slice_in_dim(counts[0], me_z * share, share, 0)[:, None]
    grouped, slope, hidden_t, index, count = lax.optimization_barrier((grouped, slope, hidden_t, index, count))

    scored = score(grouped, observed[0], index, count, channels)
    returned = lax.all_to_all(scored, "member", split_axis=0, concat_axis=0, tiled=True)
    latent_t = ordered_transpose(source, rows_in)
    returned, latent_t = lax.optimization_barrier((returned, latent_t))

    def shift_core(value, j):
        return lax.ppermute(value, "tile", [(t, t // nc * nc + (t % nc + j) % nc) for t in range(nt)])

    def shift_x(value, j):
        return lax.ppermute(value, "tile", [(t, (t // nc + j) % nx * nc + t % nc) for t in range(nt)])

    def shift_y(value, j):
        return lax.ppermute(value, "batch", [(t, (t + j) % ny) for t in range(ny)])

    def shift_near(value, j):
        return lax.ppermute(value, "member", [(t, t // near * near + (t % near + j) % near) for t in range(nz)])

    def shift_far(value, j):
        return lax.ppermute(value, "member", [(t, (t // near + j) % far * near + t % near) for t in range(nz)])

    def send_all(value, others, shift):
        if others == 1:
            return [shift(value, 1)]
        return [shift(v, j + 1) for j, v in enumerate(jnp.split(value, others, axis=0))] if others else []

    na, nb, nc_send, nc_keep, na_keep, nb_keep = sizes
    n_send, n_keep = na + nb + nc_send, nc_keep + na_keep + nb_keep
    half = n_send + n_keep

    other_send, other_keep, own_send, own_keep = products(
        returned, slope, w_out_t, latent_t, hidden_t,
        [(0, n_send), (n_send, half), (half, half + n_send), (half + n_send, 2 * half)],
    )
    core_send = shift_core(other_send, 1)
    core_keep = shift_core(other_keep, 1)
    a_send = own_send[:na] + core_send[:na]
    b_send = own_send[na:na + nb] + core_send[na:na + nb]
    c_send = own_send[na + nb:] + core_send[na + nb:]
    a_got = send_all(a_send, nx - 1, shift_x)
    b_got = send_all(b_send, ny - 1, shift_y)
    c_got = send_all(c_send, near - 1, shift_near)
    inputs = [own_keep, core_keep, *a_got, *b_got, *c_got]
    a_in = range(2, 2 + len(a_got))
    b_in = range(a_in.stop, a_in.stop + len(b_got))
    c_in = range(b_in.stop, b_in.stop + len(c_got))

    def summed(base, got, low, rows):
        return [(0, rows, [(0, base + low), (1, base + low), *[(k, low) for k in got]])]

    a_base, b_base = nc_keep, nc_keep + na_keep
    a_cut, b_cut, c_cut = na_keep // ny * (ny - 1), nb_keep // nx * (nx - 1), nc_keep // far * (far - 1)
    c_send, a_send, b_send = add_rows(
        inputs,
        [
            summed(0, c_in, 0, c_cut),
            summed(a_base, a_in, 0, a_cut),
            summed(b_base, b_in, 0, b_cut),
        ],
    )
    c_got = send_all(c_send, far - 1, shift_far)
    a_got = send_all(a_send, ny - 1, shift_y)
    b_got = send_all(b_send, nx - 1, shift_x)
    c_keep, a_keep, b_keep = add_rows(
        inputs,
        [
            summed(0, c_in, c_cut, nc_keep - c_cut),
            summed(a_base, a_in, a_cut, na_keep - a_cut),
            summed(b_base, b_in, b_cut, nb_keep - b_cut),
        ],
    )

    a_got, b_got, c_got = lax.optimization_barrier((a_got, b_got, c_got))
    inputs = [a_keep, *a_got, b_keep, *b_got]
    plan, a_low, b_low, at = [], 0, 0, 0
    for k in range(nz):
        plan.append((at, len(a_rows[k]), [(i, a_low) for i in range(1 + len(a_got))]))
        a_low, at = a_low + len(a_rows[k]), at + len(a_rows[k])
        plan.append((at, len(b_rows[k]), [(1 + len(a_got) + i, b_low) for i in range(1 + len(b_got))]))
        b_low, at = b_low + len(b_rows[k]), at + len(b_rows[k])
    (joined,) = add_rows(inputs, [plan])
    across = lax.all_to_all(
        joined.reshape(nz, height - rc, joined.shape[1]), "member", split_axis=0, concat_axis=0, tiled=True
    )
    c_rows = c_keep.shape[0]
    cut = c_rows // nx * (nx - 1)
    (c_send, c_keep) = add_rows(
        [c_keep, *c_got],
        [
            [(0, cut, [(i, 0) for i in range(1 + len(c_got))])],
            [(0, c_rows - cut, [(i, cut) for i in range(1 + len(c_got))])],
        ],
    )
    c_got = send_all(c_send, nx - 1, shift_x)
    c_rows = c_keep.shape[0]
    cut = c_rows // ny * (ny - 1)
    (c_send, c_keep) = add_rows(
        [c_keep, *c_got],
        [
            [(0, cut, [(i, 0) for i in range(1 + len(c_got))])],
            [(0, c_rows - cut, [(i, cut) for i in range(1 + len(c_got))])],
        ],
    )
    c_got = send_all(c_send, ny - 1, shift_y)
    return tuple(finish(across, [c_keep, *c_got], width, channels))


def solution(mesh):
    in_specs = (
        P("member", "batch", "tile", None),
        P(),
        P(),
        P("batch", "tile", None),
        P("batch", "tile"),
        P("batch", "tile"),
    )
    out_specs = (P(("member", "tile", "batch"), None), P(("member", "tile", "batch"), None))
    return jax.shard_map(shards, mesh=mesh, in_specs=in_specs, out_specs=out_specs, check_vma=False)
```

```python
import functools

import jax
import jax.numpy as jnp
import numpy as np
from jax import lax
from jax.experimental import pallas as pl
from jax.experimental.pallas import tpu as pltpu
from jax.sharding import PartitionSpec as P

PATCH = 16
CORES = 2
LANES = 128
MIB = 1 << 20
NT = (((1,), (1,)), ((), ()))
WHOLE = pl.BlockSpec()
ANY = pl.BlockSpec(memory_space=pl.ANY)
FEW = 24
TIGHT = 60.3
MOST = 56


def params(mib=24):
    return pltpu.CompilerParams(vmem_limit_bytes=int(mib * MIB))


def cost(flops, moved):
    return pl.CostEstimate(flops=int(flops), bytes_accessed=int(moved), transcendentals=0)


def packing(channels):
    spare = LANES - channels
    carriers = PATCH * channels // LANES
    per_cell = channels // spare
    assert carriers * LANES == PATCH * channels and per_cell * spare == channels
    return spare, carriers, per_cell


def pack(cell, channels):
    spare, carriers, per_cell = packing(channels)
    extra = [cell(j) for j in range(carriers, PATCH)]
    lane = lax.broadcasted_iota(jnp.int32, extra[0].shape, 1)
    rows = []
    for j in range(carriers):
        piece = extra[j // per_cell]
        moved = pltpu.roll(piece, channels - j % per_cell * spare, 1)
        rows.append(jnp.where(lane < channels, cell(j), moved))
    return rows


def unpack(rows, channels):
    spare, carriers, per_cell = packing(channels)
    lane = lax.broadcasted_iota(jnp.int32, rows[0].shape, 1)
    cells = list(rows)
    for first in range(0, carriers, per_cell):
        value = jnp.zeros_like(rows[0])
        for i in range(per_cell):
            moved = pltpu.roll(rows[first + i], (i * spare - channels) % LANES, 1)
            value = jnp.where((lane >= i * spare) & (lane < (i + 1) * spare), moved, value)
        cells.append(value)
    return cells


def column_steps(width):
    step = 256 if width % 256 == 0 else width
    return [slice(low, low + step) for low in range(0, width, step)]


def decode_body(latent_ref, w_in_ref, w_out_t_ref, packed_ref, rows, w_in, w_out_t, cells, packed, row_sems, w_sems, sems):
    parts, block, _ = rows.shape
    channels, width = w_out_t.shape
    share = packed.shape[2]
    column = column_steps(width)
    row_copies = [
        pltpu.make_async_copy(latent_ref.at[pl.ds(q * block, block)], rows.at[q], row_sems.at[q]) for q in range(parts)
    ]
    w_copies = [
        pltpu.make_async_copy(w_in_ref.at[:, pl.ds(c.start, c.stop - c.start)], w_in.at[:, c], w_sems.at[k])
        for k, c in enumerate(column)
    ]
    last_copy = pltpu.make_async_copy(w_out_t_ref, w_out_t, sems.at[parts])
    for copy in [*w_copies, *row_copies[:parts // 2], last_copy, *row_copies[parts // 2:]]:
        copy.start()

    results = []
    for copy in [*w_copies, *row_copies[:parts // 2], last_copy]:
        copy.wait()
    for q in range(parts):
        if q == parts // 2:
            for copy in row_copies[q:]:
                copy.wait()
        preact = jnp.dot(rows[q], w_in[...], preferred_element_type=jnp.float32)
        hidden = (preact / (1.0 + jnp.exp(-preact))).astype(jnp.bfloat16)
        cells[q, :, :channels] = lax.dot_general(hidden, w_out_t[...], NT, preferred_element_type=jnp.float32)
        for j, row in enumerate(pack(lambda j: cells[q, pl.ds(j, share, stride=PATCH), :], channels)):
            packed[q, j] = row
        results.append(pltpu.make_async_copy(packed.at[q], packed_ref.at[q], sems.at[q]))
        results[-1].start()
    for copy in results:
        copy.wait()


def decode(rows_in, w_in, w_out_t, parts):
    nrows, depth = rows_in.shape
    width = w_in.shape[1]
    channels = w_out_t.shape[0]
    block = nrows // parts
    share = block // PATCH
    carriers = packing(channels)[1]
    out = (parts, carriers, share, LANES)
    return pl.pallas_call(
        decode_body,
        in_specs=[ANY] * 3,
        out_specs=ANY,
        out_shape=jax.ShapeDtypeStruct(out, jnp.float32),
        scratch_shapes=[
            pltpu.VMEM((parts, block, depth), jnp.bfloat16),
            pltpu.VMEM((depth, width), jnp.bfloat16),
            pltpu.VMEM((channels, width), jnp.bfloat16),
            pltpu.VMEM((parts, block, LANES), jnp.float32),
            pltpu.VMEM(out, jnp.float32),
            pltpu.SemaphoreType.DMA((parts,)),
            pltpu.SemaphoreType.DMA((len(column_steps(width)),)),
            pltpu.SemaphoreType.DMA((parts + 1,)),
        ],
        compiler_params=params(MOST),
        cost_estimate=cost(2 * nrows * width * (depth + channels), 5 * MIB),
        name="decode",
    )(rows_in, w_in, w_out_t)


def fill_choice(source_ref, choice):
    picked, extent = choice.shape
    for low in range(0, picked, LANES):
        high = min(low + LANES, picked)
        across = jnp.broadcast_to(source_ref[:, low:high], (LANES, high - low))
        down = jnp.transpose(across)
        for left in range(0, extent, LANES):
            here = lax.broadcasted_iota(jnp.int32, down.shape, 1) + left
            choice[low:high, left:left + LANES] = jnp.where(down == here, 1.0, 0.0).astype(jnp.bfloat16)


def slope_body(latent_ref, w_in_ref, slope_ref, hidden_ref):
    preact = jnp.dot(latent_ref[...], w_in_ref[...], preferred_element_type=jnp.float32)
    scale = 1.0 + jnp.exp(-preact)
    sigma = 1.0 / scale
    slope_ref[...] = sigma * (1.0 + preact * (1.0 - sigma))
    hidden_ref[...] = (preact / scale).astype(jnp.bfloat16)


def slopes(rows_in, w_in):
    nrows, depth = rows_in.shape
    width = w_in.shape[1]
    block = 256 if nrows % 256 == 0 else nrows
    return pl.pallas_call(
        slope_body,
        grid=(nrows // block,),
        in_specs=[pl.BlockSpec((block, depth), lambda i: (i, 0)), pl.BlockSpec((depth, width), lambda i: (0, 0))],
        out_specs=[pl.BlockSpec((block, width), lambda i: (i, 0)), pl.BlockSpec((block, width), lambda i: (i, 0))],
        out_shape=[
            jax.ShapeDtypeStruct((nrows, width), jnp.float32),
            jax.ShapeDtypeStruct((nrows, width), jnp.bfloat16),
        ],
        compiler_params=params(MOST),
        cost_estimate=cost(2 * nrows * width * depth, 4 * MIB),
        name="slopes",
    )(rows_in, w_in)


def order_body(source_ref, latent_ref, hidden_ref, out_ref, choice):
    @pl.when(pl.program_id(0) == 0)
    def _():
        fill_choice(source_ref, choice)

    for k, matrix_ref in enumerate((latent_ref, hidden_ref)):
        ordered = lax.dot_general(choice[...], matrix_ref[...], NT, preferred_element_type=jnp.float32)
        out_ref[k] = ordered.astype(jnp.bfloat16)


def ordered_transposes(source, latent, hidden):
    nrows, extent = latent.shape
    picked = source.shape[1]
    block = 256 if nrows % 256 == 0 else nrows
    return pl.pallas_call(
        order_body,
        grid=(nrows // block,),
        in_specs=[
            pl.BlockSpec((1, picked), lambda i: (0, 0)),
            pl.BlockSpec((block, extent), lambda i: (i, 0)),
            pl.BlockSpec((block, extent), lambda i: (i, 0)),
        ],
        out_specs=pl.BlockSpec((2, picked, block), lambda i: (0, 0, i)),
        out_shape=jax.ShapeDtypeStruct((2, picked, nrows), jnp.bfloat16),
        scratch_shapes=[pltpu.VMEM((picked, extent), jnp.bfloat16)],
        compiler_params=params(MOST),
        cost_estimate=cost(nrows * extent * picked, 4 * MIB),
        name="ordered_transposes",
    )(source, latent, hidden)


def score_body(channels, x_ref, pool_ref, index_ref, count_ref, out_ref):
    members, carriers, share, _ = x_ref.shape
    npool, total = pool_ref.shape
    choose = index_ref[...] == lax.broadcasted_iota(jnp.int32, (share, npool), 1)
    flat = jnp.dot(
        jnp.where(choose, 1.0, 0.0).astype(jnp.bfloat16), pool_ref[...], preferred_element_type=jnp.float32
    )
    weight = count_ref[...].astype(jnp.float32)

    def cell(j):
        start = j * channels
        low = start // LANES * LANES
        part = flat[:, low:min(low + 2 * LANES, total)]
        return pltpu.roll(part, (low - start) % part.shape[1], 1)[:, :LANES]

    target = pack(cell, channels)

    def inverse_norm(delta):
        squares = sum(d * d for d in delta)
        return 1.0 / jnp.sqrt(jnp.sum(squares, axis=-1, keepdims=True) + 1.0)

    xs = [[x_ref[m, j] for j in range(carriers)] for m in range(members)]
    pair = [[jnp.zeros_like(xs[0][0])] * carriers for _ in range(members)]
    for m in range(members):
        for k in range(m + 1, members):
            delta = [p - q for p, q in zip(xs[m], xs[k])]
            inverse = inverse_norm(delta)
            pair[m] = [p + d * inverse for p, d in zip(pair[m], delta)]
            pair[k] = [p - d * inverse for p, d in zip(pair[k], delta)]
    for m in range(members):
        delta = [p - q for p, q in zip(xs[m], target)]
        inverse = inverse_norm(delta)
        for j in range(carriers):
            out_ref[m, j] = weight * (delta[j] * inverse / members - pair[m][j] / (members * members))


def score(grouped, pool, index, count, channels):
    return pl.pallas_call(
        functools.partial(score_body, channels),
        in_specs=[WHOLE] * 4,
        out_specs=WHOLE,
        out_shape=jax.ShapeDtypeStruct(grouped.shape, jnp.float32),
        compiler_params=params(),
        cost_estimate=cost(30 * grouped.size, 8 * grouped.size),
        name="score",
    )(grouped, pool, index, count)


def first_body(
    scored_ref, slope_ref, w_out_t_ref, ordered_ref, out_ref, gp_ref, g_ref,
    scored, slope, w_out_t, latent_t, hidden_t, cells, gp, g, result, in_sems, slope_sems, gp_sems, out_sems,
):
    parts, carriers, share, _ = scored.shape
    channels, width = w_out_t.shape
    picked = result.shape[0]
    column = column_steps(width)
    scored_copy, w_copy, hidden_copy, latent_copy = copies = [
        pltpu.make_async_copy(source, target, in_sems.at[k])
        for k, (source, target) in enumerate([
            (scored_ref, scored),
            (w_out_t_ref, w_out_t),
            (ordered_ref.at[1, pl.ds(0, picked)], hidden_t),
            (ordered_ref.at[0, pl.ds(0, picked)], latent_t),
        ])
    ]
    slope_copies = [
        pltpu.make_async_copy(slope_ref.at[:, pl.ds(c.start, c.stop - c.start)], slope.at[:, c], slope_sems.at[k])
        for k, c in enumerate(column)
    ]
    for copy in [*copies, *slope_copies]:
        copy.start()

    scored_copy.wait()
    for q in range(parts):
        rows = [scored[q, j] for j in range(carriers)]
        for j, value in enumerate(unpack(rows, channels)):
            cells[pl.ds(q * share * PATCH + j, share, stride=PATCH), :] = value
    lane = lax.broadcasted_iota(jnp.int32, cells.shape, 1)
    g[...] = jnp.where(lane < channels, cells[...], 0.0).astype(jnp.bfloat16)
    results = [pltpu.make_async_copy(g, g_ref, gp_sems.at[len(column)])]
    results[0].start()

    def put(k, c, product):
        result[:, c] = product
        target = out_ref.at[:, pl.ds(c.start, c.stop - c.start)]
        results.append(pltpu.make_async_copy(result.at[:, c], target, out_sems.at[k]))
        results[-1].start()

    w_copy.wait()
    backward = [
        jnp.dot(g[:, :channels], w_out_t[:, c], preferred_element_type=jnp.float32) for c in column
    ]
    hidden_copy.wait()
    last = slice(width, width + LANES)
    put(len(column), last, jnp.dot(hidden_t[...], g[...], preferred_element_type=jnp.float32))
    latent_copy.wait()
    for k, c in enumerate(column):
        slope_copies[k].wait()
        gp[:, c] = (backward[k] * slope[:, c]).astype(jnp.bfloat16)
        results.append(pltpu.make_async_copy(gp.at[:, c], gp_ref.at[:, pl.ds(c.start, c.stop - c.start)], gp_sems.at[k]))
        results[-1].start()
        put(k, c, jnp.dot(latent_t[...], gp[:, c], preferred_element_type=jnp.float32))
    for copy in results:
        copy.wait()


def first_products(scored, slope, w_out_t, ordered, picked):
    nrows, width = slope.shape
    channels = w_out_t.shape[0]
    steps = len(column_steps(width))
    return pl.pallas_call(
        first_body,
        in_specs=[ANY] * 4,
        out_specs=[ANY] * 3,
        out_shape=[
            jax.ShapeDtypeStruct((picked, width + LANES), jnp.float32),
            jax.ShapeDtypeStruct((nrows, width), jnp.bfloat16),
            jax.ShapeDtypeStruct((nrows, LANES), jnp.bfloat16),
        ],
        scratch_shapes=[
            pltpu.VMEM(scored.shape, jnp.float32),
            pltpu.VMEM(slope.shape, jnp.float32),
            pltpu.VMEM(w_out_t.shape, jnp.bfloat16),
            pltpu.VMEM((picked, nrows), jnp.bfloat16),
            pltpu.VMEM((picked, nrows), jnp.bfloat16),
            pltpu.VMEM((nrows, LANES), jnp.float32),
            pltpu.VMEM((nrows, width), jnp.bfloat16),
            pltpu.VMEM((nrows, LANES), jnp.bfloat16),
            pltpu.VMEM((picked, width + LANES), jnp.float32),
            pltpu.SemaphoreType.DMA((4,)),
            pltpu.SemaphoreType.DMA((steps,)),
            pltpu.SemaphoreType.DMA((steps + 1,)),
            pltpu.SemaphoreType.DMA((steps + 1,)),
        ],
        compiler_params=params(TIGHT),
        cost_estimate=cost(2 * nrows * width * (channels + picked), 10 * MIB),
        name="first_products",
    )(scored, slope, w_out_t, ordered)


def more_body(cuts, gp_ref, g_ref, ordered_ref, *refs):
    out_refs, (gp, g, latent_t, hidden_t, result, in_sems, out_sems) = refs[:len(cuts)], refs[len(cuts):]
    low, picked = cuts[0][0], result.shape[0]
    width = gp.shape[1]
    copies = [
        pltpu.make_async_copy(source, target, in_sems.at[k])
        for k, (source, target) in enumerate([
            (ordered_ref.at[1, pl.ds(low, picked)], hidden_t),
            (g_ref, g),
            (ordered_ref.at[0, pl.ds(low, picked)], latent_t),
            (gp_ref, gp),
        ])
    ]
    for copy in copies:
        copy.start()
    for copy in copies[:2]:
        copy.wait()
    results = []

    def put(k, c, product):
        result[:, c] = product
        for i, (out_ref, (start, end)) in enumerate(zip(out_refs, cuts)):
            source = result.at[pl.ds(start - low, end - start), c]
            target = out_ref.at[:, pl.ds(c.start, c.stop - c.start)]
            results.append(pltpu.make_async_copy(source, target, out_sems.at[k, i]))
            results[-1].start()

    put(0, slice(width, width + LANES), jnp.dot(hidden_t[...], g[...], preferred_element_type=jnp.float32))
    for copy in copies[2:]:
        copy.wait()
    for k, c in enumerate(column_steps(width)):
        put(k + 1, c, jnp.dot(latent_t[...], gp[:, c], preferred_element_type=jnp.float32))
    for copy in results:
        copy.wait()


def more_products(gp, g, ordered, cuts, beside=False):
    nrows, width = gp.shape
    picked = cuts[-1][1] - cuts[0][0]
    return pl.pallas_call(
        functools.partial(more_body, tuple(cuts)),
        in_specs=[ANY] * 3,
        out_specs=[ANY] * len(cuts),
        out_shape=[jax.ShapeDtypeStruct((end - start, width + LANES), jnp.float32) for start, end in cuts],
        scratch_shapes=[
            pltpu.VMEM((nrows, width), jnp.bfloat16),
            pltpu.VMEM((nrows, LANES), jnp.bfloat16),
            pltpu.VMEM((picked, nrows), jnp.bfloat16),
            pltpu.VMEM((picked, nrows), jnp.bfloat16),
            pltpu.VMEM((picked, width + LANES), jnp.float32),
            pltpu.SemaphoreType.DMA((4,)),
            pltpu.SemaphoreType.DMA((len(column_steps(width)) + 1, len(cuts))),
        ],
        compiler_params=params(FEW if beside else TIGHT),
        cost_estimate=cost(0, 0) if beside else cost(2 * nrows * picked * width, 6 * MIB),
        name="more_products",
    )(gp, g, ordered)


def add_body(plans, count, *refs):
    inputs, outputs = refs[:count], refs[count:]
    for out_ref, plan in zip(outputs, plans):
        for at, rows, sources in plan:
            total = None
            for which, low in sources:
                value = inputs[which][low:low + rows]
                total = value if total is None else total + value
            out_ref[at:at + rows] = total


def add_rows(inputs, plans):
    columns = inputs[0].shape[1]
    sizes = [sum(rows for _, rows, _ in plan) for plan in plans]
    return pl.pallas_call(
        functools.partial(add_body, plans, len(inputs)),
        in_specs=[WHOLE] * len(inputs),
        out_specs=[WHOLE] * len(plans),
        out_shape=[jax.ShapeDtypeStruct((size, columns), jnp.float32) for size in sizes],
        compiler_params=params(),
        cost_estimate=cost(3 * sum(sizes) * columns, 12 * sum(sizes) * columns),
        name="add_rows",
    )(*inputs)


def finish_body(across_ref, *refs):
    *rest_refs, first_ref, second_ref = refs
    width = first_ref.shape[1]
    rows = across_ref.shape[1]
    total = across_ref[0]
    for z in range(1, across_ref.shape[0]):
        total = total + across_ref[z]
    last = rest_refs[0][...]
    for ref in rest_refs[1:]:
        last = last + ref[...]
    for low, high, value in ((0, rows, total), (rows, first_ref.shape[0], last)):
        first_ref[low:high] = value[:, :width]
        second_ref[low:high] = value[:, width:width + second_ref.shape[1]]


def finish(across, rest, width, channels):
    height = across.shape[1] + rest[0].shape[0]
    return pl.pallas_call(
        finish_body,
        in_specs=[WHOLE] * (1 + len(rest)),
        out_specs=[WHOLE] * 2,
        out_shape=[
            jax.ShapeDtypeStruct((height, width), jnp.float32),
            jax.ShapeDtypeStruct((height, channels), jnp.float32),
        ],
        compiler_params=params(),
        cost_estimate=cost(across.size, 4 * across.size),
        name="finish",
    )(across, *rest)


def row_order(nz, nx, nc, ny, height):
    near = 2 if nz % 2 == 0 else 1
    far = nz // near
    rc = max(height // 4, 1)
    more = -(-(height - rc) * 2 // 3)
    a_rows = [range(0, more if z % 2 == 0 else height - rc - more) for z in range(nz)]
    b_rows = [range(a_rows[z].stop, height - rc) for z in range(nz)]
    c_rows = range(height - rc, height)
    x_last, y_last, far_last = [[*range(1, n), 0] for n in (nx, ny, far)]

    def part_a(xs):
        return [(x, y, 0, z // near, z % near, r) for x in xs for y in y_last for z in range(nz) for r in a_rows[z]]

    def part_b(ys):
        return [(x, y, 0, z // near, z % near, r) for y in ys for x in x_last for z in range(nz) for r in b_rows[z]]

    def part_c(nears):
        return [(x, y, 1, f, n, r) for n in nears for f in far_last for x in x_last for y in y_last for r in c_rows]

    pieces = [
        part_a(range(1, nx)), part_b(range(1, ny)), part_c(range(1, near)),
        part_c([0]), part_a([0]), part_b([0]),
    ]
    sizes = [len(piece) for piece in pieces]
    cores = [*range(1, nc), 0]
    halves = [[row for piece in part for row in piece] for part in (pieces[:3], pieces[3:])]
    table = np.array([(core, *row) for half in halves for core in cores for row in half], np.int32).T
    return table, sizes, near, far, a_rows, b_rows, rc


def shards(latent, w_in, w_out, observed, patch_index, counts):
    rows_in = latent[0, 0]
    nrows, depth = rows_in.shape
    width, channels = w_out.shape
    nz, nt, ny = (lax.axis_size(name) for name in ("member", "tile", "batch"))
    nc, nx = CORES, nt // CORES
    me_z, me_t, me_y = (lax.axis_index(name) for name in ("member", "tile", "batch"))
    me_x, me_c = me_t // nc, me_t % nc
    w_out_t = w_out.T
    height = depth // (nz * nt * ny)
    table, sizes, near, far, a_rows, b_rows, rc = row_order(nz, nx, nc, ny, height)

    share = nrows // PATCH // nz
    packed = decode(rows_in, w_in, w_out_t, nz)
    grouped = lax.all_to_all(packed, "member", split_axis=0, concat_axis=0, tiled=True)

    core, x, y, relative, f, n, row = (jnp.asarray(table[k:k + 1]) for k in range(7))
    z = (f + relative * (me_z // near)) % far * near + (n + relative * (me_z % near)) % near
    tile = (x + me_x) % nx * nc + (core + me_c) % nc
    source = ((z * nt + tile) * ny + (y + me_y) % ny) * height + row
    slope, hidden = slopes(rows_in, w_in)
    index = lax.dynamic_slice_in_dim(patch_index[0], me_z * share, share, 0)[:, None]
    count = lax.dynamic_slice_in_dim(counts[0], me_z * share, share, 0)[:, None]
    grouped, slope, hidden, source, index, count = lax.optimization_barrier(
        (grouped, slope, hidden, source, index, count)
    )

    scored = score(grouped, observed[0], index, count, channels)
    returned = lax.all_to_all(scored, "member", split_axis=0, concat_axis=0, tiled=True)
    ordered = ordered_transposes(source, rows_in, hidden)
    returned, ordered = lax.optimization_barrier((returned, ordered))

    def shift_core(value, j):
        return lax.ppermute(value, "tile", [(t, t // nc * nc + (t % nc + j) % nc) for t in range(nt)])

    def shift_x(value, j):
        return lax.ppermute(value, "tile", [(t, (t // nc + j) % nx * nc + t % nc) for t in range(nt)])

    def shift_y(value, j):
        return lax.ppermute(value, "batch", [(t, (t + j) % ny) for t in range(ny)])

    def shift_near(value, j):
        return lax.ppermute(value, "member", [(t, t // near * near + (t % near + j) % near) for t in range(nz)])

    def shift_far(value, j):
        return lax.ppermute(value, "member", [(t, (t // near + j) % far * near + t % near) for t in range(nz)])

    def send_all(value, others, shift):
        if others == 1:
            return [shift(value, 1)]
        return [shift(v, j + 1) for j, v in enumerate(jnp.split(value, others, axis=0))] if others else []

    na, nb, nc_send, nc_keep, na_keep, nb_keep = sizes
    n_send, n_keep = na + nb + nc_send, nc_keep + na_keep + nb_keep
    middle = 2 * n_send

    other_send, gp, g = first_products(returned, slope, w_out_t, ordered, n_send)
    core_send = shift_core(other_send, 1)
    (own_send,) = more_products(gp, g, ordered, [(n_send, middle)])
    a_send, b_send, c_send = add_rows(
        [own_send, core_send],
        [
            [(0, na, [(0, 0), (1, 0)])],
            [(0, nb, [(0, na), (1, na)])],
            [(0, nc_send, [(0, na + nb), (1, na + nb)])],
        ],
    )
    a_send, b_send, c_send, gp = lax.optimization_barrier((a_send, b_send, c_send, gp))
    a_got = send_all(a_send, nx - 1, shift_x)
    b_got = send_all(b_send, ny - 1, shift_y)
    c_got = send_all(c_send, near - 1, shift_near)
    a_cut, b_cut, c_cut = na_keep // ny * (ny - 1), nb_keep // nx * (nx - 1), nc_keep // far * (far - 1)
    keeps = [c_cut, nc_keep - c_cut, a_cut, na_keep - a_cut, b_cut, nb_keep - b_cut]
    offsets = [int(low) for low in np.cumsum([0, *keeps])]
    third = -(-n_keep // 24) * 8
    parts = [0, min(third, n_keep), min(2 * third, n_keep), n_keep]
    ends = [middle + low for low in parts]
    *other_keep, own_keep = more_products(
        gp, g, ordered, [*zip(ends[:-1], ends[1:]), (ends[-1], ends[-1] + n_keep)], True
    )
    core_keep = [shift_core(value, 1) for value in other_keep]

    def summed(k, got, low):
        plan = []
        for i, (start, end) in enumerate(zip(parts[:-1], parts[1:])):
            start, end = max(start, offsets[k]), min(end, offsets[k + 1])
            if start < end:
                at = start - offsets[k]
                terms = [(0, start), (1 + i, start - parts[i])]
                terms += [(1 + len(core_keep) + n, low + at) for n in range(len(got))]
                plan.append((at, end - start, terms))
        return [own_keep, *core_keep, *got], plan

    def sums(*parts):
        inputs, plans = [], []
        for sources, plan in parts:
            plans.append([(at, rows, [(len(inputs) + i, low) for i, low in terms]) for at, rows, terms in plan])
            inputs.extend(sources)
        return add_rows(inputs, plans)

    c_send, a_send, b_send = sums(summed(0, c_got, 0), summed(2, a_got, 0), summed(4, b_got, 0))
    keep_sums = [summed(1, c_got, c_cut), summed(3, a_got, a_cut), summed(5, b_got, b_cut)]
    c_got = send_all(c_send, far - 1, shift_far)
    a_got = send_all(a_send, ny - 1, shift_y)
    b_got = send_all(b_send, nx - 1, shift_x)
    c_keep, a_keep, b_keep = sums(*keep_sums)

    a_got, b_got, c_got = lax.optimization_barrier((a_got, b_got, c_got))
    inputs = [a_keep, *a_got, b_keep, *b_got]
    plan, a_low, b_low, at = [], 0, 0, 0
    for k in range(nz):
        plan.append((at, len(a_rows[k]), [(i, a_low) for i in range(1 + len(a_got))]))
        a_low, at = a_low + len(a_rows[k]), at + len(a_rows[k])
        plan.append((at, len(b_rows[k]), [(1 + len(a_got) + i, b_low) for i in range(1 + len(b_got))]))
        b_low, at = b_low + len(b_rows[k]), at + len(b_rows[k])
    (joined,) = add_rows(inputs, [plan])
    across = lax.all_to_all(
        joined.reshape(nz, height - rc, joined.shape[1]), "member", split_axis=0, concat_axis=0, tiled=True
    )
    c_rows = c_keep.shape[0]
    cut = c_rows // nx * (nx - 1)
    (c_send, c_keep) = add_rows(
        [c_keep, *c_got],
        [
            [(0, cut, [(i, 0) for i in range(1 + len(c_got))])],
            [(0, c_rows - cut, [(i, cut) for i in range(1 + len(c_got))])],
        ],
    )
    c_got = send_all(c_send, nx - 1, shift_x)
    c_rows = c_keep.shape[0]
    cut = c_rows // ny * (ny - 1)
    (c_send, c_keep) = add_rows(
        [c_keep, *c_got],
        [
            [(0, cut, [(i, 0) for i in range(1 + len(c_got))])],
            [(0, c_rows - cut, [(i, cut) for i in range(1 + len(c_got))])],
        ],
    )
    c_got = send_all(c_send, ny - 1, shift_y)
    return tuple(finish(across, [c_keep, *c_got], width, channels))


def solution(mesh):
    in_specs = (
        P("member", "batch", "tile", None),
        P(),
        P(),
        P("batch", "tile", None),
        P("batch", "tile"),
        P("batch", "tile"),
    )
    out_specs = (P(("member", "tile", "batch"), None), P(("member", "tile", "batch"), None))
    return jax.shard_map(shards, mesh=mesh, in_specs=in_specs, out_specs=out_specs, check_vma=False)
```

```python
import functools

import jax
import jax.numpy as jnp
import numpy as np
from jax import lax
from jax.experimental import pallas as pl
from jax.experimental.pallas import tpu as pltpu
from jax.sharding import PartitionSpec as P

PATCH = 16
CORES = 2
LANES = 128
MIB = 1 << 20
NT = (((1,), (1,)), ((), ()))
WHOLE = pl.BlockSpec()
ANY = pl.BlockSpec(memory_space=pl.ANY)
FEW = 24
MOST = 56


def params(mib=24):
    return pltpu.CompilerParams(vmem_limit_bytes=int(mib * MIB))


def cost(flops, moved):
    return pl.CostEstimate(flops=int(flops), bytes_accessed=int(moved), transcendentals=0)


def packing(channels):
    spare = LANES - channels
    carriers = PATCH * channels // LANES
    per_cell = channels // spare
    assert carriers * LANES == PATCH * channels and per_cell * spare == channels
    return spare, carriers, per_cell


def pack(cell, channels):
    spare, carriers, per_cell = packing(channels)
    extra = [cell(j) for j in range(carriers, PATCH)]
    lane = lax.broadcasted_iota(jnp.int32, extra[0].shape, 1)
    rows = []
    for j in range(carriers):
        piece = extra[j // per_cell]
        moved = pltpu.roll(piece, channels - j % per_cell * spare, 1)
        rows.append(jnp.where(lane < channels, cell(j), moved))
    return rows


def unpack(rows, channels):
    spare, carriers, per_cell = packing(channels)
    lane = lax.broadcasted_iota(jnp.int32, rows[0].shape, 1)
    cells = list(rows)
    for first in range(0, carriers, per_cell):
        value = jnp.zeros_like(rows[0])
        for i in range(per_cell):
            moved = pltpu.roll(rows[first + i], (i * spare - channels) % LANES, 1)
            value = jnp.where((lane >= i * spare) & (lane < (i + 1) * spare), moved, value)
        cells.append(value)
    return cells


def in_hbm(value):
    return pltpu.with_memory_space_constraint(value, pltpu.HBM)


def column_steps(width):
    step = 256 if width % 256 == 0 else width
    return [slice(low, low + step) for low in range(0, width, step)]


def decode_body(latent_ref, w_in_ref, w_out_t_ref, packed_ref, rows, w_in, w_out_t, cells, packed, row_sems, w_sems, sems):
    parts, block, _ = rows.shape
    channels, width = w_out_t.shape
    share = packed.shape[2]
    column = column_steps(width)
    row_copies = [
        pltpu.make_async_copy(latent_ref.at[pl.ds(q * block, block)], rows.at[q], row_sems.at[q]) for q in range(parts)
    ]
    w_copies = [
        pltpu.make_async_copy(w_in_ref.at[:, pl.ds(c.start, c.stop - c.start)], w_in.at[:, c], w_sems.at[k])
        for k, c in enumerate(column)
    ]
    last_copy = pltpu.make_async_copy(w_out_t_ref, w_out_t, sems.at[parts])
    for copy in [*w_copies, *row_copies[:parts // 2], last_copy, *row_copies[parts // 2:]]:
        copy.start()

    results = []
    for copy in [*w_copies, *row_copies[:parts // 2], last_copy]:
        copy.wait()
    for q in range(parts):
        if q == parts // 2:
            for copy in row_copies[q:]:
                copy.wait()
        preact = jnp.dot(rows[q], w_in[...], preferred_element_type=jnp.float32)
        hidden = (preact / (1.0 + jnp.exp(-preact))).astype(jnp.bfloat16)
        cells[q, :, :channels] = lax.dot_general(hidden, w_out_t[...], NT, preferred_element_type=jnp.float32)
        for j, row in enumerate(pack(lambda j: cells[q, pl.ds(j, share, stride=PATCH), :], channels)):
            packed[q, j] = row
        results.append(pltpu.make_async_copy(packed.at[q], packed_ref.at[q], sems.at[q]))
        results[-1].start()
    for copy in results:
        copy.wait()


def decode(rows_in, w_in, w_out_t, parts):
    nrows, depth = rows_in.shape
    width = w_in.shape[1]
    channels = w_out_t.shape[0]
    block = nrows // parts
    share = block // PATCH
    carriers = packing(channels)[1]
    out = (parts, carriers, share, LANES)
    return pl.pallas_call(
        decode_body,
        in_specs=[ANY] * 3,
        out_specs=ANY,
        out_shape=jax.ShapeDtypeStruct(out, jnp.float32),
        scratch_shapes=[
            pltpu.VMEM((parts, block, depth), jnp.bfloat16),
            pltpu.VMEM((depth, width), jnp.bfloat16),
            pltpu.VMEM((channels, width), jnp.bfloat16),
            pltpu.VMEM((parts, block, LANES), jnp.float32),
            pltpu.VMEM(out, jnp.float32),
            pltpu.SemaphoreType.DMA((parts,)),
            pltpu.SemaphoreType.DMA((len(column_steps(width)),)),
            pltpu.SemaphoreType.DMA((parts + 1,)),
        ],
        compiler_params=params(MOST),
        cost_estimate=cost(2 * nrows * width * (depth + channels), 5 * MIB),
        name="decode",
    )(rows_in, w_in, w_out_t)


def fill_choice(source_ref, choice):
    picked, extent = choice.shape
    for low in range(0, picked, LANES):
        high = min(low + LANES, picked)
        across = jnp.broadcast_to(source_ref[:, low:high], (LANES, high - low))
        down = jnp.transpose(across)
        for left in range(0, extent, LANES):
            here = lax.broadcasted_iota(jnp.int32, down.shape, 1) + left
            choice[low:high, left:left + LANES] = jnp.where(down == here, 1.0, 0.0).astype(jnp.bfloat16)


def slope_body(latent_ref, w_in_ref, slope_ref, hidden_ref):
    preact = jnp.dot(latent_ref[...], w_in_ref[...], preferred_element_type=jnp.float32)
    scale = 1.0 + jnp.exp(-preact)
    sigma = 1.0 / scale
    slope_ref[...] = sigma * (1.0 + preact * (1.0 - sigma))
    hidden_ref[...] = (preact / scale).astype(jnp.bfloat16)


def slopes(rows_in, w_in):
    nrows, depth = rows_in.shape
    width = w_in.shape[1]
    block = 256 if nrows % 256 == 0 else nrows
    return pl.pallas_call(
        slope_body,
        grid=(nrows // block,),
        in_specs=[pl.BlockSpec((block, depth), lambda i: (i, 0)), pl.BlockSpec((depth, width), lambda i: (0, 0))],
        out_specs=[pl.BlockSpec((block, width), lambda i: (i, 0)), pl.BlockSpec((block, width), lambda i: (i, 0))],
        out_shape=[
            jax.ShapeDtypeStruct((nrows, width), jnp.float32),
            jax.ShapeDtypeStruct((nrows, width), jnp.bfloat16),
        ],
        compiler_params=params(MOST),
        cost_estimate=cost(2 * nrows * width * depth, 4 * MIB),
        name="slopes",
    )(rows_in, w_in)


def order_body(source_ref, latent_ref, hidden_ref, out_ref, choice):
    @pl.when(pl.program_id(0) == 0)
    def _():
        fill_choice(source_ref, choice)

    for k, matrix_ref in enumerate((latent_ref, hidden_ref)):
        ordered = lax.dot_general(choice[...], matrix_ref[...], NT, preferred_element_type=jnp.float32)
        out_ref[k] = ordered.astype(jnp.bfloat16)


def ordered_transposes(source, latent, hidden):
    nrows, extent = latent.shape
    picked = source.shape[1]
    block = 256 if nrows % 256 == 0 else nrows
    return pl.pallas_call(
        order_body,
        grid=(nrows // block,),
        in_specs=[
            pl.BlockSpec((1, picked), lambda i: (0, 0)),
            pl.BlockSpec((block, extent), lambda i: (i, 0)),
            pl.BlockSpec((block, extent), lambda i: (i, 0)),
        ],
        out_specs=pl.BlockSpec((2, picked, block), lambda i: (0, 0, i)),
        out_shape=jax.ShapeDtypeStruct((2, picked, nrows), jnp.bfloat16),
        scratch_shapes=[pltpu.VMEM((picked, extent), jnp.bfloat16)],
        compiler_params=params(MOST),
        cost_estimate=cost(nrows * extent * picked, 4 * MIB),
        name="ordered_transposes",
    )(source, latent, hidden)


def score_body(channels, x_ref, pool_ref, index_ref, count_ref, out_ref):
    members, carriers, share, _ = x_ref.shape
    npool, total = pool_ref.shape
    choose = index_ref[...] == lax.broadcasted_iota(jnp.int32, (share, npool), 1)
    flat = jnp.dot(
        jnp.where(choose, 1.0, 0.0).astype(jnp.bfloat16), pool_ref[...], preferred_element_type=jnp.float32
    )
    weight = count_ref[...].astype(jnp.float32)

    def cell(j):
        start = j * channels
        low = start // LANES * LANES
        part = flat[:, low:min(low + 2 * LANES, total)]
        return pltpu.roll(part, (low - start) % part.shape[1], 1)[:, :LANES]

    target = pack(cell, channels)

    def inverse_norm(delta):
        squares = sum(d * d for d in delta)
        return 1.0 / jnp.sqrt(jnp.sum(squares, axis=-1, keepdims=True) + 1.0)

    xs = [[x_ref[m, j] for j in range(carriers)] for m in range(members)]
    pair = [[jnp.zeros_like(xs[0][0])] * carriers for _ in range(members)]
    for m in range(members):
        for k in range(m + 1, members):
            delta = [p - q for p, q in zip(xs[m], xs[k])]
            inverse = inverse_norm(delta)
            pair[m] = [p + d * inverse for p, d in zip(pair[m], delta)]
            pair[k] = [p - d * inverse for p, d in zip(pair[k], delta)]
    for m in range(members):
        delta = [p - q for p, q in zip(xs[m], target)]
        inverse = inverse_norm(delta)
        for j in range(carriers):
            out_ref[m, j] = weight * (delta[j] * inverse / members - pair[m][j] / (members * members))


def score(grouped, pool, index, count, channels):
    return pl.pallas_call(
        functools.partial(score_body, channels),
        in_specs=[WHOLE] * 4,
        out_specs=WHOLE,
        out_shape=jax.ShapeDtypeStruct(grouped.shape, jnp.float32),
        compiler_params=params(),
        cost_estimate=cost(30 * grouped.size, 8 * grouped.size),
        name="score",
    )(grouped, pool, index, count)


def first_body(
    scored, slope_ref, w_out_t_ref, ordered_ref, result, gp, g,
    slope, w_out_t, latent_t, hidden_t, cells, in_sems, slope_sems,
):
    parts, carriers, share, _ = scored.shape
    channels, width = w_out_t.shape
    picked = result.shape[0]
    column = column_steps(width)
    w_copy, hidden_copy, latent_copy = copies = [
        pltpu.make_async_copy(source, target, in_sems.at[k])
        for k, (source, target) in enumerate([
            (w_out_t_ref, w_out_t),
            (ordered_ref.at[1, pl.ds(0, picked)], hidden_t),
            (ordered_ref.at[0, pl.ds(0, picked)], latent_t),
        ])
    ]
    slope_copies = [
        pltpu.make_async_copy(slope_ref.at[:, pl.ds(c.start, c.stop - c.start)], slope.at[:, c], slope_sems.at[k])
        for k, c in enumerate(column)
    ]
    for copy in [*copies, *slope_copies]:
        copy.start()

    for q in range(parts):
        rows = [scored[q, j] for j in range(carriers)]
        for j, value in enumerate(unpack(rows, channels)):
            cells[pl.ds(q * share * PATCH + j, share, stride=PATCH), :] = value
    lane = lax.broadcasted_iota(jnp.int32, cells.shape, 1)
    g[...] = jnp.where(lane < channels, cells[...], 0.0).astype(jnp.bfloat16)
    w_copy.wait()
    backward = [
        jnp.dot(g[:, :channels], w_out_t[:, c], preferred_element_type=jnp.float32) for c in column
    ]
    hidden_copy.wait()
    result[:, width:] = jnp.dot(hidden_t[...], g[...], preferred_element_type=jnp.float32)
    latent_copy.wait()
    for k, c in enumerate(column):
        slope_copies[k].wait()
        gp[:, c] = (backward[k] * slope[:, c]).astype(jnp.bfloat16)
        result[:, c] = jnp.dot(latent_t[...], gp[:, c], preferred_element_type=jnp.float32)


def first_products(scored, slope, w_out_t, ordered, picked):
    nrows, width = slope.shape
    channels = w_out_t.shape[0]
    steps = len(column_steps(width))
    return pl.pallas_call(
        first_body,
        in_specs=[WHOLE, ANY, ANY, ANY],
        out_specs=[WHOLE] * 3,
        out_shape=[
            jax.ShapeDtypeStruct((picked, width + LANES), jnp.float32),
            jax.ShapeDtypeStruct((nrows, width), jnp.bfloat16),
            jax.ShapeDtypeStruct((nrows, LANES), jnp.bfloat16),
        ],
        scratch_shapes=[
            pltpu.VMEM(slope.shape, jnp.float32),
            pltpu.VMEM(w_out_t.shape, jnp.bfloat16),
            pltpu.VMEM((picked, nrows), jnp.bfloat16),
            pltpu.VMEM((picked, nrows), jnp.bfloat16),
            pltpu.VMEM((nrows, LANES), jnp.float32),
            pltpu.SemaphoreType.DMA((3,)),
            pltpu.SemaphoreType.DMA((steps,)),
        ],
        compiler_params=params(FEW),
        cost_estimate=cost(2 * nrows * width * (channels + picked), 10 * MIB),
        name="first_products",
    )(scored, in_hbm(slope), in_hbm(w_out_t), in_hbm(ordered))


def more_body(cuts, gp, g, ordered_ref, *refs):
    out_refs, (latent_t, hidden_t, in_sems) = refs[:len(cuts)], refs[len(cuts):]
    low, (picked, _) = cuts[0][0], latent_t.shape
    width = gp.shape[1]
    copies = [
        pltpu.make_async_copy(ordered_ref.at[k, pl.ds(low, picked)], target, in_sems.at[k])
        for k, target in enumerate((latent_t, hidden_t))
    ]
    for copy in copies:
        copy.start()

    def put(columns, product):
        for out_ref, (start, end) in zip(out_refs, cuts):
            out_ref[:, columns] = product[start - low:end - low]

    for copy in copies:
        copy.wait()
    for columns in column_steps(width):
        put(columns, jnp.dot(latent_t[...], gp[:, columns], preferred_element_type=jnp.float32))
    put(slice(width, None), jnp.dot(hidden_t[...], g[...], preferred_element_type=jnp.float32))


def more_products(gp, g, ordered, cuts):
    nrows, width = gp.shape
    picked = cuts[-1][1] - cuts[0][0]
    return pl.pallas_call(
        functools.partial(more_body, tuple(cuts)),
        in_specs=[WHOLE, WHOLE, ANY],
        out_specs=[WHOLE] * len(cuts),
        out_shape=[jax.ShapeDtypeStruct((end - start, width + LANES), jnp.float32) for start, end in cuts],
        scratch_shapes=[
            pltpu.VMEM((picked, nrows), jnp.bfloat16),
            pltpu.VMEM((picked, nrows), jnp.bfloat16),
            pltpu.SemaphoreType.DMA((2,)),
        ],
        compiler_params=params(FEW),
        cost_estimate=cost(2 * nrows * picked * width, 6 * MIB),
        name="more_products",
    )(gp, g, in_hbm(ordered))


def add_body(plans, count, *refs):
    inputs, outputs = refs[:count], refs[count:]
    for out_ref, plan in zip(outputs, plans):
        for at, rows, sources in plan:
            total = None
            for which, low in sources:
                value = inputs[which][low:low + rows]
                total = value if total is None else total + value
            out_ref[at:at + rows] = total


def add_rows(inputs, plans):
    columns = inputs[0].shape[1]
    sizes = [sum(rows for _, rows, _ in plan) for plan in plans]
    return pl.pallas_call(
        functools.partial(add_body, plans, len(inputs)),
        in_specs=[WHOLE] * len(inputs),
        out_specs=[WHOLE] * len(plans),
        out_shape=[jax.ShapeDtypeStruct((size, columns), jnp.float32) for size in sizes],
        compiler_params=params(),
        cost_estimate=cost(3 * sum(sizes) * columns, 12 * sum(sizes) * columns),
        name="add_rows",
    )(*inputs)


def finish_body(across_ref, *refs):
    *rest_refs, first_ref, second_ref = refs
    width = first_ref.shape[1]
    rows = across_ref.shape[1]
    total = across_ref[0]
    for z in range(1, across_ref.shape[0]):
        total = total + across_ref[z]
    last = rest_refs[0][...]
    for ref in rest_refs[1:]:
        last = last + ref[...]
    for low, high, value in ((0, rows, total), (rows, first_ref.shape[0], last)):
        first_ref[low:high] = value[:, :width]
        second_ref[low:high] = value[:, width:width + second_ref.shape[1]]


def finish(across, rest, width, channels):
    height = across.shape[1] + rest[0].shape[0]
    return pl.pallas_call(
        finish_body,
        in_specs=[WHOLE] * (1 + len(rest)),
        out_specs=[WHOLE] * 2,
        out_shape=[
            jax.ShapeDtypeStruct((height, width), jnp.float32),
            jax.ShapeDtypeStruct((height, channels), jnp.float32),
        ],
        compiler_params=params(),
        cost_estimate=cost(across.size, 4 * across.size),
        name="finish",
    )(across, *rest)


def row_order(nz, nx, nc, ny, height):
    near = 2 if nz % 2 == 0 else 1
    far = nz // near
    rc = max(height // 4, 1)
    main_rows, c_rows = range(height - rc), range(height - rc, height)
    first_last, second_last, far_last = [[*range(1, n), 0] for n in (nx, ny, far)]

    def main(firsts):
        return [(f, s, 0, z // near, z % near, r) for f in firsts for s in second_last for z in range(nz) for r in main_rows]

    def part_c(nears):
        return [(f, s, 1, o, n, r) for n in nears for o in far_last for f in first_last for s in second_last for r in c_rows]

    pieces = [main(range(1, nx)), part_c(range(1, near)), part_c([0]), main([0])]
    sizes = [len(piece) for piece in pieces]
    cores = [*range(1, nc), 0]
    halves = [[row for piece in part for row in piece] for part in (pieces[:2], pieces[2:])]
    table = np.array([(core, *row) for half in halves for core in cores for row in half], np.int32).T
    return table, sizes, near, far, rc


def shards(latent, w_in, w_out, observed, patch_index, counts):
    rows_in = latent[0, 0]
    nrows, depth = rows_in.shape
    width, channels = w_out.shape
    nz, nt, ny = (lax.axis_size(name) for name in ("member", "tile", "batch"))
    nc, nx = CORES, nt // CORES
    me_z, me_t, me_y = (lax.axis_index(name) for name in ("member", "tile", "batch"))
    me_x, me_c = me_t // nc, me_t % nc
    w_out_t = w_out.T
    height = depth // (nz * nt * ny)
    table, sizes, near, far, rc = row_order(nz, nx, nc, ny, height)
    turned = 1 if nx == ny else 0

    share = nrows // PATCH // nz
    packed = decode(rows_in, w_in, w_out_t, nz)
    grouped = lax.all_to_all(packed, "member", split_axis=0, concat_axis=0, tiled=True)

    core, first, second, relative, f, n, row = (jnp.asarray(table[k:k + 1]) for k in range(7))
    z = (f + relative * (me_z // near)) % far * near + (n + relative * (me_z % near)) % near
    core = (core + me_c) % nc
    turn = core * turned
    x, y = first + turn * (second - first), second + turn * (first - second)
    tile = (x + me_x) % nx * nc + core
    source = ((z * nt + tile) * ny + (y + me_y) % ny) * height + row
    slope, hidden = slopes(rows_in, w_in)
    index = lax.dynamic_slice_in_dim(patch_index[0], me_z * share, share, 0)[:, None]
    count = lax.dynamic_slice_in_dim(counts[0], me_z * share, share, 0)[:, None]
    grouped, slope, hidden, source, index, count = lax.optimization_barrier(
        (grouped, slope, hidden, source, index, count)
    )

    scored = score(grouped, observed[0], index, count, channels)
    returned = lax.all_to_all(scored, "member", split_axis=0, concat_axis=0, tiled=True)
    ordered = ordered_transposes(source, rows_in, hidden)
    returned, ordered = lax.optimization_barrier((returned, ordered))

    everywhere = [(z, x, c, y) for z in range(nz) for x in range(nx) for c in range(nc) for y in range(ny)]

    def shift(value, target):
        def number(z, x, c, y):
            return (z * nt + x * nc + c) * ny + y

        return lax.ppermute(
            value, ("member", "tile", "batch"), [(number(*place), number(*target(*place))) for place in everywhere]
        )

    def shift_core(value, j):
        return shift(value, lambda z, x, c, y: (z, x, (c + j) % nc, y))

    def along(of_core):
        def shift_one(value, j):
            def target(z, x, c, y):
                return (z, (x + j) % nx, c, y) if of_core(c) == 0 else (z, x, c, (y + j) % ny)

            return shift(value, target)

        return shift_one

    shift_first, shift_second = along(lambda c: c * turned), along(lambda c: 1 - c * turned)

    def shift_near(value, j):
        return shift(value, lambda z, x, c, y: (z // near * near + (z + j) % near, x, c, y))

    def shift_far(value, j):
        return shift(value, lambda z, x, c, y: ((z // near + j) % far * near + z % near, x, c, y))

    def send_all(value, others, shift_one):
        if others == 1:
            return [shift_one(value, 1)]
        return [shift_one(v, j + 1) for j, v in enumerate(jnp.split(value, others, axis=0))] if others else []

    n_main, nc_send, nc_keep, main_keep = sizes
    n_send, n_keep = n_main + nc_send, nc_keep + main_keep
    middle = 2 * n_send

    other_send, gp, g = first_products(returned, slope, w_out_t, ordered, n_send)
    core_send = shift_core(other_send, 1)
    own_send, other_keep = more_products(gp, g, ordered, [(n_send, middle), (middle, middle + n_keep)])
    core_keep = shift_core(other_keep, 1)
    main_send, c_send = add_rows(
        [own_send, core_send],
        [[(0, n_main, [(0, 0), (1, 0)])], [(0, nc_send, [(0, n_main), (1, n_main)])]],
    )
    main_send, c_send, gp = lax.optimization_barrier((main_send, c_send, gp))
    main_got = send_all(main_send, nx - 1, shift_first)
    c_got = send_all(c_send, near - 1, shift_near)
    c_cut, main_cut = nc_keep // far * (far - 1), main_keep // ny * (ny - 1)
    keeps = [c_cut, nc_keep - c_cut, main_cut, main_keep - main_cut]
    offsets = [int(low) for low in np.cumsum([0, *keeps])]
    (own_keep,) = more_products(gp, g, ordered, [(middle + n_keep, middle + 2 * n_keep)])

    def summed(k, got, low):
        terms = [(0, offsets[k]), (1, offsets[k]), *[(2 + i, low) for i in range(len(got))]]
        return [own_keep, core_keep, *got], [(0, keeps[k], terms)]

    def sums(*wanted):
        inputs, plans = [], []
        for sources, plan in wanted:
            plans.append([(at, rows, [(len(inputs) + i, low) for i, low in terms]) for at, rows, terms in plan])
            inputs.extend(sources)
        return add_rows(inputs, plans)

    c_send, main_send = sums(summed(0, c_got, 0), summed(2, main_got, 0))
    kept = [summed(1, c_got, c_cut), summed(3, main_got, main_cut)]
    c_got = send_all(c_send, far - 1, shift_far)
    main_got = send_all(main_send, ny - 1, shift_second)
    c_keep, main_keep = sums(*kept)

    def split_sums(keep, got, n):
        rows = keep.shape[0]
        cut = rows // n * (n - 1)
        sources = range(1 + len(got))
        return add_rows(
            [keep, *got],
            [[(0, cut, [(i, 0) for i in sources])], [(0, rows - cut, [(i, cut) for i in sources])]],
        )

    main_got, c_got = lax.optimization_barrier((main_got, c_got))
    rows = main_keep.shape[0]
    (joined,) = add_rows([main_keep, *main_got], [[(0, rows, [(i, 0) for i in range(1 + len(main_got))])]])
    across = lax.all_to_all(
        joined.reshape(nz, height - rc, joined.shape[1]), "member", split_axis=0, concat_axis=0, tiled=True
    )
    c_send, c_keep = split_sums(c_keep, c_got, nx)
    c_got = send_all(c_send, nx - 1, shift_first)
    c_send, c_keep = split_sums(c_keep, c_got, ny)
    c_got = send_all(c_send, ny - 1, shift_second)
    return tuple(finish(across, [c_keep, *c_got], width, channels))


def solution(mesh):
    in_specs = (
        P("member", "batch", "tile", None),
        P(),
        P(),
        P("batch", "tile", None),
        P("batch", "tile"),
        P("batch", "tile"),
    )
    out_specs = (P(("member", "tile", "batch"), None), P(("member", "tile", "batch"), None))
    return jax.shard_map(shards, mesh=mesh, in_specs=in_specs, out_specs=out_specs, check_vma=False)
```

```python
import functools

import jax
import jax.numpy as jnp
import numpy as np
from jax import lax
from jax.experimental import pallas as pl
from jax.experimental.pallas import tpu as pltpu
from jax.sharding import PartitionSpec as P

PATCH = 16
CORES = 2
LANES = 128
MIB = 1 << 20
NT = (((1,), (1,)), ((), ()))
WHOLE = pl.BlockSpec()
ANY = pl.BlockSpec(memory_space=pl.ANY)
FEW = 24
MOST = 56


def partner(z, k, nz):
    return z ^ k if nz & (nz - 1) == 0 else (z + k) % nz


def params(mib=24):
    return pltpu.CompilerParams(vmem_limit_bytes=int(mib * MIB))


def cost(flops, moved):
    return pl.CostEstimate(flops=int(flops), bytes_accessed=int(moved), transcendentals=0)


def packing(channels):
    spare = LANES - channels
    carriers = PATCH * channels // LANES
    per_cell = channels // spare
    assert carriers * LANES == PATCH * channels and per_cell * spare == channels
    return spare, carriers, per_cell


def pack(cell, channels):
    spare, carriers, per_cell = packing(channels)
    extra = [cell(j) for j in range(carriers, PATCH)]
    lane = lax.broadcasted_iota(jnp.int32, extra[0].shape, 1)
    rows = []
    for j in range(carriers):
        piece = extra[j // per_cell]
        moved = pltpu.roll(piece, channels - j % per_cell * spare, 1)
        rows.append(jnp.where(lane < channels, cell(j), moved))
    return rows


def unpack(rows, channels):
    spare, carriers, per_cell = packing(channels)
    lane = lax.broadcasted_iota(jnp.int32, rows[0].shape, 1)
    cells = list(rows)
    for first in range(0, carriers, per_cell):
        value = jnp.zeros_like(rows[0])
        for i in range(per_cell):
            moved = pltpu.roll(rows[first + i], (i * spare - channels) % LANES, 1)
            value = jnp.where((lane >= i * spare) & (lane < (i + 1) * spare), moved, value)
        cells.append(value)
    return cells


def in_hbm(value):
    return pltpu.with_memory_space_constraint(value, pltpu.HBM)


def column_steps(width):
    step = 256 if width % 256 == 0 else width
    return [slice(low, low + step) for low in range(0, width, step)]


def decode_body(pieces, latent_ref, w_in_ref, w_out_t_ref, *refs):
    out_refs, (rows, w_in, w_out_t, cells, row_sems, sems) = refs[:len(pieces)], refs[len(pieces):]
    count, block, _ = rows.shape
    channels = w_out_t.shape[0]
    share = out_refs[0].shape[1]
    half = max(count // 2, 1)
    me_z, nz = lax.axis_index("member"), lax.axis_size("member")
    row_copies = []
    for i, k in enumerate(pieces):
        start = pl.multiple_of(partner(me_z, k, nz) * block, block)
        row_copies.append(pltpu.make_async_copy(latent_ref.at[pl.ds(start, block)], rows.at[i], row_sems.at[i]))
    w_copies = [pltpu.make_async_copy(w_in_ref, w_in, sems.at[0]), pltpu.make_async_copy(w_out_t_ref, w_out_t, sems.at[1])]
    for copy in [*w_copies, *row_copies]:
        copy.start()
    for copy in [*w_copies, *row_copies[:half]]:
        copy.wait()
    for i in range(count):
        if i == half:
            for copy in row_copies[half:]:
                copy.wait()
        preact = jnp.dot(rows[i], w_in[...], preferred_element_type=jnp.float32)
        hidden = (preact / (1.0 + jnp.exp(-preact))).astype(jnp.bfloat16)
        cells[i, :, :channels] = lax.dot_general(hidden, w_out_t[...], NT, preferred_element_type=jnp.float32)
        for j, row in enumerate(pack(lambda j: cells[i, pl.ds(j, share, stride=PATCH), :], channels)):
            out_refs[i][j] = row


def decode(rows_in, w_in, w_out_t, parts, pieces):
    nrows, depth = rows_in.shape
    width = w_in.shape[1]
    channels = w_out_t.shape[0]
    block = nrows // parts
    share = block // PATCH
    carriers = packing(channels)[1]
    count = len(pieces)
    return pl.pallas_call(
        functools.partial(decode_body, tuple(pieces)),
        in_specs=[ANY] * 3,
        out_specs=[WHOLE] * count,
        out_shape=[jax.ShapeDtypeStruct((carriers, share, LANES), jnp.float32)] * count,
        scratch_shapes=[
            pltpu.VMEM((count, block, depth), jnp.bfloat16),
            pltpu.VMEM((depth, width), jnp.bfloat16),
            pltpu.VMEM((channels, width), jnp.bfloat16),
            pltpu.VMEM((count, block, LANES), jnp.float32),
            pltpu.SemaphoreType.DMA((count,)),
            pltpu.SemaphoreType.DMA((2,)),
        ],
        compiler_params=params(MOST),
        cost_estimate=cost(2 * nrows * width * (depth + channels), 5 * MIB),
        name="decode",
    )(rows_in, w_in, w_out_t)


def fill_choice(source_ref, choice):
    picked, extent = choice.shape
    for low in range(0, picked, LANES):
        high = min(low + LANES, picked)
        across = jnp.broadcast_to(source_ref[:, low:high], (LANES, high - low))
        down = jnp.transpose(across)
        for left in range(0, extent, LANES):
            here = lax.broadcasted_iota(jnp.int32, down.shape, 1) + left
            choice[low:high, left:left + LANES] = jnp.where(down == here, 1.0, 0.0).astype(jnp.bfloat16)


def slope_body(latent_ref, w_in_ref, slope_ref, hidden_ref):
    preact = jnp.dot(latent_ref[...], w_in_ref[...], preferred_element_type=jnp.float32)
    scale = 1.0 + jnp.exp(-preact)
    sigma = 1.0 / scale
    slope_ref[...] = sigma * (1.0 + preact * (1.0 - sigma))
    hidden_ref[...] = (preact / scale).astype(jnp.bfloat16)


def slopes(rows_in, w_in):
    nrows, depth = rows_in.shape
    width = w_in.shape[1]
    block = 256 if nrows % 256 == 0 else nrows
    return pl.pallas_call(
        slope_body,
        grid=(nrows // block,),
        in_specs=[pl.BlockSpec((block, depth), lambda i: (i, 0)), pl.BlockSpec((depth, width), lambda i: (0, 0))],
        out_specs=[pl.BlockSpec((block, width), lambda i: (i, 0)), pl.BlockSpec((block, width), lambda i: (i, 0))],
        out_shape=[
            jax.ShapeDtypeStruct((nrows, width), jnp.float32),
            jax.ShapeDtypeStruct((nrows, width), jnp.bfloat16),
        ],
        compiler_params=params(MOST),
        cost_estimate=cost(2 * nrows * width * depth, 4 * MIB),
        name="slopes",
    )(rows_in, w_in)


def order_body(source_ref, latent_ref, hidden_ref, out_ref, choice):
    @pl.when(pl.program_id(0) == 0)
    def _():
        fill_choice(source_ref, choice)

    for k, matrix_ref in enumerate((latent_ref, hidden_ref)):
        ordered = lax.dot_general(choice[...], matrix_ref[...], NT, preferred_element_type=jnp.float32)
        out_ref[k] = ordered.astype(jnp.bfloat16)


def ordered_transposes(source, latent, hidden):
    nrows, extent = latent.shape
    picked = source.shape[1]
    block = 256 if nrows % 256 == 0 else nrows
    return pl.pallas_call(
        order_body,
        grid=(nrows // block,),
        in_specs=[
            pl.BlockSpec((1, picked), lambda i: (0, 0)),
            pl.BlockSpec((block, extent), lambda i: (i, 0)),
            pl.BlockSpec((block, extent), lambda i: (i, 0)),
        ],
        out_specs=pl.BlockSpec((2, picked, block), lambda i: (0, 0, i)),
        out_shape=jax.ShapeDtypeStruct((2, picked, nrows), jnp.bfloat16),
        scratch_shapes=[pltpu.VMEM((picked, extent), jnp.bfloat16)],
        compiler_params=params(MOST),
        cost_estimate=cost(nrows * extent * picked, 4 * MIB),
        name="ordered_transposes",
    )(source, latent, hidden)


def target_body(channels, pool_ref, index_ref, target_ref):
    carriers, share, _ = target_ref.shape
    npool, total = pool_ref.shape
    choose = index_ref[...] == lax.broadcasted_iota(jnp.int32, (share, npool), 1)
    flat = jnp.dot(
        jnp.where(choose, 1.0, 0.0).astype(jnp.bfloat16), pool_ref[...], preferred_element_type=jnp.float32
    )

    def cell(j):
        start = j * channels
        low = start // LANES * LANES
        part = flat[:, low:min(low + 2 * LANES, total)]
        return pltpu.roll(part, (low - start) % part.shape[1], 1)[:, :LANES]

    for j, row in enumerate(pack(cell, channels)):
        target_ref[j] = row


def targets(pool, index, channels):
    share = index.shape[0]
    carriers = packing(channels)[1]
    return pl.pallas_call(
        functools.partial(target_body, channels),
        in_specs=[WHOLE] * 2,
        out_specs=WHOLE,
        out_shape=jax.ShapeDtypeStruct((carriers, share, LANES), jnp.float32),
        compiler_params=params(),
        cost_estimate=cost(2 * share * pool.size, 2 * pool.size),
        name="targets",
    )(pool, index)


def score_body(members, *refs):
    x_refs, (target_ref, count_ref), out_refs = refs[:members], refs[members:members + 2], refs[members + 2:]
    carriers = target_ref.shape[0]
    weight = count_ref[...].astype(jnp.float32)

    def inverse_norm(delta):
        squares = sum(d * d for d in delta)
        return 1.0 / jnp.sqrt(jnp.sum(squares, axis=-1, keepdims=True) + 1.0)

    target = [target_ref[j] for j in range(carriers)]
    xs = [[ref[j] for j in range(carriers)] for ref in x_refs]
    pair = [[jnp.zeros_like(target[0])] * carriers for _ in range(members)]
    for m in range(members):
        for k in range(m + 1, members):
            delta = [p - q for p, q in zip(xs[m], xs[k])]
            inverse = inverse_norm(delta)
            pair[m] = [p + d * inverse for p, d in zip(pair[m], delta)]
            pair[k] = [p - d * inverse for p, d in zip(pair[k], delta)]
    for m in range(members):
        delta = [p - q for p, q in zip(xs[m], target)]
        inverse = inverse_norm(delta)
        for j in range(carriers):
            out_refs[m][j] = weight * (delta[j] * inverse / members - pair[m][j] / (members * members))


def score(pieces, target, count):
    members = len(pieces)
    size = members * target.size
    return pl.pallas_call(
        functools.partial(score_body, members),
        in_specs=[WHOLE] * (members + 2),
        out_specs=[WHOLE] * members,
        out_shape=[jax.ShapeDtypeStruct(target.shape, jnp.float32)] * members,
        compiler_params=params(),
        cost_estimate=cost(30 * size, 8 * size),
        name="score",
    )(*pieces, target, count)


def first_body(parts, *refs):
    scored_refs, refs = refs[:parts], refs[parts:]
    slope_ref, w_out_t_ref, ordered_ref, result, gp, g, slope, w_out_t, latent_t, hidden_t, cells, in_sems, slope_sems = refs
    carriers, share, _ = scored_refs[0].shape
    channels, width = w_out_t.shape
    picked = result.shape[0]
    column = column_steps(width)
    w_copy, hidden_copy, latent_copy = copies = [
        pltpu.make_async_copy(source, target, in_sems.at[k])
        for k, (source, target) in enumerate([
            (w_out_t_ref, w_out_t),
            (ordered_ref.at[1, pl.ds(0, picked)], hidden_t),
            (ordered_ref.at[0, pl.ds(0, picked)], latent_t),
        ])
    ]
    slope_copies = [
        pltpu.make_async_copy(slope_ref.at[:, pl.ds(c.start, c.stop - c.start)], slope.at[:, c], slope_sems.at[k])
        for k, c in enumerate(column)
    ]
    for copy in [*copies, *slope_copies]:
        copy.start()

    me_z = lax.axis_index("member")
    for k, scored_ref in enumerate(scored_refs):
        base = partner(me_z, k, parts) * (share * PATCH)
        for j, value in enumerate(unpack([scored_ref[j] for j in range(carriers)], channels)):
            cells[pl.ds(base + j, share, stride=PATCH), :] = value
    lane = lax.broadcasted_iota(jnp.int32, cells.shape, 1)
    g[...] = jnp.where(lane < channels, cells[...], 0.0).astype(jnp.bfloat16)
    w_copy.wait()
    backward = [
        jnp.dot(g[:, :channels], w_out_t[:, c], preferred_element_type=jnp.float32) for c in column
    ]
    hidden_copy.wait()
    result[:, width:] = jnp.dot(hidden_t[...], g[...], preferred_element_type=jnp.float32)
    latent_copy.wait()
    for k, c in enumerate(column):
        slope_copies[k].wait()
        gp[:, c] = (backward[k] * slope[:, c]).astype(jnp.bfloat16)
        result[:, c] = jnp.dot(latent_t[...], gp[:, c], preferred_element_type=jnp.float32)


def first_products(scored, slope, w_out_t, ordered, picked):
    nrows, width = slope.shape
    channels = w_out_t.shape[0]
    steps = len(column_steps(width))
    return pl.pallas_call(
        functools.partial(first_body, len(scored)),
        in_specs=[*[WHOLE] * len(scored), ANY, ANY, ANY],
        out_specs=[WHOLE] * 3,
        out_shape=[
            jax.ShapeDtypeStruct((picked, width + LANES), jnp.float32),
            jax.ShapeDtypeStruct((nrows, width), jnp.bfloat16),
            jax.ShapeDtypeStruct((nrows, LANES), jnp.bfloat16),
        ],
        scratch_shapes=[
            pltpu.VMEM(slope.shape, jnp.float32),
            pltpu.VMEM(w_out_t.shape, jnp.bfloat16),
            pltpu.VMEM((picked, nrows), jnp.bfloat16),
            pltpu.VMEM((picked, nrows), jnp.bfloat16),
            pltpu.VMEM((nrows, LANES), jnp.float32),
            pltpu.SemaphoreType.DMA((3,)),
            pltpu.SemaphoreType.DMA((steps,)),
        ],
        compiler_params=params(FEW),
        cost_estimate=cost(2 * nrows * width * (channels + picked), 10 * MIB),
        name="first_products",
    )(*scored, in_hbm(slope), in_hbm(w_out_t), in_hbm(ordered))


def more_body(cuts, gp, g, ordered_ref, *refs):
    out_refs, (latent_t, hidden_t, in_sems) = refs[:len(cuts)], refs[len(cuts):]
    low, (picked, _) = cuts[0][0], latent_t.shape
    width = gp.shape[1]
    copies = [
        pltpu.make_async_copy(ordered_ref.at[k, pl.ds(low, picked)], target, in_sems.at[k])
        for k, target in enumerate((latent_t, hidden_t))
    ]
    for copy in copies:
        copy.start()

    def put(columns, product):
        for out_ref, (start, end) in zip(out_refs, cuts):
            out_ref[:, columns] = product[start - low:end - low]

    for copy in copies:
        copy.wait()
    for columns in column_steps(width):
        put(columns, jnp.dot(latent_t[...], gp[:, columns], preferred_element_type=jnp.float32))
    put(slice(width, None), jnp.dot(hidden_t[...], g[...], preferred_element_type=jnp.float32))


def more_products(gp, g, ordered, cuts):
    nrows, width = gp.shape
    picked = cuts[-1][1] - cuts[0][0]
    return pl.pallas_call(
        functools.partial(more_body, tuple(cuts)),
        in_specs=[WHOLE, WHOLE, ANY],
        out_specs=[WHOLE] * len(cuts),
        out_shape=[jax.ShapeDtypeStruct((end - start, width + LANES), jnp.float32) for start, end in cuts],
        scratch_shapes=[
            pltpu.VMEM((picked, nrows), jnp.bfloat16),
            pltpu.VMEM((picked, nrows), jnp.bfloat16),
            pltpu.SemaphoreType.DMA((2,)),
        ],
        compiler_params=params(FEW),
        cost_estimate=cost(2 * nrows * picked * width, 6 * MIB),
        name="more_products",
    )(gp, g, in_hbm(ordered))


def add_body(plans, count, *refs):
    inputs, outputs = refs[:count], refs[count:]
    for out_ref, plan in zip(outputs, plans):
        for at, rows, sources in plan:
            total = None
            for which, low in sources:
                value = inputs[which][low:low + rows]
                total = value if total is None else total + value
            out_ref[at:at + rows] = total


def add_rows(inputs, plans):
    columns = inputs[0].shape[1]
    sizes = [sum(rows for _, rows, _ in plan) for plan in plans]
    return pl.pallas_call(
        functools.partial(add_body, plans, len(inputs)),
        in_specs=[WHOLE] * len(inputs),
        out_specs=[WHOLE] * len(plans),
        out_shape=[jax.ShapeDtypeStruct((size, columns), jnp.float32) for size in sizes],
        compiler_params=params(),
        cost_estimate=cost(3 * sum(sizes) * columns, 12 * sum(sizes) * columns),
        name="add_rows",
    )(*inputs)


def finish_body(count, *refs):
    main_refs, rest_refs, (first_ref, second_ref) = refs[:count], refs[count:-2], refs[-2:]
    width, channels = first_ref.shape[1], second_ref.shape[1]
    rows = main_refs[0].shape[0]
    for low, high, refs in ((0, rows, main_refs), (rows, first_ref.shape[0], rest_refs)):
        total = refs[0][...]
        for ref in refs[1:]:
            total = total + ref[...]
        first_ref[low:high] = total[:, :width]
        second_ref[low:high] = total[:, width:width + channels]


def finish(main, rest, width, channels):
    height = main[0].shape[0] + rest[0].shape[0]
    return pl.pallas_call(
        functools.partial(finish_body, len(main)),
        in_specs=[WHOLE] * (len(main) + len(rest)),
        out_specs=[WHOLE] * 2,
        out_shape=[
            jax.ShapeDtypeStruct((height, width), jnp.float32),
            jax.ShapeDtypeStruct((height, channels), jnp.float32),
        ],
        compiler_params=params(),
        cost_estimate=cost(4 * height * width, 20 * height * width),
        name="finish",
    )(*main, *rest)


def row_order(nz, nx, nc, ny, height):
    near = 2 if nz % 2 == 0 else 1
    far = nz // near
    rc = max(height // 4, 1)
    main_rows, c_rows = range(height - rc), range(height - rc, height)
    first_last, second_last, far_last = [[*range(1, n), 0] for n in (nx, ny, far)]

    def main(firsts):
        return [(f, s, 0, 0, k, r) for f in firsts for s in second_last for k in reversed(range(nz)) for r in main_rows]

    def part_c(nears):
        return [(f, s, 1, o, n, r) for n in nears for o in far_last for f in first_last for s in second_last for r in c_rows]

    pieces = [main(range(1, nx)), part_c(range(1, near)), part_c([0]), main([0])]
    sizes = [len(piece) for piece in pieces]
    cores = [*range(1, nc), 0]
    halves = [[row for piece in part for row in piece] for part in (pieces[:2], pieces[2:])]
    table = np.array([(core, *row) for half in halves for core in cores for row in half], np.int32).T
    return table, sizes, near, far, rc


def shards(latent, w_in, w_out, observed, patch_index, counts):
    rows_in = latent[0, 0]
    nrows, depth = rows_in.shape
    width, channels = w_out.shape
    nz, nt, ny = (lax.axis_size(name) for name in ("member", "tile", "batch"))
    nc, nx = CORES, nt // CORES
    me_z, me_t, me_y = (lax.axis_index(name) for name in ("member", "tile", "batch"))
    me_x, me_c = me_t // nc, me_t % nc
    w_out_t = w_out.T
    height = depth // (nz * nt * ny)
    table, sizes, near, far, rc = row_order(nz, nx, nc, ny, height)
    turned = 1 if nx == ny else 0

    everywhere = [(z, x, c, y) for z in range(nz) for x in range(nx) for c in range(nc) for y in range(ny)]

    def shift(value, target):
        def number(z, x, c, y):
            return (z * nt + x * nc + c) * ny + y

        return lax.ppermute(
            value, ("member", "tile", "batch"), [(number(*place), number(*target(*place))) for place in everywhere]
        )

    def exchange(values):
        got = {k: shift(values[k], lambda z, x, c, y: (partner(z, k, nz), x, c, y)) for k in reversed(range(1, nz))}
        return [values[0], *[got[k] for k in range(1, nz)]]

    share = nrows // PATCH // nz
    far_first = [*reversed(range(nz))]
    packed = dict(zip(far_first, decode(rows_in, w_in, w_out_t, nz, far_first)))
    grouped = exchange(packed)

    core, first, second, relative, f, n, row = (jnp.asarray(table[k:k + 1]) for k in range(7))
    z_main = partner(me_z, n, nz)
    z_far = (f + me_z // near) % far * near + (n + me_z % near) % near
    z = z_main + relative * (z_far - z_main)
    core = (core + me_c) % nc
    turn = core * turned
    x, y = first + turn * (second - first), second + turn * (first - second)
    tile = (x + me_x) % nx * nc + core
    source = ((z * nt + tile) * ny + (y + me_y) % ny) * height + row
    slope, hidden = slopes(rows_in, w_in)
    index = lax.dynamic_slice_in_dim(patch_index[0], me_z * share, share, 0)[:, None]
    count = lax.dynamic_slice_in_dim(counts[0], me_z * share, share, 0)[:, None]
    target = targets(observed[0], index, channels)
    grouped, slope, hidden, source, target, count = lax.optimization_barrier(
        (grouped, slope, hidden, source, target, count)
    )

    scored = score(grouped, target, count)
    returned = exchange(scored)
    ordered = ordered_transposes(source, rows_in, hidden)
    returned, ordered = lax.optimization_barrier((returned, ordered))

    def shift_core(value, j):
        return shift(value, lambda z, x, c, y: (z, x, (c + j) % nc, y))

    def along(of_core):
        def shift_one(value, j):
            def target(z, x, c, y):
                return (z, (x + j) % nx, c, y) if of_core(c) == 0 else (z, x, c, (y + j) % ny)

            return shift(value, target)

        return shift_one

    shift_first, shift_second = along(lambda c: c * turned), along(lambda c: 1 - c * turned)

    def shift_near(value, j):
        return shift(value, lambda z, x, c, y: (z // near * near + (z + j) % near, x, c, y))

    def shift_far(value, j):
        return shift(value, lambda z, x, c, y: ((z // near + j) % far * near + z % near, x, c, y))

    def send_all(value, others, shift_one):
        if others == 1:
            return [shift_one(value, 1)]
        return [shift_one(v, j + 1) for j, v in enumerate(jnp.split(value, others, axis=0))] if others else []

    n_main, nc_send, nc_keep, main_keep = sizes
    n_send, n_keep = n_main + nc_send, nc_keep + main_keep
    middle = 2 * n_send

    other_send, gp, g = first_products(returned, slope, w_out_t, ordered, n_send)
    core_send = shift_core(other_send, 1)
    own_send, other_keep = more_products(gp, g, ordered, [(n_send, middle), (middle, middle + n_keep)])
    core_keep = shift_core(other_keep, 1)
    main_send, c_send = add_rows(
        [own_send, core_send],
        [[(0, n_main, [(0, 0), (1, 0)])], [(0, nc_send, [(0, n_main), (1, n_main)])]],
    )
    main_send, c_send, gp = lax.optimization_barrier((main_send, c_send, gp))
    main_got = send_all(main_send, nx - 1, shift_first)
    c_got = send_all(c_send, near - 1, shift_near)
    c_cut, main_cut = nc_keep // far * (far - 1), main_keep // ny * (ny - 1)
    keeps = [c_cut, nc_keep - c_cut, main_cut, main_keep - main_cut]
    offsets = [int(low) for low in np.cumsum([0, *keeps])]
    (own_keep,) = more_products(gp, g, ordered, [(middle + n_keep, middle + 2 * n_keep)])

    def summed(k, got, low):
        terms = [(0, offsets[k]), (1, offsets[k]), *[(2 + i, low) for i in range(len(got))]]
        return [own_keep, core_keep, *got], [(0, keeps[k], terms)]

    def sums(*wanted):
        inputs, plans = [], []
        for sources, plan in wanted:
            plans.append([(at, rows, [(len(inputs) + i, low) for i, low in terms]) for at, rows, terms in plan])
            inputs.extend(sources)
        return add_rows(inputs, plans)

    c_send, main_send = sums(summed(0, c_got, 0), summed(2, main_got, 0))
    kept = [summed(1, c_got, c_cut), summed(3, main_got, main_cut)]
    c_got = send_all(c_send, far - 1, shift_far)
    main_got = send_all(main_send, ny - 1, shift_second)
    c_keep, main_keep = sums(*kept)

    def split_sums(keep, got, n):
        rows = keep.shape[0]
        cut = rows // n * (n - 1)
        sources = range(1 + len(got))
        return add_rows(
            [keep, *got],
            [[(0, cut, [(i, 0) for i in sources])], [(0, rows - cut, [(i, cut) for i in sources])]],
        )

    main_got, c_got = lax.optimization_barrier((main_got, c_got))
    rows = main_keep.shape[0] // nz
    sources = range(1 + len(main_got))
    joined = add_rows(
        [main_keep, *main_got], [[(0, rows, [(i, k * rows) for i in sources])] for k in range(nz)]
    )
    main = exchange(joined[::-1])
    c_send, c_keep = split_sums(c_keep, c_got, nx)
    c_got = send_all(c_send, nx - 1, shift_first)
    c_send, c_keep = split_sums(c_keep, c_got, ny)
    c_got = send_all(c_send, ny - 1, shift_second)
    return tuple(finish(main, [c_keep, *c_got], width, channels))


def solution(mesh):
    in_specs = (
        P("member", "batch", "tile", None),
        P(),
        P(),
        P("batch", "tile", None),
        P("batch", "tile"),
        P("batch", "tile"),
    )
    out_specs = (P(("member", "tile", "batch"), None), P(("member", "tile", "batch"), None))
    return jax.shard_map(shards, mesh=mesh, in_specs=in_specs, out_specs=out_specs, check_vma=False)
```

```python
import functools

import jax
import jax.numpy as jnp
import numpy as np
from jax import lax
from jax.experimental import pallas as pl
from jax.experimental.pallas import tpu as pltpu
from jax.sharding import PartitionSpec as P

PATCH = 16
CORES = 2
LANES = 128
MIB = 1 << 20
NT = (((1,), (1,)), ((), ()))
WHOLE = pl.BlockSpec()
ANY = pl.BlockSpec(memory_space=pl.ANY)
FEW = 24
MOST = 56


def partner(z, k, nz):
    return z ^ k if nz & (nz - 1) == 0 else (z + k) % nz


def params(mib=24):
    return pltpu.CompilerParams(vmem_limit_bytes=int(mib * MIB))


def cost(flops, moved):
    return pl.CostEstimate(flops=int(flops), bytes_accessed=int(moved), transcendentals=0)


def packing(channels):
    spare = LANES - channels
    carriers = PATCH * channels // LANES
    per_cell = channels // spare
    assert carriers * LANES == PATCH * channels and per_cell * spare == channels
    return spare, carriers, per_cell


def pack(cell, channels):
    spare, carriers, per_cell = packing(channels)
    extra = [cell(j) for j in range(carriers, PATCH)]
    lane = lax.broadcasted_iota(jnp.int32, extra[0].shape, 1)
    rows = []
    for j in range(carriers):
        piece = extra[j // per_cell]
        moved = pltpu.roll(piece, channels - j % per_cell * spare, 1)
        rows.append(jnp.where(lane < channels, cell(j), moved))
    return rows


def unpack(rows, channels):
    spare, carriers, per_cell = packing(channels)
    lane = lax.broadcasted_iota(jnp.int32, rows[0].shape, 1)
    cells = list(rows)
    for first in range(0, carriers, per_cell):
        value = jnp.zeros_like(rows[0])
        for i in range(per_cell):
            moved = pltpu.roll(rows[first + i], (i * spare - channels) % LANES, 1)
            value = jnp.where((lane >= i * spare) & (lane < (i + 1) * spare), moved, value)
        cells.append(value)
    return cells


def in_hbm(value):
    return pltpu.with_memory_space_constraint(value, pltpu.HBM)


def column_steps(width):
    step = 256 if width % 256 == 0 else width
    return [slice(low, low + step) for low in range(0, width, step)]


def decode_body(pieces, latent_ref, w_in_ref, w_out_t_ref, *refs):
    out_refs, (rows, w_in, w_out_t, cells, row_sems, sems) = refs[:len(pieces)], refs[len(pieces):]
    count, block, _ = rows.shape
    channels = w_out_t.shape[0]
    share = out_refs[0].shape[1]
    half = max(count // 2, 1)
    me_z, nz = lax.axis_index("member"), lax.axis_size("member")
    row_copies = []
    for i, k in enumerate(pieces):
        start = pl.multiple_of(partner(me_z, k, nz) * block, block)
        row_copies.append(pltpu.make_async_copy(latent_ref.at[pl.ds(start, block)], rows.at[i], row_sems.at[i]))
    w_copies = [pltpu.make_async_copy(w_in_ref, w_in, sems.at[0]), pltpu.make_async_copy(w_out_t_ref, w_out_t, sems.at[1])]
    for copy in [*w_copies, *row_copies]:
        copy.start()
    for copy in [*w_copies, *row_copies[:half]]:
        copy.wait()
    for i in range(count):
        if i == half:
            for copy in row_copies[half:]:
                copy.wait()
        preact = jnp.dot(rows[i], w_in[...], preferred_element_type=jnp.float32)
        hidden = (preact / (1.0 + jnp.exp(-preact))).astype(jnp.bfloat16)
        cells[i, :, :channels] = lax.dot_general(hidden, w_out_t[...], NT, preferred_element_type=jnp.float32)
        for j, row in enumerate(pack(lambda j: cells[i, pl.ds(j, share, stride=PATCH), :], channels)):
            out_refs[i][j] = row


def decode(rows_in, w_in, w_out_t, parts, pieces):
    nrows, depth = rows_in.shape
    width = w_in.shape[1]
    channels = w_out_t.shape[0]
    block = nrows // parts
    share = block // PATCH
    carriers = packing(channels)[1]
    count = len(pieces)
    return pl.pallas_call(
        functools.partial(decode_body, tuple(pieces)),
        in_specs=[ANY] * 3,
        out_specs=[WHOLE] * count,
        out_shape=[jax.ShapeDtypeStruct((carriers, share, LANES), jnp.float32)] * count,
        scratch_shapes=[
            pltpu.VMEM((count, block, depth), jnp.bfloat16),
            pltpu.VMEM((depth, width), jnp.bfloat16),
            pltpu.VMEM((channels, width), jnp.bfloat16),
            pltpu.VMEM((count, block, LANES), jnp.float32),
            pltpu.SemaphoreType.DMA((count,)),
            pltpu.SemaphoreType.DMA((2,)),
        ],
        compiler_params=params(MOST),
        cost_estimate=cost(2 * nrows * width * (depth + channels), 5 * MIB),
        name="decode",
    )(rows_in, w_in, w_out_t)


def fill_choice(source, choice):
    picked, extent = choice.shape
    for low in range(0, picked, LANES):
        high = min(low + LANES, picked)
        across = jnp.broadcast_to(source[:, low:high], (LANES, high - low))
        down = jnp.transpose(across)
        for left in range(0, extent, LANES):
            here = lax.broadcasted_iota(jnp.int32, down.shape, 1) + left
            choice[low:high, left:left + LANES] = jnp.where(down == here, 1.0, 0.0).astype(jnp.bfloat16)


def slope_body(latent_ref, w_in_ref, slope_ref, hidden_ref):
    preact = jnp.dot(latent_ref[...], w_in_ref[...], preferred_element_type=jnp.float32)
    scale = 1.0 + jnp.exp(-preact)
    sigma = 1.0 / scale
    slope_ref[...] = sigma * (1.0 + preact * (1.0 - sigma))
    hidden_ref[...] = (preact / scale).astype(jnp.bfloat16)


def slopes(rows_in, w_in):
    nrows, depth = rows_in.shape
    width = w_in.shape[1]
    block = 256 if nrows % 256 == 0 else nrows
    return pl.pallas_call(
        slope_body,
        grid=(nrows // block,),
        in_specs=[pl.BlockSpec((block, depth), lambda i: (i, 0)), pl.BlockSpec((depth, width), lambda i: (0, 0))],
        out_specs=[pl.BlockSpec((block, width), lambda i: (i, 0)), pl.BlockSpec((block, width), lambda i: (i, 0))],
        out_shape=[
            jax.ShapeDtypeStruct((nrows, width), jnp.float32),
            jax.ShapeDtypeStruct((nrows, width), jnp.bfloat16),
        ],
        compiler_params=params(MOST),
        cost_estimate=cost(2 * nrows * width * depth, 4 * MIB),
        name="slopes",
    )(rows_in, w_in)


def order_body(source_of, table_ref, latent_ref, hidden_ref, out_ref, choice):
    @pl.when(pl.program_id(0) == 0)
    def _():
        fill_choice(source_of([table_ref[k:k + 1] for k in range(table_ref.shape[0])]), choice)

    for k, matrix_ref in enumerate((latent_ref, hidden_ref)):
        ordered = lax.dot_general(choice[...], matrix_ref[...], NT, preferred_element_type=jnp.float32)
        out_ref[k] = ordered.astype(jnp.bfloat16)


def ordered_transposes(table, source_of, latent, hidden):
    nrows, extent = latent.shape
    picked = table.shape[1]
    block = 256 if nrows % 256 == 0 else nrows
    return pl.pallas_call(
        functools.partial(order_body, source_of),
        grid=(nrows // block,),
        in_specs=[
            pl.BlockSpec(table.shape, lambda i: (0, 0)),
            pl.BlockSpec((block, extent), lambda i: (i, 0)),
            pl.BlockSpec((block, extent), lambda i: (i, 0)),
        ],
        out_specs=pl.BlockSpec((2, picked, block), lambda i: (0, 0, i)),
        out_shape=jax.ShapeDtypeStruct((2, picked, nrows), jnp.bfloat16),
        scratch_shapes=[pltpu.VMEM((picked, extent), jnp.bfloat16)],
        compiler_params=params(MOST),
        cost_estimate=cost(nrows * extent * picked, 4 * MIB),
        name="ordered_transposes",
    )(table, latent, hidden)


def target_body(channels, pool_ref, index_ref, count_ref, target_ref, weight_ref):
    carriers, share, _ = target_ref.shape
    npool, total = pool_ref.shape
    npatch = index_ref.shape[1]
    own = lax.broadcasted_iota(jnp.int32, (share, npatch), 0) + lax.axis_index("member") * share
    own = own == lax.broadcasted_iota(jnp.int32, (share, npatch), 1)
    index = jnp.sum(jnp.where(own, index_ref[...], 0), axis=1, keepdims=True)
    count = jnp.sum(jnp.where(own, count_ref[...], 0), axis=1, keepdims=True)
    weight_ref[...] = jnp.broadcast_to(count.astype(jnp.float32), weight_ref.shape)
    choose = index == lax.broadcasted_iota(jnp.int32, (share, npool), 1)
    flat = jnp.dot(
        jnp.where(choose, 1.0, 0.0).astype(jnp.bfloat16), pool_ref[...], preferred_element_type=jnp.float32
    )

    def cell(j):
        start = j * channels
        low = start // LANES * LANES
        part = flat[:, low:min(low + 2 * LANES, total)]
        return pltpu.roll(part, (low - start) % part.shape[1], 1)[:, :LANES]

    for j, row in enumerate(pack(cell, channels)):
        target_ref[j] = row


def targets(pool, index, count, share, channels):
    carriers = packing(channels)[1]
    return pl.pallas_call(
        functools.partial(target_body, channels),
        in_specs=[WHOLE] * 3,
        out_specs=[WHOLE] * 2,
        out_shape=[
            jax.ShapeDtypeStruct((carriers, share, LANES), jnp.float32),
            jax.ShapeDtypeStruct((share, LANES), jnp.float32),
        ],
        compiler_params=params(),
        cost_estimate=cost(2 * share * pool.size, 2 * pool.size),
        name="targets",
    )(pool, index, count)


def score_body(members, *refs):
    x_refs, (target_ref, weight_ref), out_refs = refs[:members], refs[members:members + 2], refs[members + 2:]
    carriers = target_ref.shape[0]
    weight = weight_ref[...]

    def inverse_norm(delta):
        squares = sum(d * d for d in delta)
        return 1.0 / jnp.sqrt(jnp.sum(squares, axis=-1, keepdims=True) + 1.0)

    target = [target_ref[j] for j in range(carriers)]
    xs = [[ref[j] for j in range(carriers)] for ref in x_refs]
    pair = [[jnp.zeros_like(target[0])] * carriers for _ in range(members)]
    for m in range(members):
        for k in range(m + 1, members):
            delta = [p - q for p, q in zip(xs[m], xs[k])]
            inverse = inverse_norm(delta)
            pair[m] = [p + d * inverse for p, d in zip(pair[m], delta)]
            pair[k] = [p - d * inverse for p, d in zip(pair[k], delta)]
    for m in range(members):
        delta = [p - q for p, q in zip(xs[m], target)]
        inverse = inverse_norm(delta)
        for j in range(carriers):
            out_refs[m][j] = weight * (delta[j] * inverse / members - pair[m][j] / (members * members))


def score(pieces, target, weight):
    members = len(pieces)
    size = members * target.size
    return pl.pallas_call(
        functools.partial(score_body, members),
        in_specs=[WHOLE] * (members + 2),
        out_specs=[WHOLE] * members,
        out_shape=[jax.ShapeDtypeStruct(target.shape, jnp.float32)] * members,
        compiler_params=params(),
        cost_estimate=cost(30 * size, 8 * size),
        name="score",
    )(*pieces, target, weight)


def first_body(parts, *refs):
    scored_refs, refs = refs[:parts], refs[parts:]
    slope_ref, w_out_t_ref, ordered_ref, result, gp, g, slope, w_out_t, latent_t, hidden_t, cells, in_sems, slope_sems = refs
    carriers, share, _ = scored_refs[0].shape
    channels, width = w_out_t.shape
    picked = result.shape[0]
    column = column_steps(width)
    w_copy, hidden_copy, latent_copy = copies = [
        pltpu.make_async_copy(source, target, in_sems.at[k])
        for k, (source, target) in enumerate([
            (w_out_t_ref, w_out_t),
            (ordered_ref.at[1, pl.ds(0, picked)], hidden_t),
            (ordered_ref.at[0, pl.ds(0, picked)], latent_t),
        ])
    ]
    slope_copies = [
        pltpu.make_async_copy(slope_ref.at[:, pl.ds(c.start, c.stop - c.start)], slope.at[:, c], slope_sems.at[k])
        for k, c in enumerate(column)
    ]
    for copy in [*copies, *slope_copies]:
        copy.start()

    me_z = lax.axis_index("member")
    for k, scored_ref in zip(reversed(range(parts)), scored_refs):
        base = partner(me_z, k, parts) * (share * PATCH)
        for j, value in enumerate(unpack([scored_ref[j] for j in range(carriers)], channels)):
            cells[pl.ds(base + j, share, stride=PATCH), :] = value
    lane = lax.broadcasted_iota(jnp.int32, cells.shape, 1)
    g[...] = jnp.where(lane < channels, cells[...], 0.0).astype(jnp.bfloat16)
    w_copy.wait()
    backward = [
        jnp.dot(g[:, :channels], w_out_t[:, c], preferred_element_type=jnp.float32) for c in column
    ]
    hidden_copy.wait()
    result[:, width:] = jnp.dot(hidden_t[...], g[...], preferred_element_type=jnp.float32)
    latent_copy.wait()
    for k, c in enumerate(column):
        slope_copies[k].wait()
        gp[:, c] = (backward[k] * slope[:, c]).astype(jnp.bfloat16)
        result[:, c] = jnp.dot(latent_t[...], gp[:, c], preferred_element_type=jnp.float32)


def first_products(scored, slope, w_out_t, ordered, picked):
    nrows, width = slope.shape
    channels = w_out_t.shape[0]
    steps = len(column_steps(width))
    return pl.pallas_call(
        functools.partial(first_body, len(scored)),
        in_specs=[*[WHOLE] * len(scored), ANY, ANY, ANY],
        out_specs=[WHOLE] * 3,
        out_shape=[
            jax.ShapeDtypeStruct((picked, width + LANES), jnp.float32),
            jax.ShapeDtypeStruct((nrows, width), jnp.bfloat16),
            jax.ShapeDtypeStruct((nrows, LANES), jnp.bfloat16),
        ],
        scratch_shapes=[
            pltpu.VMEM(slope.shape, jnp.float32),
            pltpu.VMEM(w_out_t.shape, jnp.bfloat16),
            pltpu.VMEM((picked, nrows), jnp.bfloat16),
            pltpu.VMEM((picked, nrows), jnp.bfloat16),
            pltpu.VMEM((nrows, LANES), jnp.float32),
            pltpu.SemaphoreType.DMA((3,)),
            pltpu.SemaphoreType.DMA((steps,)),
        ],
        compiler_params=params(FEW),
        cost_estimate=cost(2 * nrows * width * (channels + picked), 10 * MIB),
        name="first_products",
    )(*scored, in_hbm(slope), in_hbm(w_out_t), in_hbm(ordered))


def more_body(cuts, gp, g, ordered_ref, *refs):
    out_refs, (latent_t, hidden_t, in_sems) = refs[:len(cuts)], refs[len(cuts):]
    low, (picked, _) = cuts[0][0], latent_t.shape
    width = gp.shape[1]
    copies = [
        pltpu.make_async_copy(ordered_ref.at[k, pl.ds(low, picked)], target, in_sems.at[k])
        for k, target in enumerate((latent_t, hidden_t))
    ]
    for copy in copies:
        copy.start()

    def put(columns, product):
        for out_ref, (start, end) in zip(out_refs, cuts):
            out_ref[:, columns] = product[start - low:end - low]

    for copy in copies:
        copy.wait()
    for columns in column_steps(width):
        put(columns, jnp.dot(latent_t[...], gp[:, columns], preferred_element_type=jnp.float32))
    put(slice(width, None), jnp.dot(hidden_t[...], g[...], preferred_element_type=jnp.float32))


def more_products(gp, g, ordered, cuts):
    nrows, width = gp.shape
    picked = cuts[-1][1] - cuts[0][0]
    return pl.pallas_call(
        functools.partial(more_body, tuple(cuts)),
        in_specs=[WHOLE, WHOLE, ANY],
        out_specs=[WHOLE] * len(cuts),
        out_shape=[jax.ShapeDtypeStruct((end - start, width + LANES), jnp.float32) for start, end in cuts],
        scratch_shapes=[
            pltpu.VMEM((picked, nrows), jnp.bfloat16),
            pltpu.VMEM((picked, nrows), jnp.bfloat16),
            pltpu.SemaphoreType.DMA((2,)),
        ],
        compiler_params=params(FEW),
        cost_estimate=cost(2 * nrows * picked * width, 6 * MIB),
        name="more_products",
    )(gp, g, in_hbm(ordered))


def add_body(plans, count, *refs):
    inputs, outputs = refs[:count], refs[count:]
    for out_ref, plan in zip(outputs, plans):
        for at, rows, sources in plan:
            total = None
            for which, low in sources:
                value = inputs[which][low:low + rows]
                total = value if total is None else total + value
            out_ref[at:at + rows] = total


def add_rows(inputs, plans):
    columns = inputs[0].shape[1]
    sizes = [sum(rows for _, rows, _ in plan) for plan in plans]
    return pl.pallas_call(
        functools.partial(add_body, plans, len(inputs)),
        in_specs=[WHOLE] * len(inputs),
        out_specs=[WHOLE] * len(plans),
        out_shape=[jax.ShapeDtypeStruct((size, columns), jnp.float32) for size in sizes],
        compiler_params=params(),
        cost_estimate=cost(3 * sum(sizes) * columns, 12 * sum(sizes) * columns),
        name="add_rows",
    )(*inputs)


def finish_body(*refs):
    *parts, first_ref, second_ref = refs
    width, channels = first_ref.shape[1], second_ref.shape[1]
    total = parts[0][...]
    for ref in parts[1:]:
        total = total + ref[...]
    first_ref[...] = total[:, :width]
    second_ref[...] = total[:, width:width + channels]


def finish(parts, width, channels):
    height = parts[0].shape[0]
    return pl.pallas_call(
        finish_body,
        in_specs=[WHOLE] * len(parts),
        out_specs=[WHOLE] * 2,
        out_shape=[
            jax.ShapeDtypeStruct((height, width), jnp.float32),
            jax.ShapeDtypeStruct((height, channels), jnp.float32),
        ],
        compiler_params=params(),
        cost_estimate=cost(4 * height * width, 20 * height * width),
        name="finish",
    )(*parts)


def row_order(nz, nx, nc, ny, height):
    first_last, second_last = [[*range(1, n), 0] for n in (nx, ny)]
    z_last = [*reversed(range(nz))]
    step = max(nz // 4, 1)
    chunks = [z_last[low:low + step] for low in range(0, nz, step)]

    def part(firsts, ks):
        return [(f, s, k, r) for f in firsts for s in second_last for k in ks for r in range(height)]

    halves = [[part(firsts, ks) for ks in chunks] for firsts in (first_last[:-1], [0])]
    table = np.array(
        [(core, *row) for half in halves for core in [*range(1, nc), 0] for piece in half for row in piece], np.int32
    ).T
    sent, kept = [[len(piece) for piece in half] for half in halves]
    return table, chunks, sent, kept


def shards(latent, w_in, w_out, observed, patch_index, counts):
    rows_in = latent[0, 0]
    nrows, depth = rows_in.shape
    width, channels = w_out.shape
    nz, nt, ny = (lax.axis_size(name) for name in ("member", "tile", "batch"))
    nc, nx = CORES, nt // CORES
    w_out_t = w_out.T
    height = depth // (nz * nt * ny)
    table, chunks, sent, kept = row_order(nz, nx, nc, ny, height)
    turned = 1 if nx == ny else 0

    far_first = [*reversed(range(nz))]
    everywhere = [(z, x, c, y) for z in range(nz) for x in range(nx) for c in range(nc) for y in range(ny)]

    def shift(value, target):
        def number(z, x, c, y):
            return (z * nt + x * nc + c) * ny + y

        return lax.ppermute(
            value, ("member", "tile", "batch"), [(number(*place), number(*target(*place))) for place in everywhere]
        )

    def send_to(value, k):
        return shift(value, lambda z, x, c, y: (partner(z, k, nz), x, c, y))

    def exchange(values):
        return [send_to(values[k], k) if k else values[0] for k in far_first]

    def shift_core(value, j):
        return shift(value, lambda z, x, c, y: (z, x, (c + j) % nc, y))

    def along(of_core):
        def shift_one(value, j):
            def target(z, x, c, y):
                return (z, (x + j) % nx, c, y) if of_core(c) == 0 else (z, x, c, (y + j) % ny)

            return shift(value, target)

        return shift_one

    shift_first, shift_second = along(lambda c: c * turned), along(lambda c: 1 - c * turned)

    def send_all(value, others, shift_one):
        if others == 1:
            return [shift_one(value, 1)]
        return [shift_one(v, j + 1) for j, v in enumerate(jnp.split(value, others, axis=0))] if others else []

    share = nrows // PATCH // nz
    packed = dict(zip(far_first, decode(rows_in, w_in, w_out_t, nz, far_first)))
    grouped = exchange(packed)

    def source_of(columns):
        me_z, me_t, me_y = (lax.axis_index(name) for name in ("member", "tile", "batch"))
        core, first, second, k, row = columns[:5]
        z = partner(me_z, k, nz)
        core = lax.rem(core + lax.rem(me_t, nc), nc)
        turn = core * turned
        x, y = first + turn * (second - first), second + turn * (first - second)
        tile = lax.rem(x + me_t // nc, nx) * nc + core
        return ((z * nt + tile) * ny + lax.rem(y + me_y, ny)) * height + row

    table = np.concatenate([table, np.zeros((-len(table) % 8, table.shape[1]), np.int32)])
    n_send, n_keep = sum(sent), sum(kept)
    middle = 2 * n_send

    slope, hidden = slopes(rows_in, w_in)
    target, weight = targets(observed[0], patch_index, counts, share, channels)
    grouped, slope, hidden, target, weight = lax.optimization_barrier((grouped, slope, hidden, target, weight))

    scored = score(grouped, target, weight)
    returned = exchange(dict(zip(far_first, scored)))
    ordered = ordered_transposes(table, source_of, rows_in, hidden)
    returned, ordered = lax.optimization_barrier((returned, ordered))

    other_send, gp, g = first_products(returned, slope, w_out_t, ordered, n_send)
    core_send = shift_core(other_send, 1)
    own_send, other_keep = more_products(gp, g, ordered, [(n_send, middle), (middle, middle + n_keep)])
    core_keep = shift_core(other_keep, 1)

    def added(inputs, pieces):
        return list(add_rows(inputs, [[(0, rows, [(i, low) for i in range(len(inputs))])] for low, rows in pieces]))

    def pieces_of(sizes, low=0):
        return [(low + int(at), size) for at, size in zip(np.cumsum([0, *sizes[:-1]]), sizes)]

    first_sends = added([own_send, core_send], pieces_of(sent))
    first_sends, gp = lax.optimization_barrier((first_sends, gp))
    first_got = [send_all(value, nx - 1, shift_first) for value in first_sends]
    (own_keep,) = more_products(gp, g, ordered, [(middle + n_keep, middle + 2 * n_keep)])

    joined, early = {}, {}
    for ks, (low, size), got in zip(chunks, pieces_of(kept), first_got):
        if ks == chunks[-1] and len(chunks) > 1:
            early[far_first[0]] = send_to(joined[far_first[0]], far_first[0])
            got, early[far_first[0]] = lax.optimization_barrier((got, early[far_first[0]]))
        cut = size // ny * (ny - 1)
        terms = [(0, low), (1, low), *[(2 + i, 0) for i in range(len(got))]]
        second_send, second_keep = add_rows(
            [own_keep, core_keep, *got],
            [[(0, rows, [(i, start + at) for i, start in terms])] for at, rows in ((0, cut), (cut, size - cut))],
        )
        got = send_all(second_send, ny - 1, shift_second)
        joined.update(zip(ks, added([second_keep, *got], pieces_of([height] * len(ks)))))
    parts = [early[k] if k in early else send_to(joined[k], k) if k else joined[k] for k in far_first]
    return tuple(finish(parts, width, channels))


def solution(mesh):
    in_specs = (
        P("member", "batch", "tile", None),
        P(),
        P(),
        P("batch", "tile", None),
        P("batch", "tile"),
        P("batch", "tile"),
    )
    out_specs = (P(("member", "tile", "batch"), None), P(("member", "tile", "batch"), None))
    return jax.shard_map(shards, mesh=mesh, in_specs=in_specs, out_specs=out_specs, check_vma=False)
```

```python
import functools

import jax
import jax.numpy as jnp
import numpy as np
from jax import lax
from jax.experimental import pallas as pl
from jax.experimental.pallas import tpu as pltpu
from jax.sharding import PartitionSpec as P

PATCH = 16
CORES = 2
LANES = 128
MIB = 1 << 20
NT = (((1,), (1,)), ((), ()))
WHOLE = pl.BlockSpec()
ANY = pl.BlockSpec(memory_space=pl.ANY)
FEW = 24
MOST = 56


def partner(z, k, nz):
    return z ^ k if nz & (nz - 1) == 0 else (z + k) % nz


def params(mib=24):
    return pltpu.CompilerParams(vmem_limit_bytes=int(mib * MIB))


def cost(flops, moved):
    return pl.CostEstimate(flops=int(flops), bytes_accessed=int(moved), transcendentals=0)


def packing(channels):
    spare = LANES - channels
    carriers = PATCH * channels // LANES
    per_cell = channels // spare
    assert carriers * LANES == PATCH * channels and per_cell * spare == channels
    return spare, carriers, per_cell


def pack(cell, channels):
    spare, carriers, per_cell = packing(channels)
    extra = [cell(j) for j in range(carriers, PATCH)]
    lane = lax.broadcasted_iota(jnp.int32, extra[0].shape, 1)
    rows = []
    for j in range(carriers):
        piece = extra[j // per_cell]
        moved = pltpu.roll(piece, channels - j % per_cell * spare, 1)
        rows.append(jnp.where(lane < channels, cell(j), moved))
    return rows


def unpack(rows, channels):
    spare, carriers, per_cell = packing(channels)
    lane = lax.broadcasted_iota(jnp.int32, rows[0].shape, 1)
    cells = list(rows)
    for first in range(0, carriers, per_cell):
        value = jnp.zeros_like(rows[0])
        for i in range(per_cell):
            moved = pltpu.roll(rows[first + i], (i * spare - channels) % LANES, 1)
            value = jnp.where((lane >= i * spare) & (lane < (i + 1) * spare), moved, value)
        cells.append(value)
    return cells


def in_hbm(value):
    return pltpu.with_memory_space_constraint(value, pltpu.HBM)


def column_steps(width):
    step = 256 if width % 256 == 0 else width
    return [slice(low, low + step) for low in range(0, width, step)]


def decode_body(pieces, latent_ref, w_in_ref, w_out_t_ref, *refs):
    out_refs, (rows, w_in, w_out_t, cells, row_sems, sems) = refs[:len(pieces)], refs[len(pieces):]
    count, block, _ = rows.shape
    channels = w_out_t.shape[0]
    share = out_refs[0].shape[1]
    half = max(count // 2, 1)
    me_z, nz = lax.axis_index("member"), lax.axis_size("member")
    row_copies = []
    for i, k in enumerate(pieces):
        start = pl.multiple_of(partner(me_z, k, nz) * block, block)
        row_copies.append(pltpu.make_async_copy(latent_ref.at[pl.ds(start, block)], rows.at[i], row_sems.at[i]))
    w_copies = [pltpu.make_async_copy(w_in_ref, w_in, sems.at[0]), pltpu.make_async_copy(w_out_t_ref, w_out_t, sems.at[1])]
    for copy in [*w_copies, *row_copies]:
        copy.start()
    for copy in [*w_copies, *row_copies[:half]]:
        copy.wait()
    for i in range(count):
        if i == half:
            for copy in row_copies[half:]:
                copy.wait()
        preact = jnp.dot(rows[i], w_in[...], preferred_element_type=jnp.float32)
        hidden = (preact / (1.0 + jnp.exp(-preact))).astype(jnp.bfloat16)
        cells[i, :, :channels] = lax.dot_general(hidden, w_out_t[...], NT, preferred_element_type=jnp.float32)
        for j, row in enumerate(pack(lambda j: cells[i, pl.ds(j, share, stride=PATCH), :], channels)):
            out_refs[i][j] = row


def decode(rows_in, w_in, w_out_t, parts, pieces):
    nrows, depth = rows_in.shape
    width = w_in.shape[1]
    channels = w_out_t.shape[0]
    block = nrows // parts
    share = block // PATCH
    carriers = packing(channels)[1]
    count = len(pieces)
    return pl.pallas_call(
        functools.partial(decode_body, tuple(pieces)),
        in_specs=[ANY] * 3,
        out_specs=[WHOLE] * count,
        out_shape=[jax.ShapeDtypeStruct((carriers, share, LANES), jnp.float32)] * count,
        scratch_shapes=[
            pltpu.VMEM((count, block, depth), jnp.bfloat16),
            pltpu.VMEM((depth, width), jnp.bfloat16),
            pltpu.VMEM((channels, width), jnp.bfloat16),
            pltpu.VMEM((count, block, LANES), jnp.float32),
            pltpu.SemaphoreType.DMA((count,)),
            pltpu.SemaphoreType.DMA((2,)),
        ],
        compiler_params=params(MOST),
        cost_estimate=cost(2 * nrows * width * (depth + channels), 5 * MIB),
        name="decode",
    )(rows_in, w_in, w_out_t)


def fill_choice(source, choice):
    picked, extent = choice.shape
    for low in range(0, picked, LANES):
        high = min(low + LANES, picked)
        across = jnp.broadcast_to(source[:, low:high], (LANES, high - low))
        down = jnp.transpose(across)
        for left in range(0, extent, LANES):
            here = lax.broadcasted_iota(jnp.int32, down.shape, 1) + left
            choice[low:high, left:left + LANES] = jnp.where(down == here, 1.0, 0.0).astype(jnp.bfloat16)


def slope_body(latent_ref, w_in_ref, slope_ref, hidden_ref):
    preact = jnp.dot(latent_ref[...], w_in_ref[...], preferred_element_type=jnp.float32)
    scale = 1.0 + jnp.exp(-preact)
    sigma = 1.0 / scale
    slope_ref[...] = sigma * (1.0 + preact * (1.0 - sigma))
    hidden_ref[...] = (preact / scale).astype(jnp.bfloat16)


def slopes(rows_in, w_in):
    nrows, depth = rows_in.shape
    width = w_in.shape[1]
    block = 256 if nrows % 256 == 0 else nrows
    return pl.pallas_call(
        slope_body,
        grid=(nrows // block,),
        in_specs=[pl.BlockSpec((block, depth), lambda i: (i, 0)), pl.BlockSpec((depth, width), lambda i: (0, 0))],
        out_specs=[pl.BlockSpec((block, width), lambda i: (i, 0)), pl.BlockSpec((block, width), lambda i: (i, 0))],
        out_shape=[
            jax.ShapeDtypeStruct((nrows, width), jnp.float32),
            jax.ShapeDtypeStruct((nrows, width), jnp.bfloat16),
        ],
        compiler_params=params(FEW),
        cost_estimate=cost(2 * nrows * width * depth, 4 * MIB),
        name="slopes",
    )(in_hbm(rows_in), in_hbm(w_in))


def order_body(source_of, table_ref, latent_ref, hidden_ref, out_ref, choice):
    @pl.when(pl.program_id(0) == 0)
    def _():
        fill_choice(source_of([table_ref[k:k + 1] for k in range(table_ref.shape[0])]), choice)

    for k, matrix_ref in enumerate((latent_ref, hidden_ref)):
        ordered = lax.dot_general(choice[...], matrix_ref[...], NT, preferred_element_type=jnp.float32)
        out_ref[k] = ordered.astype(jnp.bfloat16)


def ordered_transposes(table, source_of, latent, hidden):
    nrows, extent = latent.shape
    picked = table.shape[1]
    block = 256 if nrows % 256 == 0 else nrows
    return pl.pallas_call(
        functools.partial(order_body, source_of),
        grid=(nrows // block,),
        in_specs=[
            pl.BlockSpec(table.shape, lambda i: (0, 0)),
            pl.BlockSpec((block, extent), lambda i: (i, 0)),
            pl.BlockSpec((block, extent), lambda i: (i, 0)),
        ],
        out_specs=pl.BlockSpec((2, picked, block), lambda i: (0, 0, i)),
        out_shape=jax.ShapeDtypeStruct((2, picked, nrows), jnp.bfloat16),
        scratch_shapes=[pltpu.VMEM((picked, extent), jnp.bfloat16)],
        compiler_params=params(FEW),
        cost_estimate=cost(nrows * extent * picked, 4 * MIB),
        name="ordered_transposes",
    )(table, in_hbm(latent), hidden)


def target_body(channels, pool_ref, index_ref, count_ref, target_ref, weight_ref):
    carriers, share, _ = target_ref.shape
    npool, total = pool_ref.shape
    npatch = index_ref.shape[1]
    own = lax.broadcasted_iota(jnp.int32, (share, npatch), 0) + lax.axis_index("member") * share
    own = own == lax.broadcasted_iota(jnp.int32, (share, npatch), 1)
    index = jnp.sum(jnp.where(own, index_ref[...], 0), axis=1, keepdims=True)
    count = jnp.sum(jnp.where(own, count_ref[...], 0), axis=1, keepdims=True)
    weight_ref[...] = jnp.broadcast_to(count.astype(jnp.float32), weight_ref.shape)
    choose = index == lax.broadcasted_iota(jnp.int32, (share, npool), 1)
    flat = jnp.dot(
        jnp.where(choose, 1.0, 0.0).astype(jnp.bfloat16), pool_ref[...], preferred_element_type=jnp.float32
    )

    def cell(j):
        start = j * channels
        low = start // LANES * LANES
        part = flat[:, low:min(low + 2 * LANES, total)]
        return pltpu.roll(part, (low - start) % part.shape[1], 1)[:, :LANES]

    for j, row in enumerate(pack(cell, channels)):
        target_ref[j] = row


def targets(pool, index, count, share, channels):
    carriers = packing(channels)[1]
    return pl.pallas_call(
        functools.partial(target_body, channels),
        in_specs=[WHOLE] * 3,
        out_specs=[WHOLE] * 2,
        out_shape=[
            jax.ShapeDtypeStruct((carriers, share, LANES), jnp.float32),
            jax.ShapeDtypeStruct((share, LANES), jnp.float32),
        ],
        compiler_params=params(),
        cost_estimate=cost(2 * share * pool.size, 2 * pool.size),
        name="targets",
    )(pool, index, count)


def score_body(members, *refs):
    x_refs, (target_ref, weight_ref), out_refs = refs[:members], refs[members:members + 2], refs[members + 2:]
    carriers = target_ref.shape[0]
    weight = weight_ref[...]

    def inverse_norm(delta):
        squares = sum(d * d for d in delta)
        return 1.0 / jnp.sqrt(jnp.sum(squares, axis=-1, keepdims=True) + 1.0)

    target = [target_ref[j] for j in range(carriers)]
    xs = [[ref[j] for j in range(carriers)] for ref in x_refs]
    pair = [[jnp.zeros_like(target[0])] * carriers for _ in range(members)]
    for m in range(members):
        for k in range(m + 1, members):
            delta = [p - q for p, q in zip(xs[m], xs[k])]
            inverse = inverse_norm(delta)
            pair[m] = [p + d * inverse for p, d in zip(pair[m], delta)]
            pair[k] = [p - d * inverse for p, d in zip(pair[k], delta)]
    for m in range(members):
        delta = [p - q for p, q in zip(xs[m], target)]
        inverse = inverse_norm(delta)
        for j in range(carriers):
            out_refs[m][j] = weight * (delta[j] * inverse / members - pair[m][j] / (members * members))


def score(pieces, target, weight):
    members = len(pieces)
    size = members * target.size
    return pl.pallas_call(
        functools.partial(score_body, members),
        in_specs=[WHOLE] * (members + 2),
        out_specs=[WHOLE] * members,
        out_shape=[jax.ShapeDtypeStruct(target.shape, jnp.float32)] * members,
        compiler_params=params(),
        cost_estimate=cost(30 * size, 8 * size),
        name="score",
    )(*pieces, target, weight)


def first_body(parts, *refs):
    scored_refs, (slope, w_out_t, ordered, result, gp, g, cells) = refs[:parts], refs[parts:]
    carriers, share, _ = scored_refs[0].shape
    channels, width = w_out_t.shape
    picked = result.shape[0]
    me_z = lax.axis_index("member")
    for k, scored_ref in zip(reversed(range(parts)), scored_refs):
        base = partner(me_z, k, parts) * (share * PATCH)
        for j, value in enumerate(unpack([scored_ref[j] for j in range(carriers)], channels)):
            cells[pl.ds(base + j, share, stride=PATCH), :] = value
    lane = lax.broadcasted_iota(jnp.int32, cells.shape, 1)
    g[...] = jnp.where(lane < channels, cells[...], 0.0).astype(jnp.bfloat16)
    result[:, width:] = jnp.dot(ordered[1, :picked], g[...], preferred_element_type=jnp.float32)
    for c in column_steps(width):
        backward = jnp.dot(g[:, :channels], w_out_t[:, c], preferred_element_type=jnp.float32)
        gp[:, c] = (backward * slope[:, c]).astype(jnp.bfloat16)
        result[:, c] = jnp.dot(ordered[0, :picked], gp[:, c], preferred_element_type=jnp.float32)


def first_products(scored, slope, w_out_t, ordered, picked):
    nrows, width = slope.shape
    channels = w_out_t.shape[0]
    return pl.pallas_call(
        functools.partial(first_body, len(scored)),
        in_specs=[WHOLE] * (len(scored) + 3),
        out_specs=[WHOLE] * 3,
        out_shape=[
            jax.ShapeDtypeStruct((picked, width + LANES), jnp.float32),
            jax.ShapeDtypeStruct((nrows, width), jnp.bfloat16),
            jax.ShapeDtypeStruct((nrows, LANES), jnp.bfloat16),
        ],
        scratch_shapes=[pltpu.VMEM((nrows, LANES), jnp.float32)],
        compiler_params=params(FEW),
        cost_estimate=cost(2 * nrows * width * (channels + picked), 10 * MIB),
        name="first_products",
    )(*scored, slope, w_out_t, ordered)


def more_body(cuts, gp, g, ordered, *out_refs):
    low, high = cuts[0][0], cuts[-1][1]
    width = gp.shape[1]

    def put(columns, product):
        for out_ref, (start, end) in zip(out_refs, cuts):
            out_ref[:, columns] = product[start - low:end - low]

    for columns in column_steps(width):
        put(columns, jnp.dot(ordered[0, low:high], gp[:, columns], preferred_element_type=jnp.float32))
    put(slice(width, None), jnp.dot(ordered[1, low:high], g[...], preferred_element_type=jnp.float32))


def more_products(gp, g, ordered, cuts):
    nrows, width = gp.shape
    picked = cuts[-1][1] - cuts[0][0]
    return pl.pallas_call(
        functools.partial(more_body, tuple(cuts)),
        in_specs=[WHOLE] * 3,
        out_specs=[WHOLE] * len(cuts),
        out_shape=[jax.ShapeDtypeStruct((end - start, width + LANES), jnp.float32) for start, end in cuts],
        compiler_params=params(FEW),
        cost_estimate=cost(2 * nrows * picked * width, 6 * MIB),
        name="more_products",
    )(gp, g, ordered)


def add_body(plans, count, *refs):
    inputs, outputs = refs[:count], refs[count:]
    for out_ref, plan in zip(outputs, plans):
        for at, rows, sources in plan:
            total = None
            for which, low in sources:
                value = inputs[which][low:low + rows]
                total = value if total is None else total + value
            out_ref[at:at + rows] = total


def add_rows(inputs, plans, flops=0):
    columns = inputs[0].shape[1]
    sizes = [sum(rows for _, rows, _ in plan) for plan in plans]
    return pl.pallas_call(
        functools.partial(add_body, plans, len(inputs)),
        in_specs=[WHOLE] * len(inputs),
        out_specs=[WHOLE] * len(plans),
        out_shape=[jax.ShapeDtypeStruct((size, columns), jnp.float32) for size in sizes],
        compiler_params=params(),
        cost_estimate=cost(flops or 3 * sum(sizes) * columns, 12 * sum(sizes) * columns),
        name="add_rows",
    )(*inputs)


def finish_body(*refs):
    *parts, first_ref, second_ref = refs
    width, channels = first_ref.shape[1], second_ref.shape[1]
    total = parts[0][...]
    for ref in parts[1:]:
        total = total + ref[...]
    first_ref[...] = total[:, :width]
    second_ref[...] = total[:, width:width + channels]


def finish(parts, width, channels):
    height = parts[0].shape[0]
    return pl.pallas_call(
        finish_body,
        in_specs=[WHOLE] * len(parts),
        out_specs=[WHOLE] * 2,
        out_shape=[
            jax.ShapeDtypeStruct((height, width), jnp.float32),
            jax.ShapeDtypeStruct((height, channels), jnp.float32),
        ],
        compiler_params=params(),
        cost_estimate=cost(4 * height * width, 20 * height * width),
        name="finish",
    )(*parts)


def row_order(nz, nx, nc, ny, height):
    first_last, second_last = [[*range(1, n), 0] for n in (nx, ny)]
    z_last = [*reversed(range(nz))]
    by_neighbour = nz > 1 and nz & (nz - 1) == 0
    far = [k for k in z_last if k > 1] if by_neighbour else z_last
    chunks = [ks for ks in ([k for k in far if k % 2], [k for k in far if k % 2 == 0]) if ks]

    def part(firsts, ks):
        return [(f, s, k, r) for f in firsts for s in second_last for k in ks for r in range(height)]

    sent, kept = [[part(firsts, ks) for ks in chunks] for firsts in (first_last[:-1], [0])]
    if by_neighbour:
        sent.append(part(first_last, [1]))
        kept.append(part(first_last, [0]))
    table = np.array(
        [(core, *row) for half in (sent, kept) for core in [*range(1, nc), 0] for piece in half for row in piece],
        np.int32,
    ).T
    sent, kept = [[len(piece) for piece in half] for half in (sent, kept)]
    return table, chunks, by_neighbour, sent, kept


def shards(latent, w_in, w_out, observed, patch_index, counts):
    rows_in = latent[0, 0]
    nrows, depth = rows_in.shape
    width, channels = w_out.shape
    nz, nt, ny = (lax.axis_size(name) for name in ("member", "tile", "batch"))
    nc, nx = CORES, nt // CORES
    w_out_t = w_out.T
    height = depth // (nz * nt * ny)
    table, chunks, by_neighbour, sent, kept = row_order(nz, nx, nc, ny, height)
    turned = 1 if nx == ny else 0

    far_first = [*reversed(range(nz))]
    everywhere = [(z, x, c, y) for z in range(nz) for x in range(nx) for c in range(nc) for y in range(ny)]

    def shift(value, target):
        def number(z, x, c, y):
            return (z * nt + x * nc + c) * ny + y

        return lax.ppermute(
            value, ("member", "tile", "batch"), [(number(*place), number(*target(*place))) for place in everywhere]
        )

    def send_to(value, k):
        return shift(value, lambda z, x, c, y: (partner(z, k, nz), x, c, y))

    def exchange(values):
        return [send_to(values[k], k) if k else values[0] for k in far_first]

    def shift_core(value, j):
        return shift(value, lambda z, x, c, y: (z, x, (c + j) % nc, y))

    def along(of_core):
        def shift_one(value, j):
            def target(z, x, c, y):
                return (z, (x + j) % nx, c, y) if of_core(c) == 0 else (z, x, c, (y + j) % ny)

            return shift(value, target)

        return shift_one

    shift_first, shift_second = along(lambda c: c * turned), along(lambda c: 1 - c * turned)

    def send_all(value, others, shift_one):
        if others == 1:
            return [shift_one(value, 1)]
        return [shift_one(v, j + 1) for j, v in enumerate(jnp.split(value, others, axis=0))] if others else []

    share = nrows // PATCH // nz
    packed = dict(zip(far_first, decode(rows_in, w_in, w_out_t, nz, far_first)))
    grouped = exchange(packed)

    def source_of(columns):
        me_z, me_t, me_y = (lax.axis_index(name) for name in ("member", "tile", "batch"))
        core, first, second, k, row = columns[:5]
        z = partner(me_z, k, nz)
        core = lax.rem(core + lax.rem(me_t, nc), nc)
        turn = core * turned
        x, y = first + turn * (second - first), second + turn * (first - second)
        tile = lax.rem(x + me_t // nc, nx) * nc + core
        return ((z * nt + tile) * ny + lax.rem(y + me_y, ny)) * height + row

    table = np.concatenate([table, np.zeros((-len(table) % 8, table.shape[1]), np.int32)])
    n_send, n_keep = sum(sent), sum(kept)
    middle = 2 * n_send

    slope, hidden = slopes(rows_in, w_in)
    target, weight = targets(observed[0], patch_index, counts, share, channels)
    grouped, slope, hidden, target, weight = lax.optimization_barrier((grouped, slope, hidden, target, weight))

    scored = score(grouped, target, weight)
    returned = exchange(dict(zip(far_first, scored)))
    ordered = ordered_transposes(table, source_of, rows_in, hidden)
    returned, ordered = lax.optimization_barrier((returned, ordered))

    other_send, gp, g = first_products(returned, slope, w_out_t, ordered, n_send)
    core_send = shift_core(other_send, 1)
    own_send, other_keep = more_products(gp, g, ordered, [(n_send, middle), (middle, middle + n_keep)])
    core_keep = shift_core(other_keep, 1)

    def added(inputs, pieces, flops=0):
        return list(add_rows(inputs, [[(0, rows, [(i, low) for i in range(len(inputs))])] for low, rows in pieces], flops))

    def pieces_of(sizes, low=0):
        return [(low + int(at), size) for at, size in zip(np.cumsum([0, *sizes[:-1]]), sizes)]

    first_sends = added([own_send, core_send], pieces_of(sent))
    first_sends, gp = lax.optimization_barrier((first_sends, gp))
    first_got = [send_all(value, nx - 1, shift_first) for value in first_sends[:len(chunks)]]
    neighbour = [send_to(value, 1) for value in first_sends[len(chunks):]]
    (own_keep,) = more_products(gp, g, ordered, [(middle + n_keep, middle + 2 * n_keep)])

    def split_sums(inputs, lows, rows, n):
        cut = rows // n * (n - 1)
        plans = [[(0, size, [(i, low + at) for i, low in enumerate(lows)])] for at, size in ((0, cut), (cut, rows - cut))]
        return add_rows(inputs, plans)

    joined = {}
    for ks, (low, size), got in zip(chunks, pieces_of(kept), first_got):
        value, keep = split_sums([own_keep, core_keep, *got], [low, low, *[0] * len(got)], size, ny)
        got = send_all(value, ny - 1, shift_second)
        joined.update(zip(ks, added([keep, *got], pieces_of([height] * len(ks)))))
    if not by_neighbour:
        return tuple(finish(exchange(joined), width, channels))

    near = {k: send_to(joined[k], 1) for k in range(nz - 1, 1, -2)}
    far = [send_to(added([joined[k], near[k + 1]], [(0, height)])[0], k) for k in range(2, nz, 2)]
    low, size = pieces_of(kept)[-1]
    value, keep = split_sums([own_keep, core_keep, *neighbour], [low, low, 0], size, nx)
    got = send_all(value, nx - 1, shift_first)
    value, keep = split_sums([keep, *got], [0] * (1 + len(got)), keep.shape[0], ny)
    parts = [keep, *send_all(value, ny - 1, shift_second)]
    if far:
        parts += added(far, [(0, height)], 4e9)
    return tuple(finish(parts, width, channels))


def solution(mesh):
    in_specs = (
        P("member", "batch", "tile", None),
        P(),
        P(),
        P("batch", "tile", None),
        P("batch", "tile"),
        P("batch", "tile"),
    )
    out_specs = (P(("member", "tile", "batch"), None), P(("member", "tile", "batch"), None))
    return jax.shard_map(shards, mesh=mesh, in_specs=in_specs, out_specs=out_specs, check_vma=False)
```

```python
import functools

import jax
import jax.numpy as jnp
import numpy as np
from jax import lax
from jax.experimental import pallas as pl
from jax.experimental.pallas import tpu as pltpu
from jax.sharding import PartitionSpec as P

PATCH = 16
CORES = 2
LANES = 128
MIB = 1 << 20
NT = (((1,), (1,)), ((), ()))
WHOLE = pl.BlockSpec()
ANY = pl.BlockSpec(memory_space=pl.ANY)
FEW = 24
MOST = 56


def partner(z, k, nz):
    return z ^ k if nz & (nz - 1) == 0 else (z + k) % nz


def params(mib=24):
    return pltpu.CompilerParams(vmem_limit_bytes=int(mib * MIB))


def cost(flops, moved):
    return pl.CostEstimate(flops=int(flops), bytes_accessed=int(moved), transcendentals=0)


def packing(channels):
    spare = LANES - channels
    carriers = PATCH * channels // LANES
    per_cell = channels // spare
    assert carriers * LANES == PATCH * channels and per_cell * spare == channels
    return spare, carriers, per_cell


def pack(cell, channels):
    spare, carriers, per_cell = packing(channels)
    extra = [cell(j) for j in range(carriers, PATCH)]
    lane = lax.broadcasted_iota(jnp.int32, extra[0].shape, 1)
    rows = []
    for j in range(carriers):
        piece = extra[j // per_cell]
        moved = pltpu.roll(piece, channels - j % per_cell * spare, 1)
        rows.append(jnp.where(lane < channels, cell(j), moved))
    return rows


def unpack(rows, channels):
    spare, carriers, per_cell = packing(channels)
    lane = lax.broadcasted_iota(jnp.int32, rows[0].shape, 1)
    cells = list(rows)
    for first in range(0, carriers, per_cell):
        value = jnp.zeros_like(rows[0])
        for i in range(per_cell):
            moved = pltpu.roll(rows[first + i], (i * spare - channels) % LANES, 1)
            value = jnp.where((lane >= i * spare) & (lane < (i + 1) * spare), moved, value)
        cells.append(value)
    return cells


def in_hbm(value):
    return pltpu.with_memory_space_constraint(value, pltpu.HBM)


def column_steps(width):
    step = 256 if width % 256 == 0 else width
    return [slice(low, low + step) for low in range(0, width, step)]


def decode_body(pieces, latent_ref, w_in_ref, w_out_t_ref, *refs):
    out_refs, (rows, w_in, w_out_t, cells, row_sems, sems) = refs[:len(pieces)], refs[len(pieces):]
    count, block, _ = rows.shape
    channels = w_out_t.shape[0]
    share = out_refs[0].shape[1]
    half = max(count // 2, 1)
    me_z, nz = lax.axis_index("member"), lax.axis_size("member")
    row_copies = []
    for i, k in enumerate(pieces):
        start = pl.multiple_of(partner(me_z, k, nz) * block, block)
        row_copies.append(pltpu.make_async_copy(latent_ref.at[pl.ds(start, block)], rows.at[i], row_sems.at[i]))
    w_copies = [pltpu.make_async_copy(w_in_ref, w_in, sems.at[0]), pltpu.make_async_copy(w_out_t_ref, w_out_t, sems.at[1])]
    for copy in [*w_copies, *row_copies]:
        copy.start()
    for copy in [*w_copies, *row_copies[:half]]:
        copy.wait()
    for i in range(count):
        if i == half:
            for copy in row_copies[half:]:
                copy.wait()
        preact = jnp.dot(rows[i], w_in[...], preferred_element_type=jnp.float32)
        hidden = (preact / (1.0 + jnp.exp(-preact))).astype(jnp.bfloat16)
        cells[i, :, :channels] = lax.dot_general(hidden, w_out_t[...], NT, preferred_element_type=jnp.float32)
        for j, row in enumerate(pack(lambda j: cells[i, pl.ds(j, share, stride=PATCH), :], channels)):
            out_refs[i][j] = row


def decode(rows_in, w_in, w_out_t, parts, pieces):
    nrows, depth = rows_in.shape
    width = w_in.shape[1]
    channels = w_out_t.shape[0]
    block = nrows // parts
    share = block // PATCH
    carriers = packing(channels)[1]
    count = len(pieces)
    return pl.pallas_call(
        functools.partial(decode_body, tuple(pieces)),
        in_specs=[ANY] * 3,
        out_specs=[WHOLE] * count,
        out_shape=[jax.ShapeDtypeStruct((carriers, share, LANES), jnp.float32)] * count,
        scratch_shapes=[
            pltpu.VMEM((count, block, depth), jnp.bfloat16),
            pltpu.VMEM((depth, width), jnp.bfloat16),
            pltpu.VMEM((channels, width), jnp.bfloat16),
            pltpu.VMEM((count, block, LANES), jnp.float32),
            pltpu.SemaphoreType.DMA((count,)),
            pltpu.SemaphoreType.DMA((2,)),
        ],
        compiler_params=params(MOST),
        cost_estimate=cost(2 * nrows * width * (depth + channels), 5 * MIB),
        name="decode",
    )(rows_in, w_in, w_out_t)


def fill_choice(source, choice):
    picked, extent = choice.shape
    for low in range(0, picked, LANES):
        high = min(low + LANES, picked)
        across = jnp.broadcast_to(source[:, low:high], (LANES, high - low))
        down = jnp.transpose(across)
        for left in range(0, extent, LANES):
            here = lax.broadcasted_iota(jnp.int32, down.shape, 1) + left
            choice[low:high, left:left + LANES] = jnp.where(down == here, 1.0, 0.0).astype(jnp.bfloat16)


def slope_body(latent_ref, w_in_ref, slope_ref, hidden_ref):
    preact = jnp.dot(latent_ref[...], w_in_ref[...], preferred_element_type=jnp.float32)
    scale = 1.0 + jnp.exp(-preact)
    sigma = 1.0 / scale
    slope_ref[...] = sigma * (1.0 + preact * (1.0 - sigma))
    hidden_ref[...] = (preact / scale).astype(jnp.bfloat16)


def slopes(rows_in, w_in):
    nrows, depth = rows_in.shape
    width = w_in.shape[1]
    block = 256 if nrows % 256 == 0 else nrows
    return pl.pallas_call(
        slope_body,
        grid=(nrows // block,),
        in_specs=[pl.BlockSpec((block, depth), lambda i: (i, 0)), pl.BlockSpec((depth, width), lambda i: (0, 0))],
        out_specs=[pl.BlockSpec((block, width), lambda i: (i, 0)), pl.BlockSpec((block, width), lambda i: (i, 0))],
        out_shape=[
            jax.ShapeDtypeStruct((nrows, width), jnp.float32),
            jax.ShapeDtypeStruct((nrows, width), jnp.bfloat16),
        ],
        compiler_params=params(FEW),
        cost_estimate=cost(2 * nrows * width * depth, 4 * MIB),
        name="slopes",
    )(in_hbm(rows_in), in_hbm(w_in))


def order_body(source_of, table_ref, latent_ref, hidden_ref, out_ref, choice):
    @pl.when(pl.program_id(0) == 0)
    def _():
        fill_choice(source_of([table_ref[k:k + 1] for k in range(table_ref.shape[0])]), choice)

    for k, matrix_ref in enumerate((latent_ref, hidden_ref)):
        ordered = lax.dot_general(choice[...], matrix_ref[...], NT, preferred_element_type=jnp.float32)
        out_ref[k] = ordered.astype(jnp.bfloat16)


def ordered_transposes(table, source_of, latent, hidden):
    nrows, extent = latent.shape
    picked = table.shape[1]
    block = 256 if nrows % 256 == 0 else nrows
    return pl.pallas_call(
        functools.partial(order_body, source_of),
        grid=(nrows // block,),
        in_specs=[
            pl.BlockSpec(table.shape, lambda i: (0, 0)),
            pl.BlockSpec((block, extent), lambda i: (i, 0)),
            pl.BlockSpec((block, extent), lambda i: (i, 0)),
        ],
        out_specs=pl.BlockSpec((2, picked, block), lambda i: (0, 0, i)),
        out_shape=jax.ShapeDtypeStruct((2, picked, nrows), jnp.bfloat16),
        scratch_shapes=[pltpu.VMEM((picked, extent), jnp.bfloat16)],
        compiler_params=params(FEW),
        cost_estimate=cost(nrows * extent * picked, 4 * MIB),
        name="ordered_transposes",
    )(table, in_hbm(latent), hidden)


def target_body(channels, pool_ref, index_ref, count_ref, target_ref, weight_ref):
    carriers, share, _ = target_ref.shape
    npool, total = pool_ref.shape
    npatch = index_ref.shape[1]
    own = lax.broadcasted_iota(jnp.int32, (share, npatch), 0) + lax.axis_index("member") * share
    own = own == lax.broadcasted_iota(jnp.int32, (share, npatch), 1)
    index = jnp.sum(jnp.where(own, index_ref[...], 0), axis=1, keepdims=True)
    count = jnp.sum(jnp.where(own, count_ref[...], 0), axis=1, keepdims=True)
    weight_ref[...] = jnp.broadcast_to(count.astype(jnp.float32), weight_ref.shape)
    choose = index == lax.broadcasted_iota(jnp.int32, (share, npool), 1)
    flat = jnp.dot(
        jnp.where(choose, 1.0, 0.0).astype(jnp.bfloat16), pool_ref[...], preferred_element_type=jnp.float32
    )

    def cell(j):
        start = j * channels
        low = start // LANES * LANES
        part = flat[:, low:min(low + 2 * LANES, total)]
        return pltpu.roll(part, (low - start) % part.shape[1], 1)[:, :LANES]

    for j, row in enumerate(pack(cell, channels)):
        target_ref[j] = row


def targets(pool, index, count, share, channels):
    carriers = packing(channels)[1]
    return pl.pallas_call(
        functools.partial(target_body, channels),
        in_specs=[WHOLE] * 3,
        out_specs=[WHOLE] * 2,
        out_shape=[
            jax.ShapeDtypeStruct((carriers, share, LANES), jnp.float32),
            jax.ShapeDtypeStruct((share, LANES), jnp.float32),
        ],
        compiler_params=params(),
        cost_estimate=cost(2 * share * pool.size, 2 * pool.size),
        name="targets",
    )(pool, index, count)


def score_body(members, *refs):
    x_refs, (target_ref, weight_ref), out_refs = refs[:members], refs[members:members + 2], refs[members + 2:]
    carriers = target_ref.shape[0]
    weight = weight_ref[...]

    def inverse_norm(delta):
        squares = sum(d * d for d in delta)
        return 1.0 / jnp.sqrt(jnp.sum(squares, axis=-1, keepdims=True) + 1.0)

    target = [target_ref[j] for j in range(carriers)]
    xs = [[ref[j] for j in range(carriers)] for ref in x_refs]
    pair = [[jnp.zeros_like(target[0])] * carriers for _ in range(members)]
    for m in range(members):
        for k in range(m + 1, members):
            delta = [p - q for p, q in zip(xs[m], xs[k])]
            inverse = inverse_norm(delta)
            pair[m] = [p + d * inverse for p, d in zip(pair[m], delta)]
            pair[k] = [p - d * inverse for p, d in zip(pair[k], delta)]
    for m in range(members):
        delta = [p - q for p, q in zip(xs[m], target)]
        inverse = inverse_norm(delta)
        for j in range(carriers):
            out_refs[m][j] = weight * (delta[j] * inverse / members - pair[m][j] / (members * members))


def score(pieces, target, weight):
    members = len(pieces)
    size = members * target.size
    return pl.pallas_call(
        functools.partial(score_body, members),
        in_specs=[WHOLE] * (members + 2),
        out_specs=[WHOLE] * members,
        out_shape=[jax.ShapeDtypeStruct(target.shape, jnp.float32)] * members,
        compiler_params=params(),
        cost_estimate=cost(30 * size, 8 * size),
        name="score",
    )(*pieces, target, weight)


def first_body(parts, *refs):
    scored_refs, (slope, w_out_t, ordered, result, gp, g, cells) = refs[:parts], refs[parts:]
    carriers, share, _ = scored_refs[0].shape
    channels, width = w_out_t.shape
    picked = result.shape[0]
    me_z = lax.axis_index("member")
    for k, scored_ref in zip(reversed(range(parts)), scored_refs):
        base = partner(me_z, k, parts) * (share * PATCH)
        for j, value in enumerate(unpack([scored_ref[j] for j in range(carriers)], channels)):
            cells[pl.ds(base + j, share, stride=PATCH), :] = value
    lane = lax.broadcasted_iota(jnp.int32, cells.shape, 1)
    g[...] = jnp.where(lane < channels, cells[...], 0.0).astype(jnp.bfloat16)
    result[:, width:] = jnp.dot(ordered[1, :picked], g[...], preferred_element_type=jnp.float32)
    for c in column_steps(width):
        backward = jnp.dot(g[:, :channels], w_out_t[:, c], preferred_element_type=jnp.float32)
        gp[:, c] = (backward * slope[:, c]).astype(jnp.bfloat16)
        result[:, c] = jnp.dot(ordered[0, :picked], gp[:, c], preferred_element_type=jnp.float32)


def first_products(scored, slope, w_out_t, ordered, picked):
    nrows, width = slope.shape
    channels = w_out_t.shape[0]
    return pl.pallas_call(
        functools.partial(first_body, len(scored)),
        in_specs=[WHOLE] * (len(scored) + 3),
        out_specs=[WHOLE] * 3,
        out_shape=[
            jax.ShapeDtypeStruct((picked, width + LANES), jnp.float32),
            jax.ShapeDtypeStruct((nrows, width), jnp.bfloat16),
            jax.ShapeDtypeStruct((nrows, LANES), jnp.bfloat16),
        ],
        scratch_shapes=[pltpu.VMEM((nrows, LANES), jnp.float32)],
        compiler_params=params(FEW),
        cost_estimate=cost(2 * nrows * width * (channels + picked), 10 * MIB),
        name="first_products",
    )(*scored, slope, w_out_t, ordered)


def more_body(cuts, gp, g, ordered, *out_refs):
    low, high = cuts[0][0], cuts[-1][1]
    width = gp.shape[1]

    def put(columns, product):
        for out_ref, (start, end) in zip(out_refs, cuts):
            out_ref[:, columns] = product[start - low:end - low]

    for columns in column_steps(width):
        put(columns, jnp.dot(ordered[0, low:high], gp[:, columns], preferred_element_type=jnp.float32))
    put(slice(width, None), jnp.dot(ordered[1, low:high], g[...], preferred_element_type=jnp.float32))


def more_products(gp, g, ordered, cuts):
    nrows, width = gp.shape
    picked = cuts[-1][1] - cuts[0][0]
    return pl.pallas_call(
        functools.partial(more_body, tuple(cuts)),
        in_specs=[WHOLE] * 3,
        out_specs=[WHOLE] * len(cuts),
        out_shape=[jax.ShapeDtypeStruct((end - start, width + LANES), jnp.float32) for start, end in cuts],
        compiler_params=params(FEW),
        cost_estimate=cost(2 * nrows * picked * width, 6 * MIB),
        name="more_products",
    )(gp, g, ordered)


def add_body(plans, count, *refs):
    inputs, outputs = refs[:count], refs[count:]
    for out_ref, plan in zip(outputs, plans):
        for at, rows, sources in plan:
            total = None
            for which, low in sources:
                value = inputs[which][low:low + rows]
                total = value if total is None else total + value
            out_ref[at:at + rows] = total


def add_rows(inputs, plans, flops=0):
    columns = inputs[0].shape[1]
    sizes = [sum(rows for _, rows, _ in plan) for plan in plans]
    return pl.pallas_call(
        functools.partial(add_body, plans, len(inputs)),
        in_specs=[WHOLE] * len(inputs),
        out_specs=[WHOLE] * len(plans),
        out_shape=[jax.ShapeDtypeStruct((size, columns), jnp.float32) for size in sizes],
        compiler_params=params(),
        cost_estimate=cost(flops or 3 * sum(sizes) * columns, 12 * sum(sizes) * columns),
        name="add_rows",
    )(*inputs)


def finish_body(*refs):
    *parts, first_ref, second_ref = refs
    width, channels = first_ref.shape[1], second_ref.shape[1]
    total = parts[0][...]
    for ref in parts[1:]:
        total = total + ref[...]
    first_ref[...] = total[:, :width]
    second_ref[...] = total[:, width:width + channels]


def finish(parts, width, channels):
    height = parts[0].shape[0]
    return pl.pallas_call(
        finish_body,
        in_specs=[WHOLE] * len(parts),
        out_specs=[WHOLE] * 2,
        out_shape=[
            jax.ShapeDtypeStruct((height, width), jnp.float32),
            jax.ShapeDtypeStruct((height, channels), jnp.float32),
        ],
        compiler_params=params(),
        cost_estimate=cost(4 * height * width, 20 * height * width),
        name="finish",
    )(*parts)


def row_order(nz, nx, nc, ny, height):
    first_last, second_last = [[*range(1, n), 0] for n in (nx, ny)]
    z_last = [*reversed(range(nz))]
    far = [k for k in z_last if k > 1]
    chunks = [[k for k in far if k % 2], [k for k in far if k % 2 == 0], *[[k] for k in z_last if k < 2]]
    chunks = [ks for ks in chunks if ks]

    def part(firsts, ks):
        return [(f, s, k, r) for f in firsts for s in second_last for k in ks for r in range(height)]

    halves = [[part(firsts, ks) for ks in chunks] for firsts in (first_last[:-1], [0])]
    table = np.array(
        [(core, *row) for half in halves for core in [*range(1, nc), 0] for piece in half for row in piece], np.int32
    ).T
    sent, kept = [[len(piece) for piece in half] for half in halves]
    return table, chunks, sent, kept


def shards(latent, w_in, w_out, observed, patch_index, counts):
    rows_in = latent[0, 0]
    nrows, depth = rows_in.shape
    width, channels = w_out.shape
    nz, nt, ny = (lax.axis_size(name) for name in ("member", "tile", "batch"))
    nc, nx = CORES, nt // CORES
    w_out_t = w_out.T
    height = depth // (nz * nt * ny)
    table, chunks, sent, kept = row_order(nz, nx, nc, ny, height)
    turned = 1 if nx == ny else 0

    far_first = [*reversed(range(nz))]
    everywhere = [(z, x, c, y) for z in range(nz) for x in range(nx) for c in range(nc) for y in range(ny)]

    def shift(value, target):
        def number(z, x, c, y):
            return (z * nt + x * nc + c) * ny + y

        return lax.ppermute(
            value, ("member", "tile", "batch"), [(number(*place), number(*target(*place))) for place in everywhere]
        )

    def send_to(value, k):
        return shift(value, lambda z, x, c, y: (partner(z, k, nz), x, c, y))

    def exchange(values):
        return [send_to(values[k], k) if k else values[0] for k in far_first]

    def shift_core(value, j):
        return shift(value, lambda z, x, c, y: (z, x, (c + j) % nc, y))

    def along(of_core):
        def shift_one(value, j):
            def target(z, x, c, y):
                return (z, (x + j) % nx, c, y) if of_core(c) == 0 else (z, x, c, (y + j) % ny)

            return shift(value, target)

        return shift_one

    shift_first, shift_second = along(lambda c: c * turned), along(lambda c: 1 - c * turned)

    def send_all(value, others, shift_one):
        if others == 1:
            return [shift_one(value, 1)]
        return [shift_one(v, j + 1) for j, v in enumerate(jnp.split(value, others, axis=0))] if others else []

    share = nrows // PATCH // nz
    packed = dict(zip(far_first, decode(rows_in, w_in, w_out_t, nz, far_first)))
    grouped = exchange(packed)

    def source_of(columns):
        me_z, me_t, me_y = (lax.axis_index(name) for name in ("member", "tile", "batch"))
        core, first, second, k, row = columns[:5]
        z = partner(me_z, k, nz)
        core = lax.rem(core + lax.rem(me_t, nc), nc)
        turn = core * turned
        x, y = first + turn * (second - first), second + turn * (first - second)
        tile = lax.rem(x + me_t // nc, nx) * nc + core
        return ((z * nt + tile) * ny + lax.rem(y + me_y, ny)) * height + row

    table = np.concatenate([table, np.zeros((-len(table) % 8, table.shape[1]), np.int32)])
    n_send, n_keep = sum(sent), sum(kept)
    middle = 2 * n_send

    slope, hidden = slopes(rows_in, w_in)
    target, weight = targets(observed[0], patch_index, counts, share, channels)
    grouped, slope, hidden, target, weight = lax.optimization_barrier((grouped, slope, hidden, target, weight))

    scored = score(grouped, target, weight)
    returned = exchange(dict(zip(far_first, scored)))
    ordered = ordered_transposes(table, source_of, rows_in, hidden)
    returned, ordered = lax.optimization_barrier((returned, ordered))

    other_send, gp, g = first_products(returned, slope, w_out_t, ordered, n_send)
    core_send = shift_core(other_send, 1)
    own_send, other_keep = more_products(gp, g, ordered, [(n_send, middle), (middle, middle + n_keep)])
    core_keep = shift_core(other_keep, 1)

    def added(inputs, pieces, flops=0):
        return list(add_rows(inputs, [[(0, rows, [(i, low) for i in range(len(inputs))])] for low, rows in pieces], flops))

    def pieces_of(sizes, low=0):
        return [(low + int(at), size) for at, size in zip(np.cumsum([0, *sizes[:-1]]), sizes)]

    first_sends = added([own_send, core_send], pieces_of(sent))
    first_sends, gp = lax.optimization_barrier((first_sends, gp))
    first_got = [send_all(value, nx - 1, shift_first) for value in first_sends]
    (own_keep,) = more_products(gp, g, ordered, [(middle + n_keep, middle + 2 * n_keep)])

    joined, near = {}, {}
    for ks, (low, size), got in zip(chunks, pieces_of(kept), first_got):
        if ks == chunks[-1] and len(chunks) > 3 and nz & (nz - 1) == 0:
            near = {k: send_to(joined[k], 1) for k in chunks[0]}
            got, near = lax.optimization_barrier((got, near))
        cut = size // ny * (ny - 1)
        terms = [(0, low), (1, low), *[(2 + i, 0) for i in range(len(got))]]
        second_send, second_keep = add_rows(
            [own_keep, core_keep, *got],
            [[(0, rows, [(i, start + at) for i, start in terms])] for at, rows in ((0, cut), (cut, size - cut))],
        )
        got = send_all(second_send, ny - 1, shift_second)
        joined.update(zip(ks, added([second_keep, *got], pieces_of([height] * len(ks)))))

    if nz & (nz - 1):
        return tuple(finish(exchange(joined), width, channels))
    near.update({k: send_to(joined[k], 1) for k in range(1, nz, 2) if k not in near})
    parts = [joined[0], *([near[1]] if near else [])]
    far = [send_to(added([joined[k], near[k + 1]], [(0, height)])[0], k) for k in range(2, nz, 2)]
    if far:
        parts += added(far, [(0, height)], 1.2e10)
    return tuple(finish(parts[::-1], width, channels))


def solution(mesh):
    in_specs = (
        P("member", "batch", "tile", None),
        P(),
        P(),
        P("batch", "tile", None),
        P("batch", "tile"),
        P("batch", "tile"),
    )
    out_specs = (P(("member", "tile", "batch"), None), P(("member", "tile", "batch"), None))
    return jax.shard_map(shards, mesh=mesh, in_specs=in_specs, out_specs=out_specs, check_vma=False)
```

```python
import functools

import jax
import jax.numpy as jnp
import numpy as np
from jax import lax
from jax.experimental import pallas as pl
from jax.experimental.pallas import tpu as pltpu
from jax.sharding import PartitionSpec as P

PATCH = 16
CORES = 2
LANES = 128
MIB = 1 << 20
NT = (((1,), (1,)), ((), ()))
WHOLE = pl.BlockSpec()
ANY = pl.BlockSpec(memory_space=pl.ANY)
FEW = 24
MOST = 56


def partner(z, k, nz):
    return z ^ k if nz & (nz - 1) == 0 else (z + k) % nz


def params(mib=24):
    return pltpu.CompilerParams(vmem_limit_bytes=int(mib * MIB))


def cost(flops, moved):
    return pl.CostEstimate(flops=int(flops), bytes_accessed=int(moved), transcendentals=0)


def packing(channels):
    spare = LANES - channels
    carriers = PATCH * channels // LANES
    per_cell = channels // spare
    assert carriers * LANES == PATCH * channels and per_cell * spare == channels
    return spare, carriers, per_cell


def pack(cell, channels):
    spare, carriers, per_cell = packing(channels)
    extra = [cell(j) for j in range(carriers, PATCH)]
    lane = lax.broadcasted_iota(jnp.int32, extra[0].shape, 1)
    rows = []
    for j in range(carriers):
        piece = extra[j // per_cell]
        moved = pltpu.roll(piece, channels - j % per_cell * spare, 1)
        rows.append(jnp.where(lane < channels, cell(j), moved))
    return rows


def unpack(rows, channels):
    spare, carriers, per_cell = packing(channels)
    lane = lax.broadcasted_iota(jnp.int32, rows[0].shape, 1)
    cells = list(rows)
    for first in range(0, carriers, per_cell):
        value = jnp.zeros_like(rows[0])
        for i in range(per_cell):
            moved = pltpu.roll(rows[first + i], (i * spare - channels) % LANES, 1)
            value = jnp.where((lane >= i * spare) & (lane < (i + 1) * spare), moved, value)
        cells.append(value)
    return cells


def in_hbm(value):
    return pltpu.with_memory_space_constraint(value, pltpu.HBM)


def column_steps(width):
    step = 256 if width % 256 == 0 else width
    return [slice(low, low + step) for low in range(0, width, step)]


def decode_body(pieces, latent_ref, w_in_ref, w_out_t_ref, *refs):
    out_refs, (rows, w_in, w_out_t, cells, row_sems, sems) = refs[:len(pieces)], refs[len(pieces):]
    count, block, _ = rows.shape
    channels = w_out_t.shape[0]
    share = out_refs[0].shape[1]
    half = max(count // 2, 1)
    me_z, nz = lax.axis_index("member"), lax.axis_size("member")
    row_copies = []
    for i, k in enumerate(pieces):
        start = pl.multiple_of(partner(me_z, k, nz) * block, block)
        row_copies.append(pltpu.make_async_copy(latent_ref.at[pl.ds(start, block)], rows.at[i], row_sems.at[i]))
    w_copies = [pltpu.make_async_copy(w_in_ref, w_in, sems.at[0]), pltpu.make_async_copy(w_out_t_ref, w_out_t, sems.at[1])]
    for copy in [*w_copies, *row_copies]:
        copy.start()
    for copy in [*w_copies, *row_copies[:half]]:
        copy.wait()
    for i in range(count):
        if i == half:
            for copy in row_copies[half:]:
                copy.wait()
        preact = jnp.dot(rows[i], w_in[...], preferred_element_type=jnp.float32)
        hidden = (preact / (1.0 + jnp.exp(-preact))).astype(jnp.bfloat16)
        cells[i, :, :channels] = lax.dot_general(hidden, w_out_t[...], NT, preferred_element_type=jnp.float32)
        for j, row in enumerate(pack(lambda j: cells[i, pl.ds(j, share, stride=PATCH), :], channels)):
            out_refs[i][j] = row


def decode(rows_in, w_in, w_out_t, parts, pieces):
    nrows, depth = rows_in.shape
    width = w_in.shape[1]
    channels = w_out_t.shape[0]
    block = nrows // parts
    share = block // PATCH
    carriers = packing(channels)[1]
    count = len(pieces)
    return pl.pallas_call(
        functools.partial(decode_body, tuple(pieces)),
        in_specs=[ANY] * 3,
        out_specs=[WHOLE] * count,
        out_shape=[jax.ShapeDtypeStruct((carriers, share, LANES), jnp.float32)] * count,
        scratch_shapes=[
            pltpu.VMEM((count, block, depth), jnp.bfloat16),
            pltpu.VMEM((depth, width), jnp.bfloat16),
            pltpu.VMEM((channels, width), jnp.bfloat16),
            pltpu.VMEM((count, block, LANES), jnp.float32),
            pltpu.SemaphoreType.DMA((count,)),
            pltpu.SemaphoreType.DMA((2,)),
        ],
        compiler_params=params(MOST),
        cost_estimate=cost(2 * nrows * width * (depth + channels), 5 * MIB),
        name="decode",
    )(rows_in, w_in, w_out_t)


def fill_choice(source, choice):
    picked, extent = choice.shape
    for low in range(0, picked, LANES):
        high = min(low + LANES, picked)
        across = jnp.broadcast_to(source[:, low:high], (LANES, high - low))
        down = jnp.transpose(across)
        for left in range(0, extent, LANES):
            here = lax.broadcasted_iota(jnp.int32, down.shape, 1) + left
            choice[low:high, left:left + LANES] = jnp.where(down == here, 1.0, 0.0).astype(jnp.bfloat16)


def slope_body(latent_ref, w_in_ref, slope_ref, hidden_ref):
    preact = jnp.dot(latent_ref[...], w_in_ref[...], preferred_element_type=jnp.float32)
    scale = 1.0 + jnp.exp(-preact)
    sigma = 1.0 / scale
    slope_ref[...] = sigma * (1.0 + preact * (1.0 - sigma))
    hidden_ref[...] = (preact / scale).astype(jnp.bfloat16)


def slopes(rows_in, w_in):
    nrows, depth = rows_in.shape
    width = w_in.shape[1]
    block = 256 if nrows % 256 == 0 else nrows
    return pl.pallas_call(
        slope_body,
        grid=(nrows // block,),
        in_specs=[pl.BlockSpec((block, depth), lambda i: (i, 0)), pl.BlockSpec((depth, width), lambda i: (0, 0))],
        out_specs=[pl.BlockSpec((block, width), lambda i: (i, 0)), pl.BlockSpec((block, width), lambda i: (i, 0))],
        out_shape=[
            jax.ShapeDtypeStruct((nrows, width), jnp.float32),
            jax.ShapeDtypeStruct((nrows, width), jnp.bfloat16),
        ],
        compiler_params=params(FEW),
        cost_estimate=cost(2 * nrows * width * depth, 4 * MIB),
        name="slopes",
    )(in_hbm(rows_in), in_hbm(w_in))


def order_body(source_of, table_ref, latent_ref, hidden_ref, out_ref, choice):
    @pl.when(pl.program_id(0) == 0)
    def _():
        fill_choice(source_of([table_ref[k:k + 1] for k in range(table_ref.shape[0])]), choice)

    for k, matrix_ref in enumerate((latent_ref, hidden_ref)):
        ordered = lax.dot_general(choice[...], matrix_ref[...], NT, preferred_element_type=jnp.float32)
        out_ref[k] = ordered.astype(jnp.bfloat16)


def ordered_transposes(table, source_of, latent, hidden):
    nrows, extent = latent.shape
    picked = table.shape[1]
    block = 256 if nrows % 256 == 0 else nrows
    return pl.pallas_call(
        functools.partial(order_body, source_of),
        grid=(nrows // block,),
        in_specs=[
            pl.BlockSpec(table.shape, lambda i: (0, 0)),
            pl.BlockSpec((block, extent), lambda i: (i, 0)),
            pl.BlockSpec((block, extent), lambda i: (i, 0)),
        ],
        out_specs=pl.BlockSpec((2, picked, block), lambda i: (0, 0, i)),
        out_shape=jax.ShapeDtypeStruct((2, picked, nrows), jnp.bfloat16),
        scratch_shapes=[pltpu.VMEM((picked, extent), jnp.bfloat16)],
        compiler_params=params(FEW),
        cost_estimate=cost(nrows * extent * picked, 4 * MIB),
        name="ordered_transposes",
    )(table, in_hbm(latent), hidden)


def target_body(channels, pool_ref, index_ref, count_ref, target_ref, weight_ref):
    carriers, share, _ = target_ref.shape
    npool, total = pool_ref.shape
    npatch = index_ref.shape[1]
    own = lax.broadcasted_iota(jnp.int32, (share, npatch), 0) + lax.axis_index("member") * share
    own = own == lax.broadcasted_iota(jnp.int32, (share, npatch), 1)
    index = jnp.sum(jnp.where(own, index_ref[...], 0), axis=1, keepdims=True)
    count = jnp.sum(jnp.where(own, count_ref[...], 0), axis=1, keepdims=True)
    weight_ref[...] = jnp.broadcast_to(count.astype(jnp.float32), weight_ref.shape)
    choose = index == lax.broadcasted_iota(jnp.int32, (share, npool), 1)
    flat = jnp.dot(
        jnp.where(choose, 1.0, 0.0).astype(jnp.bfloat16), pool_ref[...], preferred_element_type=jnp.float32
    )

    def cell(j):
        start = j * channels
        low = start // LANES * LANES
        part = flat[:, low:min(low + 2 * LANES, total)]
        return pltpu.roll(part, (low - start) % part.shape[1], 1)[:, :LANES]

    for j, row in enumerate(pack(cell, channels)):
        target_ref[j] = row


def targets(pool, index, count, share, channels):
    carriers = packing(channels)[1]
    return pl.pallas_call(
        functools.partial(target_body, channels),
        in_specs=[WHOLE] * 3,
        out_specs=[WHOLE] * 2,
        out_shape=[
            jax.ShapeDtypeStruct((carriers, share, LANES), jnp.float32),
            jax.ShapeDtypeStruct((share, LANES), jnp.float32),
        ],
        compiler_params=params(),
        cost_estimate=cost(2 * share * pool.size, 2 * pool.size),
        name="targets",
    )(pool, index, count)


def score_body(members, *refs):
    x_refs, (target_ref, weight_ref), out_refs = refs[:members], refs[members:members + 2], refs[members + 2:]
    carriers = target_ref.shape[0]
    weight = weight_ref[...]

    def inverse_norm(delta):
        squares = sum(d * d for d in delta)
        return 1.0 / jnp.sqrt(jnp.sum(squares, axis=-1, keepdims=True) + 1.0)

    target = [target_ref[j] for j in range(carriers)]
    xs = [[ref[j] for j in range(carriers)] for ref in x_refs]
    pair = [[jnp.zeros_like(target[0])] * carriers for _ in range(members)]
    for m in range(members):
        for k in range(m + 1, members):
            delta = [p - q for p, q in zip(xs[m], xs[k])]
            inverse = inverse_norm(delta)
            pair[m] = [p + d * inverse for p, d in zip(pair[m], delta)]
            pair[k] = [p - d * inverse for p, d in zip(pair[k], delta)]
    for m in range(members):
        delta = [p - q for p, q in zip(xs[m], target)]
        inverse = inverse_norm(delta)
        for j in range(carriers):
            out_refs[m][j] = weight * (delta[j] * inverse / members - pair[m][j] / (members * members))


def score(pieces, target, weight):
    members = len(pieces)
    size = members * target.size
    return pl.pallas_call(
        functools.partial(score_body, members),
        in_specs=[WHOLE] * (members + 2),
        out_specs=[WHOLE] * members,
        out_shape=[jax.ShapeDtypeStruct(target.shape, jnp.float32)] * members,
        compiler_params=params(),
        cost_estimate=cost(30 * size, 8 * size),
        name="score",
    )(*pieces, target, weight)


def first_body(parts, cuts, *refs):
    scored_refs, (slope, w_out_t, ordered, *results, gp, g, cells) = refs[:parts], refs[parts:]
    carriers, share, _ = scored_refs[0].shape
    channels, width = w_out_t.shape
    picked = cuts[-1]

    def put(columns, product):
        for result, low, high in zip(results, cuts[:-1], cuts[1:]):
            result[:, columns] = product[low:high]

    me_z = lax.axis_index("member")
    for k, scored_ref in zip(reversed(range(parts)), scored_refs):
        base = partner(me_z, k, parts) * (share * PATCH)
        for j, value in enumerate(unpack([scored_ref[j] for j in range(carriers)], channels)):
            cells[pl.ds(base + j, share, stride=PATCH), :] = value
    lane = lax.broadcasted_iota(jnp.int32, cells.shape, 1)
    g[...] = jnp.where(lane < channels, cells[...], 0.0).astype(jnp.bfloat16)
    put(slice(width, None), jnp.dot(ordered[1, :picked], g[...], preferred_element_type=jnp.float32))
    for c in column_steps(width):
        backward = jnp.dot(g[:, :channels], w_out_t[:, c], preferred_element_type=jnp.float32)
        gp[:, c] = (backward * slope[:, c]).astype(jnp.bfloat16)
        put(c, jnp.dot(ordered[0, :picked], gp[:, c], preferred_element_type=jnp.float32))


def first_products(scored, slope, w_out_t, ordered, cuts):
    nrows, width = slope.shape
    channels = w_out_t.shape[0]
    return pl.pallas_call(
        functools.partial(first_body, len(scored), tuple(cuts)),
        in_specs=[WHOLE] * (len(scored) + 3),
        out_specs=[WHOLE] * (len(cuts) + 1),
        out_shape=[
            *[jax.ShapeDtypeStruct((high - low, width + LANES), jnp.float32) for low, high in zip(cuts[:-1], cuts[1:])],
            jax.ShapeDtypeStruct((nrows, width), jnp.bfloat16),
            jax.ShapeDtypeStruct((nrows, LANES), jnp.bfloat16),
        ],
        scratch_shapes=[pltpu.VMEM((nrows, LANES), jnp.float32)],
        compiler_params=params(FEW),
        cost_estimate=cost(2 * nrows * width * (channels + cuts[-1]), 10 * MIB),
        name="first_products",
    )(*scored, slope, w_out_t, ordered)


def more_body(cuts, gp, g, ordered, *out_refs):
    low, high = cuts[0][0], cuts[-1][1]
    width = gp.shape[1]

    def put(columns, product):
        for out_ref, (start, end) in zip(out_refs, cuts):
            out_ref[:, columns] = product[start - low:end - low]

    for columns in column_steps(width):
        put(columns, jnp.dot(ordered[0, low:high], gp[:, columns], preferred_element_type=jnp.float32))
    put(slice(width, None), jnp.dot(ordered[1, low:high], g[...], preferred_element_type=jnp.float32))


def more_products(gp, g, ordered, cuts):
    nrows, width = gp.shape
    picked = cuts[-1][1] - cuts[0][0]
    return pl.pallas_call(
        functools.partial(more_body, tuple(cuts)),
        in_specs=[WHOLE] * 3,
        out_specs=[WHOLE] * len(cuts),
        out_shape=[jax.ShapeDtypeStruct((end - start, width + LANES), jnp.float32) for start, end in cuts],
        compiler_params=params(FEW),
        cost_estimate=cost(2 * nrows * picked * width, 6 * MIB),
        name="more_products",
    )(gp, g, ordered)


def add_body(plans, count, *refs):
    inputs, outputs = refs[:count], refs[count:]
    for out_ref, plan in zip(outputs, plans):
        for at, rows, sources in plan:
            total = None
            for which, low in sources:
                value = inputs[which][low:low + rows]
                total = value if total is None else total + value
            out_ref[at:at + rows] = total


def add_rows(inputs, plans, flops=0):
    columns = inputs[0].shape[1]
    sizes = [sum(rows for _, rows, _ in plan) for plan in plans]
    return pl.pallas_call(
        functools.partial(add_body, plans, len(inputs)),
        in_specs=[WHOLE] * len(inputs),
        out_specs=[WHOLE] * len(plans),
        out_shape=[jax.ShapeDtypeStruct((size, columns), jnp.float32) for size in sizes],
        compiler_params=params(),
        cost_estimate=cost(flops or 3 * sum(sizes) * columns, 12 * sum(sizes) * columns),
        name="add_rows",
    )(*inputs)


def finish_body(*refs):
    *parts, first_ref, second_ref = refs
    width, channels = first_ref.shape[1], second_ref.shape[1]
    total = parts[0][...]
    for ref in parts[1:]:
        total = total + ref[...]
    first_ref[...] = total[:, :width]
    second_ref[...] = total[:, width:width + channels]


def finish(parts, width, channels):
    height = parts[0].shape[0]
    return pl.pallas_call(
        finish_body,
        in_specs=[WHOLE] * len(parts),
        out_specs=[WHOLE] * 2,
        out_shape=[
            jax.ShapeDtypeStruct((height, width), jnp.float32),
            jax.ShapeDtypeStruct((height, channels), jnp.float32),
        ],
        compiler_params=params(),
        cost_estimate=cost(4 * height * width, 20 * height * width),
        name="finish",
    )(*parts)


def row_order(nz, nx, nc, ny, height):
    first_last, second_last = [[*range(1, n), 0] for n in (nx, ny)]
    z_last = [*reversed(range(nz))]
    far = [k for k in z_last if k > 1]
    chunks = [[k for k in far if k % 2], [k for k in far if k % 2 == 0], *[[k] for k in z_last if k < 2]]
    chunks = [ks for ks in chunks if ks]

    def part(firsts, ks):
        return [(f, s, k, r) for f in firsts for s in second_last for k in ks for r in range(height)]

    halves = [[part(firsts, ks) for ks in chunks] for firsts in (first_last[:-1], [0])]
    table = np.array(
        [(core, *row) for half in halves for core in [*range(1, nc), 0] for piece in half for row in piece], np.int32
    ).T
    sent, kept = [[len(piece) for piece in half] for half in halves]
    return table, chunks, sent, kept


def shards(latent, w_in, w_out, observed, patch_index, counts):
    rows_in = latent[0, 0]
    nrows, depth = rows_in.shape
    width, channels = w_out.shape
    nz, nt, ny = (lax.axis_size(name) for name in ("member", "tile", "batch"))
    nc, nx = CORES, nt // CORES
    w_out_t = w_out.T
    height = depth // (nz * nt * ny)
    table, chunks, sent, kept = row_order(nz, nx, nc, ny, height)
    turned = 1 if nx == ny else 0

    far_first = [*reversed(range(nz))]
    everywhere = [(z, x, c, y) for z in range(nz) for x in range(nx) for c in range(nc) for y in range(ny)]

    def shift(value, target):
        def number(z, x, c, y):
            return (z * nt + x * nc + c) * ny + y

        return lax.ppermute(
            value, ("member", "tile", "batch"), [(number(*place), number(*target(*place))) for place in everywhere]
        )

    def send_to(value, k):
        return shift(value, lambda z, x, c, y: (partner(z, k, nz), x, c, y))

    def exchange(values):
        return [send_to(values[k], k) if k else values[0] for k in far_first]

    def shift_core(value, j):
        return shift(value, lambda z, x, c, y: (z, x, (c + j) % nc, y))

    def along(of_core):
        def shift_one(value, j):
            def target(z, x, c, y):
                return (z, (x + j) % nx, c, y) if of_core(c) == 0 else (z, x, c, (y + j) % ny)

            return shift(value, target)

        return shift_one

    shift_first, shift_second = along(lambda c: c * turned), along(lambda c: 1 - c * turned)

    def send_all(value, others, shift_one):
        if others == 1:
            return [shift_one(value, 1)]
        return [shift_one(v, j + 1) for j, v in enumerate(jnp.split(value, others, axis=0))] if others else []

    share = nrows // PATCH // nz
    packed = dict(zip(far_first, decode(rows_in, w_in, w_out_t, nz, far_first)))
    grouped = exchange(packed)

    def source_of(columns):
        me_z, me_t, me_y = (lax.axis_index(name) for name in ("member", "tile", "batch"))
        core, first, second, k, row = columns[:5]
        z = partner(me_z, k, nz)
        core = lax.rem(core + lax.rem(me_t, nc), nc)
        turn = core * turned
        x, y = first + turn * (second - first), second + turn * (first - second)
        tile = lax.rem(x + me_t // nc, nx) * nc + core
        return ((z * nt + tile) * ny + lax.rem(y + me_y, ny)) * height + row

    table = np.concatenate([table, np.zeros((-len(table) % 8, table.shape[1]), np.int32)])
    n_send, n_keep = sum(sent), sum(kept)
    middle = 2 * n_send

    slope, hidden = slopes(rows_in, w_in)
    target, weight = targets(observed[0], patch_index, counts, share, channels)
    grouped, slope, hidden, target, weight = lax.optimization_barrier((grouped, slope, hidden, target, weight))

    scored = score(grouped, target, weight)
    returned = exchange(dict(zip(far_first, scored)))
    ordered = ordered_transposes(table, source_of, rows_in, hidden)
    returned, ordered = lax.optimization_barrier((returned, ordered))

    cuts = [0, sum(sent[:2]), n_send] if len(sent) > 2 else [0, n_send]
    *other_sends, gp, g = first_products(returned, slope, w_out_t, ordered, cuts)
    core_send = shift_core(other_sends[0], 1)
    own_send, other_keep = more_products(gp, g, ordered, [(n_send, middle), (middle, middle + n_keep)])

    def added(inputs, pieces, flops=0):
        return list(add_rows(inputs, [[(0, rows, [(i, low) for i in range(len(inputs))])] for low, rows in pieces], flops))

    def pieces_of(sizes, low=0):
        return [(low + int(at), size) for at, size in zip(np.cumsum([0, *sizes[:-1]]), sizes)]


    def summed_sends(value, start, end):
        plans = [
            [(0, rows, [(0, low), (1, low - start)])] for low, rows in pieces_of(sent) if start <= low < end
        ]
        return list(add_rows([own_send, value], plans))

    first_sends = summed_sends(core_send, 0, cuts[1])
    first_sends, gp, other_keep, later = lax.optimization_barrier((first_sends, gp, other_keep, other_sends[1:]))
    for value, start, end in zip(later, cuts[1:-1], cuts[2:]):
        first_sends += summed_sends(shift_core(value, 1), start, end)
    core_keep = shift_core(other_keep, 1)
    first_got = [send_all(value, nx - 1, shift_first) for value in first_sends]
    (own_keep,) = more_products(gp, g, ordered, [(middle + n_keep, middle + 2 * n_keep)])

    joined, near = {}, {}
    for ks, (low, size), got in zip(chunks, pieces_of(kept), first_got):
        if ks == chunks[-1] and len(chunks) > 3 and nz & (nz - 1) == 0:
            near = {k: send_to(joined[k], 1) for k in chunks[0]}
            got, near = lax.optimization_barrier((got, near))
        cut = size // ny * (ny - 1)
        terms = [(0, low), (1, low), *[(2 + i, 0) for i in range(len(got))]]
        second_send, second_keep = add_rows(
            [own_keep, core_keep, *got],
            [[(0, rows, [(i, start + at) for i, start in terms])] for at, rows in ((0, cut), (cut, size - cut))],
        )
        got = send_all(second_send, ny - 1, shift_second)
        joined.update(zip(ks, added([second_keep, *got], pieces_of([height] * len(ks)))))

    if nz & (nz - 1):
        return tuple(finish(exchange(joined), width, channels))
    near.update({k: send_to(joined[k], 1) for k in range(1, nz, 2) if k not in near})
    parts = [joined[0], *([near[1]] if near else [])]
    far = [send_to(added([joined[k], near[k + 1]], [(0, height)])[0], k) for k in range(2, nz, 2)]
    if far:
        parts += added(far, [(0, height)], 1.2e10)
    return tuple(finish(parts[::-1], width, channels))


def solution(mesh):
    in_specs = (
        P("member", "batch", "tile", None),
        P(),
        P(),
        P("batch", "tile", None),
        P("batch", "tile"),
        P("batch", "tile"),
    )
    out_specs = (P(("member", "tile", "batch"), None), P(("member", "tile", "batch"), None))
    return jax.shard_map(shards, mesh=mesh, in_specs=in_specs, out_specs=out_specs, check_vma=False)
```

```python
import functools

import jax
import jax.numpy as jnp
import numpy as np
from jax import lax
from jax.experimental import pallas as pl
from jax.experimental.pallas import tpu as pltpu
from jax.sharding import PartitionSpec as P

PATCH = 16
CORES = 2
LANES = 128
MIB = 1 << 20
NT = (((1,), (1,)), ((), ()))
WHOLE = pl.BlockSpec()
ANY = pl.BlockSpec(memory_space=pl.ANY)
FEW = 24
MOST = 56


def partner(z, k, nz):
    return z ^ k if nz & (nz - 1) == 0 else (z + k) % nz


def params(mib=24):
    return pltpu.CompilerParams(vmem_limit_bytes=int(mib * MIB))


def cost(flops, moved):
    return pl.CostEstimate(flops=int(flops), bytes_accessed=int(moved), transcendentals=0)


def packing(channels):
    spare = LANES - channels
    carriers = PATCH * channels // LANES
    per_cell = channels // spare
    assert carriers * LANES == PATCH * channels and per_cell * spare == channels
    return spare, carriers, per_cell


def pack(cell, channels):
    spare, carriers, per_cell = packing(channels)
    extra = [cell(j) for j in range(carriers, PATCH)]
    lane = lax.broadcasted_iota(jnp.int32, extra[0].shape, 1)
    rows = []
    for j in range(carriers):
        piece = extra[j // per_cell]
        moved = pltpu.roll(piece, channels - j % per_cell * spare, 1)
        rows.append(jnp.where(lane < channels, cell(j), moved))
    return rows


def unpack(rows, channels):
    spare, carriers, per_cell = packing(channels)
    lane = lax.broadcasted_iota(jnp.int32, rows[0].shape, 1)
    cells = list(rows)
    for first in range(0, carriers, per_cell):
        value = jnp.zeros_like(rows[0])
        for i in range(per_cell):
            moved = pltpu.roll(rows[first + i], (i * spare - channels) % LANES, 1)
            value = jnp.where((lane >= i * spare) & (lane < (i + 1) * spare), moved, value)
        cells.append(value)
    return cells


def in_hbm(value):
    return pltpu.with_memory_space_constraint(value, pltpu.HBM)


def column_steps(width):
    step = 256 if width % 256 == 0 else width
    return [slice(low, low + step) for low in range(0, width, step)]


def decode_body(pieces, latent_ref, w_in_ref, w_out_t_ref, *refs):
    out_refs, (rows, w_in, w_out_t, cells, row_sems, sems) = refs[:len(pieces)], refs[len(pieces):]
    count, block, _ = rows.shape
    channels = w_out_t.shape[0]
    share = out_refs[0].shape[1]
    half = max(count // 2, 1)
    me_z, nz = lax.axis_index("member"), lax.axis_size("member")
    row_copies = []
    for i, k in enumerate(pieces):
        start = pl.multiple_of(partner(me_z, k, nz) * block, block)
        row_copies.append(pltpu.make_async_copy(latent_ref.at[pl.ds(start, block)], rows.at[i], row_sems.at[i]))
    w_copies = [pltpu.make_async_copy(w_in_ref, w_in, sems.at[0]), pltpu.make_async_copy(w_out_t_ref, w_out_t, sems.at[1])]
    for copy in [*w_copies, *row_copies]:
        copy.start()
    for copy in [*w_copies, *row_copies[:half]]:
        copy.wait()
    for i in range(count):
        if i == half:
            for copy in row_copies[half:]:
                copy.wait()
        preact = jnp.dot(rows[i], w_in[...], preferred_element_type=jnp.float32)
        hidden = (preact / (1.0 + jnp.exp(-preact))).astype(jnp.bfloat16)
        cells[i, :block, :channels] = lax.dot_general(hidden, w_out_t[...], NT, preferred_element_type=jnp.float32)
        for j, row in enumerate(pack(lambda j: cells[i, pl.ds(j, share, stride=PATCH), :], channels)):
            out_refs[i][j] = row


def decode(rows_in, w_in, w_out_t, parts, pieces):
    nrows, depth = rows_in.shape
    width = w_in.shape[1]
    channels = w_out_t.shape[0]
    block = nrows // parts
    share = block // PATCH
    carriers = packing(channels)[1]
    count = len(pieces)
    return pl.pallas_call(
        functools.partial(decode_body, tuple(pieces)),
        in_specs=[ANY] * 3,
        out_specs=[WHOLE] * count,
        out_shape=[jax.ShapeDtypeStruct((carriers, share, LANES), jnp.float32)] * count,
        scratch_shapes=[
            pltpu.VMEM((count, block, depth), jnp.bfloat16),
            pltpu.VMEM((depth, width), jnp.bfloat16),
            pltpu.VMEM((channels, width), jnp.bfloat16),
            pltpu.VMEM((count, block + PATCH, LANES), jnp.float32),
            pltpu.SemaphoreType.DMA((count,)),
            pltpu.SemaphoreType.DMA((2,)),
        ],
        compiler_params=params(MOST),
        cost_estimate=cost(2 * nrows * width * (depth + channels), 5 * MIB),
        name="decode",
    )(rows_in, w_in, w_out_t)


def fill_choice(source, choice):
    picked, extent = choice.shape
    for low in range(0, picked, LANES):
        high = min(low + LANES, picked)
        across = jnp.broadcast_to(source[:, low:high], (LANES, high - low))
        down = jnp.transpose(across)
        for left in range(0, extent, LANES):
            here = lax.broadcasted_iota(jnp.int32, down.shape, 1) + left
            choice[low:high, left:left + LANES] = jnp.where(down == here, 1.0, 0.0).astype(jnp.bfloat16)


def slope_body(latent_ref, w_in_ref, slope_ref, hidden_ref):
    preact = jnp.dot(latent_ref[...], w_in_ref[...], preferred_element_type=jnp.float32)
    scale = 1.0 + jnp.exp(-preact)
    sigma = 1.0 / scale
    slope_ref[...] = sigma * (1.0 + preact * (1.0 - sigma))
    hidden_ref[...] = (preact / scale).astype(jnp.bfloat16)


def slopes(rows_in, w_in):
    nrows, depth = rows_in.shape
    width = w_in.shape[1]
    block = 256 if nrows % 256 == 0 else nrows
    return pl.pallas_call(
        slope_body,
        grid=(nrows // block,),
        in_specs=[pl.BlockSpec((block, depth), lambda i: (i, 0)), pl.BlockSpec((depth, width), lambda i: (0, 0))],
        out_specs=[pl.BlockSpec((block, width), lambda i: (i, 0)), pl.BlockSpec((block, width), lambda i: (i, 0))],
        out_shape=[
            jax.ShapeDtypeStruct((nrows, width), jnp.float32),
            jax.ShapeDtypeStruct((nrows, width), jnp.bfloat16),
        ],
        compiler_params=params(FEW),
        cost_estimate=cost(2 * nrows * width * depth, 4 * MIB),
        name="slopes",
    )(in_hbm(rows_in), in_hbm(w_in))


def order_body(source_of, table_ref, latent_ref, hidden_ref, out_ref, choice):
    @pl.when(pl.program_id(0) == 0)
    def _():
        fill_choice(source_of([table_ref[k:k + 1] for k in range(table_ref.shape[0])]), choice)

    for k, matrix_ref in enumerate((latent_ref, hidden_ref)):
        ordered = lax.dot_general(choice[...], matrix_ref[...], NT, preferred_element_type=jnp.float32)
        out_ref[k] = ordered.astype(jnp.bfloat16)


def ordered_transposes(table, source_of, latent, hidden):
    nrows, extent = latent.shape
    picked = table.shape[1]
    block = 256 if nrows % 256 == 0 else nrows
    return pl.pallas_call(
        functools.partial(order_body, source_of),
        grid=(nrows // block,),
        in_specs=[
            pl.BlockSpec(table.shape, lambda i: (0, 0)),
            pl.BlockSpec((block, extent), lambda i: (i, 0)),
            pl.BlockSpec((block, extent), lambda i: (i, 0)),
        ],
        out_specs=pl.BlockSpec((2, picked, block), lambda i: (0, 0, i)),
        out_shape=jax.ShapeDtypeStruct((2, picked, nrows), jnp.bfloat16),
        scratch_shapes=[pltpu.VMEM((picked, extent), jnp.bfloat16)],
        compiler_params=params(FEW),
        cost_estimate=cost(nrows * extent * picked, 4 * MIB),
        name="ordered_transposes",
    )(table, in_hbm(latent), hidden)


def target_body(channels, pool_ref, index_ref, count_ref, target_ref, weight_ref):
    carriers, share, _ = target_ref.shape
    npool, total = pool_ref.shape
    npatch = index_ref.shape[1]
    own = lax.broadcasted_iota(jnp.int32, (share, npatch), 0) + lax.axis_index("member") * share
    own = own == lax.broadcasted_iota(jnp.int32, (share, npatch), 1)
    index = jnp.sum(jnp.where(own, index_ref[...], 0), axis=1, keepdims=True)
    count = jnp.sum(jnp.where(own, count_ref[...], 0), axis=1, keepdims=True)
    weight_ref[...] = jnp.broadcast_to(count.astype(jnp.float32), weight_ref.shape)
    choose = index == lax.broadcasted_iota(jnp.int32, (share, npool), 1)
    flat = jnp.dot(
        jnp.where(choose, 1.0, 0.0).astype(jnp.bfloat16), pool_ref[...], preferred_element_type=jnp.float32
    )

    def cell(j):
        start = j * channels
        low = start // LANES * LANES
        part = flat[:, low:min(low + 2 * LANES, total)]
        return pltpu.roll(part, (low - start) % part.shape[1], 1)[:, :LANES]

    for j, row in enumerate(pack(cell, channels)):
        target_ref[j] = row


def targets(pool, index, count, share, channels):
    carriers = packing(channels)[1]
    return pl.pallas_call(
        functools.partial(target_body, channels),
        in_specs=[WHOLE] * 3,
        out_specs=[WHOLE] * 2,
        out_shape=[
            jax.ShapeDtypeStruct((carriers, share, LANES), jnp.float32),
            jax.ShapeDtypeStruct((share, LANES), jnp.float32),
        ],
        compiler_params=params(),
        cost_estimate=cost(2 * share * pool.size, 2 * pool.size),
        name="targets",
    )(pool, index, count)


def score_body(members, *refs):
    x_refs, (target_ref, weight_ref), out_refs = refs[:members], refs[members:members + 2], refs[members + 2:]
    carriers = target_ref.shape[0]
    weight = weight_ref[...]

    def inverse_norm(delta):
        squares = sum(d * d for d in delta)
        return 1.0 / jnp.sqrt(jnp.sum(squares, axis=-1, keepdims=True) + 1.0)

    target = [target_ref[j] for j in range(carriers)]
    xs = [[ref[j] for j in range(carriers)] for ref in x_refs]
    pair = [[jnp.zeros_like(target[0])] * carriers for _ in range(members)]
    for m in range(members):
        for k in range(m + 1, members):
            delta = [p - q for p, q in zip(xs[m], xs[k])]
            inverse = inverse_norm(delta)
            pair[m] = [p + d * inverse for p, d in zip(pair[m], delta)]
            pair[k] = [p - d * inverse for p, d in zip(pair[k], delta)]
    for m in range(members):
        delta = [p - q for p, q in zip(xs[m], target)]
        inverse = inverse_norm(delta)
        for j in range(carriers):
            out_refs[m][j] = weight * (delta[j] * inverse / members - pair[m][j] / (members * members))


def score(pieces, target, weight):
    members = len(pieces)
    size = members * target.size
    return pl.pallas_call(
        functools.partial(score_body, members),
        in_specs=[WHOLE] * (members + 2),
        out_specs=[WHOLE] * members,
        out_shape=[jax.ShapeDtypeStruct(target.shape, jnp.float32)] * members,
        compiler_params=params(),
        cost_estimate=cost(30 * size, 8 * size),
        name="score",
    )(*pieces, target, weight)


def first_body(parts, cuts, *refs):
    scored_refs, (slope, w_out_t, ordered, *results, gp, g, cells) = refs[:parts], refs[parts:]
    carriers, share, _ = scored_refs[0].shape
    channels, width = w_out_t.shape
    picked = cuts[-1]

    def put(columns, product):
        for result, low, high in zip(results, cuts[:-1], cuts[1:]):
            result[:, columns] = product[low:high]

    me_z = lax.axis_index("member")
    for k, scored_ref in zip(reversed(range(parts)), scored_refs):
        base = partner(me_z, k, parts) * (share * PATCH)
        for j, value in enumerate(unpack([scored_ref[j] for j in range(carriers)], channels)):
            cells[pl.ds(base + j, share, stride=PATCH), :] = value
    lane = lax.broadcasted_iota(jnp.int32, g.shape, 1)
    g[...] = jnp.where(lane < channels, cells[:g.shape[0]], 0.0).astype(jnp.bfloat16)
    put(slice(width, None), jnp.dot(ordered[1, :picked], g[...], preferred_element_type=jnp.float32))
    for c in column_steps(width):
        backward = jnp.dot(g[:, :channels], w_out_t[:, c], preferred_element_type=jnp.float32)
        gp[:, c] = (backward * slope[:, c]).astype(jnp.bfloat16)
        put(c, jnp.dot(ordered[0, :picked], gp[:, c], preferred_element_type=jnp.float32))


def first_products(scored, slope, w_out_t, ordered, cuts):
    nrows, width = slope.shape
    channels = w_out_t.shape[0]
    return pl.pallas_call(
        functools.partial(first_body, len(scored), tuple(cuts)),
        in_specs=[WHOLE] * (len(scored) + 3),
        out_specs=[WHOLE] * (len(cuts) + 1),
        out_shape=[
            *[jax.ShapeDtypeStruct((high - low, width + LANES), jnp.float32) for low, high in zip(cuts[:-1], cuts[1:])],
            jax.ShapeDtypeStruct((nrows, width), jnp.bfloat16),
            jax.ShapeDtypeStruct((nrows, LANES), jnp.bfloat16),
        ],
        scratch_shapes=[pltpu.VMEM((nrows + PATCH, LANES), jnp.float32)],
        compiler_params=params(FEW),
        cost_estimate=cost(2 * nrows * width * (channels + cuts[-1]), 10 * MIB),
        name="first_products",
    )(*scored, slope, w_out_t, ordered)


def more_body(cuts, gp, g, ordered, *out_refs):
    low, high = cuts[0][0], cuts[-1][1]
    width = gp.shape[1]

    def put(columns, product):
        for out_ref, (start, end) in zip(out_refs, cuts):
            out_ref[:, columns] = product[start - low:end - low]

    for columns in column_steps(width):
        put(columns, jnp.dot(ordered[0, low:high], gp[:, columns], preferred_element_type=jnp.float32))
    put(slice(width, None), jnp.dot(ordered[1, low:high], g[...], preferred_element_type=jnp.float32))


def more_products(gp, g, ordered, cuts):
    nrows, width = gp.shape
    picked = cuts[-1][1] - cuts[0][0]
    return pl.pallas_call(
        functools.partial(more_body, tuple(cuts)),
        in_specs=[WHOLE] * 3,
        out_specs=[WHOLE] * len(cuts),
        out_shape=[jax.ShapeDtypeStruct((end - start, width + LANES), jnp.float32) for start, end in cuts],
        compiler_params=params(FEW),
        cost_estimate=cost(2 * nrows * picked * width, 6 * MIB),
        name="more_products",
    )(gp, g, ordered)


def add_body(plans, count, *refs):
    inputs, outputs = refs[:count], refs[count:]
    for out_ref, plan in zip(outputs, plans):
        for at, rows, sources in plan:
            total = None
            for which, low in sources:
                value = inputs[which][low:low + rows]
                total = value if total is None else total + value
            out_ref[at:at + rows] = total


def add_rows(inputs, plans, flops=0):
    columns = inputs[0].shape[1]
    sizes = [sum(rows for _, rows, _ in plan) for plan in plans]
    return pl.pallas_call(
        functools.partial(add_body, plans, len(inputs)),
        in_specs=[WHOLE] * len(inputs),
        out_specs=[WHOLE] * len(plans),
        out_shape=[jax.ShapeDtypeStruct((size, columns), jnp.float32) for size in sizes],
        compiler_params=params(),
        cost_estimate=cost(flops or 3 * sum(sizes) * columns, 12 * sum(sizes) * columns),
        name="add_rows",
    )(*inputs)


def finish_body(*refs):
    *parts, first_ref, second_ref = refs
    width, channels = first_ref.shape[1], second_ref.shape[1]
    total = parts[0][...]
    for ref in parts[1:]:
        total = total + ref[...]
    first_ref[...] = total[:, :width]
    second_ref[...] = total[:, width:width + channels]


def finish(parts, width, channels):
    height = parts[0].shape[0]
    return pl.pallas_call(
        finish_body,
        in_specs=[WHOLE] * len(parts),
        out_specs=[WHOLE] * 2,
        out_shape=[
            jax.ShapeDtypeStruct((height, width), jnp.float32),
            jax.ShapeDtypeStruct((height, channels), jnp.float32),
        ],
        compiler_params=params(),
        cost_estimate=cost(4 * height * width, 20 * height * width),
        name="finish",
    )(*parts)


def row_order(nz, nx, nc, ny, height):
    first_last, second_last = [[*range(1, n), 0] for n in (nx, ny)]
    z_last = [*reversed(range(nz))]
    far = [k for k in z_last if k > 1]
    chunks = [[k for k in far if k % 2], [k for k in far if k % 2 == 0], *[[k] for k in z_last if k < 2]]
    chunks = [ks for ks in chunks if ks]

    def part(firsts, ks):
        return [(f, s, k, r) for f in firsts for s in second_last for k in ks for r in range(height)]

    halves = [[part(firsts, ks) for ks in chunks] for firsts in (first_last[:-1], [0])]
    table = np.array(
        [(core, *row) for half in halves for core in [*range(1, nc), 0] for piece in half for row in piece], np.int32
    ).T
    sent, kept = [[len(piece) for piece in half] for half in halves]
    return table, chunks, sent, kept


def shards(latent, w_in, w_out, observed, patch_index, counts):
    rows_in = latent[0, 0]
    nrows, depth = rows_in.shape
    width, channels = w_out.shape
    nz, nt, ny = (lax.axis_size(name) for name in ("member", "tile", "batch"))
    nc, nx = CORES, nt // CORES
    w_out_t = w_out.T
    height = depth // (nz * nt * ny)
    table, chunks, sent, kept = row_order(nz, nx, nc, ny, height)
    turned = 1 if nx == ny else 0

    far_first = [*reversed(range(nz))]
    everywhere = [(z, x, c, y) for z in range(nz) for x in range(nx) for c in range(nc) for y in range(ny)]

    def shift(value, target):
        def number(z, x, c, y):
            return (z * nt + x * nc + c) * ny + y

        return lax.ppermute(
            value, ("member", "tile", "batch"), [(number(*place), number(*target(*place))) for place in everywhere]
        )

    def send_to(value, k):
        return shift(value, lambda z, x, c, y: (partner(z, k, nz), x, c, y))

    def exchange(values):
        return [send_to(values[k], k) if k else values[0] for k in far_first]

    def shift_core(value, j):
        return shift(value, lambda z, x, c, y: (z, x, (c + j) % nc, y))

    def along(of_core):
        def shift_one(value, j):
            def target(z, x, c, y):
                return (z, (x + j) % nx, c, y) if of_core(c) == 0 else (z, x, c, (y + j) % ny)

            return shift(value, target)

        return shift_one

    shift_first, shift_second = along(lambda c: c * turned), along(lambda c: 1 - c * turned)

    def send_all(value, others, shift_one):
        if others == 1:
            return [shift_one(value, 1)]
        return [shift_one(v, j + 1) for j, v in enumerate(jnp.split(value, others, axis=0))] if others else []

    share = nrows // PATCH // nz
    packed = dict(zip(far_first, decode(rows_in, w_in, w_out_t, nz, far_first)))
    grouped = exchange(packed)

    def source_of(columns):
        me_z, me_t, me_y = (lax.axis_index(name) for name in ("member", "tile", "batch"))
        core, first, second, k, row = columns[:5]
        z = partner(me_z, k, nz)
        core = lax.rem(core + lax.rem(me_t, nc), nc)
        turn = core * turned
        x, y = first + turn * (second - first), second + turn * (first - second)
        tile = lax.rem(x + me_t // nc, nx) * nc + core
        return ((z * nt + tile) * ny + lax.rem(y + me_y, ny)) * height + row

    table = np.concatenate([table, np.zeros((-len(table) % 8, table.shape[1]), np.int32)])
    n_send, n_keep = sum(sent), sum(kept)
    middle = 2 * n_send

    slope, hidden = slopes(rows_in, w_in)
    target, weight = targets(observed[0], patch_index, counts, share, channels)
    grouped, slope, hidden, target, weight = lax.optimization_barrier((grouped, slope, hidden, target, weight))

    scored = score(grouped, target, weight)
    returned = exchange(dict(zip(far_first, scored)))
    ordered = ordered_transposes(table, source_of, rows_in, hidden)
    returned, ordered = lax.optimization_barrier((returned, ordered))

    cuts = [0, sum(sent[:2]), n_send] if len(sent) > 2 else [0, n_send]
    *other_sends, gp, g = first_products(returned, slope, w_out_t, ordered, cuts)
    core_send = shift_core(other_sends[0], 1)
    own_send, other_keep = more_products(gp, g, ordered, [(n_send, middle), (middle, middle + n_keep)])

    def added(inputs, pieces, flops=0):
        return list(add_rows(inputs, [[(0, rows, [(i, low) for i in range(len(inputs))])] for low, rows in pieces], flops))

    def pieces_of(sizes, low=0):
        return [(low + int(at), size) for at, size in zip(np.cumsum([0, *sizes[:-1]]), sizes)]


    def summed_sends(value, start, end):
        plans = [
            [(0, rows, [(0, low), (1, low - start)])] for low, rows in pieces_of(sent) if start <= low < end
        ]
        return list(add_rows([own_send, value], plans))

    first_sends = summed_sends(core_send, 0, cuts[1])
    first_sends, gp, other_keep, later = lax.optimization_barrier((first_sends, gp, other_keep, other_sends[1:]))
    for value, start, end in zip(later, cuts[1:-1], cuts[2:]):
        first_sends += summed_sends(shift_core(value, 1), start, end)
    core_keep = shift_core(other_keep, 1)
    first_got = [send_all(value, nx - 1, shift_first) for value in first_sends]
    (own_keep,) = more_products(gp, g, ordered, [(middle + n_keep, middle + 2 * n_keep)])

    joined, near = {}, {}
    for ks, (low, size), got in zip(chunks, pieces_of(kept), first_got):
        if ks == chunks[-1] and len(chunks) > 3 and nz & (nz - 1) == 0:
            near = {k: send_to(joined[k], 1) for k in chunks[0]}
            got, near = lax.optimization_barrier((got, near))
        cut = size // ny * (ny - 1)
        terms = [(0, low), (1, low), *[(2 + i, 0) for i in range(len(got))]]
        second_send, second_keep = add_rows(
            [own_keep, core_keep, *got],
            [[(0, rows, [(i, start + at) for i, start in terms])] for at, rows in ((0, cut), (cut, size - cut))],
        )
        got = send_all(second_send, ny - 1, shift_second)
        joined.update(zip(ks, added([second_keep, *got], pieces_of([height] * len(ks)))))

    if nz & (nz - 1):
        return tuple(finish(exchange(joined), width, channels))
    near.update({k: send_to(joined[k], 1) for k in range(1, nz, 2) if k not in near})
    parts = [joined[0], *([near[1]] if near else [])]
    far = [send_to(added([joined[k], near[k + 1]], [(0, height)])[0], k) for k in range(2, nz, 2)]
    if far:
        parts += added(far, [(0, height)], 1.2e10)
    return tuple(finish(parts[::-1], width, channels))


def solution(mesh):
    in_specs = (
        P("member", "batch", "tile", None),
        P(),
        P(),
        P("batch", "tile", None),
        P("batch", "tile"),
        P("batch", "tile"),
    )
    out_specs = (P(("member", "tile", "batch"), None), P(("member", "tile", "batch"), None))
    return jax.shard_map(shards, mesh=mesh, in_specs=in_specs, out_specs=out_specs, check_vma=False)
```
